32 devices in a mesh: dp: 8 (over z, x), chan: 4 (over y, core).
Axes of the slice: x: 2, y: 2, z: 4, core: 2. Of those that a mesh axis runs over, the one named last changes fastest.
Arguments:
- audio_clips: float32 [8, 8, 2304], P('dp'), may hold values from -6 to 6
- mel_frames: bfloat16 [8, 80, 72], P('dp'), may hold values from -6 to 6
- crop_offsets: int32 [8], P('dp'), may hold values from 0 to 8
- inv_weight: float32 [8, 8], replicated, may hold values from -0.11 to 1.2, as said below
- initial_projection_weight: float32 [512, 4], P('chan'), may hold values from -3 to 3
- start_bias: float32 [512], P('chan'), may hold values from -3 to 3
- cond_weight: bfloat16 [8, 2, 512, 80], P(None, None, 'chan'), may hold values from -0.625 to 0.625
- in_weight: bfloat16 [8, 2, 512, 1536], P(None, None, 'chan'), may hold values from -0.15625 to 0.15625
- in_bias: float32 [8, 2, 512], P(None, None, 'chan'), may hold values from -3 to 3
- res_weight: bfloat16 [7, 512, 512], P(None, None, 'chan'), may hold values from -0.25 to 0.25
- res_bias: float32 [7, 512], P(None, 'chan'), may hold values from -2 to 2
- skip_projection_weight: bfloat16 [8, 512, 512], P(None, None, 'chan'), may hold values from -0.25 to 0.25
- skip_output_bias: float32 [512], P('chan'), may hold values from -3 to 3
- final_projection_weight: float32 [8, 512], P(None, 'chan'), may hold values from -0.09375 to 0.09375
- end_bias: float32 [8], replicated, may hold values from -1.5 to 1.5
Outputs:
- latent: float32 [8, 8, 2048], P('dp')
- log_det: float32 [8], P('dp')
- crop_loss: float32 [8], P('dp')
- audio_grad: float32 [8, 8, 2048], P('dp')
- mel_grad: float32 [8, 80, 64], P('dp')
- inv_grad: float32 [8, 8], replicated
- initial_projection_gradient: float32 [512, 4], P('chan')
- start_bias_grad: float32 [512], P('chan')
- cond_grad: float32 [8, 2, 512, 80], P(None, None, 'chan')
- in_grad: float32 [8, 2, 512, 1536], P(None, None, 'chan')
- in_bias_grad: float32 [8, 2, 512], P(None, None, 'chan')
- res_grad: float32 [7, 512, 512], P(None, None, 'chan')
- res_bias_grad: float32 [7, 512], P(None, 'chan')
- skip_grad: float32 [8, 512, 512], P(None, None, 'chan')
- skip_bias_grad: float32 [512], P('chan')
- end_grad: float32 [8, 512], P(None, 'chan')
- end_bias_grad: float32 [8], replicated
The draws below stay inside these ranges and needn't reach their ends.
Inputs may be any that keep to these rules, and one draw needn't show every extreme that they name: `inv_weight`: each row's diagonal entry is positive and exceeds the sum of the magnitudes of the row's other entries.
All inputs are finite; a program needn't handle non-finite values.
Results may differ from the reference program's by a relative error of at most 0.025.
Values may be sent and summed in bfloat16 or wider, within the bound.
A program may use at most 256 MiB of HBM per device.

```python
import jax
import jax.numpy as jnp
from jax import lax

CH = 8
WN = 512
MEL = 80
LAYERS = 8
HOP = 32
FRAMES = 2048
MEL_SLACK = 8
CROPS = 8
CLIP = 2304
MEL_LEN = 72


def draw_inv_weight(key, part):
    key = jax.random.fold_in(key, 7)
    key_diag, key_rest = jax.random.split(key)
    diagonal = jax.random.uniform(key_diag, (CH,), jnp.float32, 0.8, 1.2)
    others = jax.random.uniform(key_rest, (CH, CH), jnp.float32, -0.11, 0.11)
    eye_mask = jnp.eye(CH, dtype=jnp.float32)
    return others * (1.0 - eye_mask) + eye_mask * diagonal[None, :]


def place_ends(values, rng, smallest, largest):
    longest = values.shape.index(max(values.shape))
    spots = []
    for shift in (0, 1):
        where = [jax.random.randint(jax.random.fold_in(rng, axis), (), 0, length) for axis, length in enumerate(values.shape)]
        where[longest] = (where[longest] + shift) % values.shape[longest]
        spots.append(tuple(where))
    return values.at[spots[0]].set(smallest).at[spots[1]].set(largest)


def steps_of(own_key, shape, pieces, low, largest):
    def one(position, shards_of):
        steps = jax.random.uniform(jax.random.fold_in(jax.random.fold_in(own_key, 6), position), (shards_of,), jnp.float32, low / len(pieces), largest / len(pieces))
        return jnp.repeat(jnp.exp(steps), shape[position] // shards_of).reshape((-1,) + (1,) * (len(shape) - position - 1))

    level = one(*pieces[0])
    for cut in pieces[1:]:
        level = level * one(*cut)
    return level


def bell_draw(own_key, shape, width, most, cuts=(), kind=jnp.bfloat16):
    gain = steps_of(own_key, shape, cuts, -0.22, 0.18) if cuts else 1.0
    result = jax.random.normal(own_key, shape, jnp.float32) * width * gain
    return jnp.minimum(jnp.maximum(result, -most), most).astype(kind)


def setup_inputs(seed: int = 0) -> dict:
    keys = jax.random.split(jax.random.key(seed), 16)
    return {
        "audio_clips": bell_draw(keys[0], (CROPS, CH, CLIP), 1.0, 6.0, ((0, 8),), jnp.float32),
        "mel_frames": bell_draw(keys[1], (CROPS, MEL, MEL_LEN), 1.0, 6.0, ((0, 8),)),
        "crop_offsets": place_ends(jax.random.randint(keys[2], (CROPS,), 0, MEL_SLACK + 1), jax.random.fold_in(keys[2], 1), 0, MEL_SLACK).astype(jnp.int32),
        "inv_weight": draw_inv_weight(jax.random.fold_in(keys[15], 71), 0),
        "initial_projection_weight": bell_draw(keys[4], (WN, CH // 2), (CH // 2) ** -0.5, 3.0, ((0, 4),), jnp.float32),
        "start_bias": bell_draw(keys[5], (WN,), 0.5, 3.0, ((0, 4),), jnp.float32),
        "cond_weight": bell_draw(keys[6], (LAYERS, 2, WN, MEL), MEL ** -0.5, 0.625, ((2, 4),)),
        "in_weight": bell_draw(keys[7], (LAYERS, 2, WN, 3 * WN), (3 * WN) ** -0.5, 0.15625, ((2, 4),)),
        "in_bias": bell_draw(keys[8], (LAYERS, 2, WN), 0.5, 3.0, ((2, 4),), jnp.float32),
        "res_weight": bell_draw(keys[9], (LAYERS - 1, WN, WN), WN ** -0.5, 0.25, ((2, 4),)),
        "res_bias": bell_draw(keys[10], (LAYERS - 1, WN), 0.3, 2.0, ((1, 4),), jnp.float32),
        "skip_projection_weight": bell_draw(keys[11], (LAYERS, WN, WN), WN ** -0.5, 0.25, ((2, 4),)),
        "skip_output_bias": bell_draw(keys[12], (WN,), 0.5, 3.0, ((0, 4),), jnp.float32),
        "final_projection_weight": bell_draw(keys[13], (CH, WN), (8 * WN) ** -0.5, 0.09375, ((1, 4),), jnp.float32),
        "end_bias": bell_draw(keys[14], (CH,), 0.3, 1.5, (), jnp.float32),
    }


UPPER_LIMIT = lax.Precision.HIGHEST

@jax.custom_vjp
def low(v):
    return lax.optimization_barrier(v.astype(jnp.bfloat16)).astype(jnp.float32)

@jax.custom_vjp
def low_back(v):
    return v

def low_keep(v):
    return (low(v), None)

def low_pass(kept, grad):
    return (grad,)

def back_keep(v):
    return (v, None)

def back_low(kept, grad):
    return (low(grad),)
low.defvjp(low_keep, low_pass)
low_back.defvjp(back_keep, back_low)

def flow_crop(params, crop_audio, crop_mel):
    inv_weight, initial_projection_weight, start_bias, cond_weight, in_weight, in_bias, res_weight, res_bias, skip_projection_weight, skip_output_bias, final_projection_weight, end_bias = params
    mixed_input = jnp.dot(inv_weight, crop_audio, precision=UPPER_LIMIT)
    leading_half_channels = mixed_input[:CH // 2]
    second_half = mixed_input[CH // 2:]
    hidden = jnp.dot(initial_projection_weight, leading_half_channels, precision=UPPER_LIMIT) + start_bias[:, None]
    upsampled = jnp.repeat(crop_mel, HOP, axis=1)
    skip_output_total = jnp.zeros((WN, FRAMES), jnp.float32)
    for layer_position in range(LAYERS):
        dilation = 2 ** layer_position
        rounded = low(hidden)
        padded = jnp.pad(rounded, ((0, 0), (dilation, dilation)))
        stacked = jnp.concatenate([padded[:, filter_position * dilation:filter_position * dilation + FRAMES] for filter_position in range(3)], axis=0)
        cond_term = jnp.einsum('gcm,mf->gcf', cond_weight[layer_position], upsampled, precision=UPPER_LIMIT)
        preact = jnp.einsum('gcj,jf->gcf', in_weight[layer_position], stacked, precision=UPPER_LIMIT)
        preact = low_back(preact + in_bias[layer_position][:, :, None] + cond_term)
        gate_activation = low(jnp.tanh(preact[0]) * jax.nn.sigmoid(preact[1]))
        if layer_position < LAYERS - 1:
            residual = low_back(jnp.dot(res_weight[layer_position], gate_activation, precision=UPPER_LIMIT) + res_bias[layer_position][:, None])
            hidden = hidden + residual
        skip_output_total = skip_output_total + low_back(jnp.dot(skip_projection_weight[layer_position], gate_activation, precision=UPPER_LIMIT))
    output = jnp.dot(final_projection_weight, skip_output_total + skip_output_bias[:, None], precision=UPPER_LIMIT) + end_bias[:, None]
    log_scale = output[:CH // 2]
    shift_term = output[CH // 2:]
    second_out = jnp.exp(log_scale) * second_half + shift_term
    latent = jnp.concatenate([leading_half_channels, second_out], axis=0)
    sign_part, log_abs = jnp.linalg.slogdet(inv_weight)
    log_det = jnp.sum(log_scale) + FRAMES * log_abs
    objective = 0.5 * jnp.sum(latent * latent) - log_det
    return (objective, (latent, log_det))

def reference(audio_clips, mel_frames, crop_offsets, inv_weight, initial_projection_weight, start_bias, cond_weight, in_weight, in_bias, res_weight, res_bias, skip_projection_weight, skip_output_bias, final_projection_weight, end_bias):

    def crop_one(clip, mel_clip, offset):
        return (lax.dynamic_slice_in_dim(clip, offset * HOP, FRAMES, 1), lax.dynamic_slice_in_dim(mel_clip, offset, FRAMES // HOP, 1))
    crop_audio, crop_mel = jax.vmap(crop_one)(audio_clips, mel_frames.astype(jnp.float32), crop_offsets.astype(jnp.int32))
    params = tuple((array.astype(jnp.float32) for array in (inv_weight, initial_projection_weight, start_bias, cond_weight, in_weight, in_bias, res_weight, res_bias, skip_projection_weight, skip_output_bias, final_projection_weight, end_bias)))
    start_sums = tuple((jnp.zeros_like(array) for array in params))

    def accumulate(totals, crop_pair):
        one_audio, one_mel = crop_pair
        objective, pullback, (latent, log_det) = jax.vjp(flow_crop, params, one_audio, one_mel, has_aux=True)
        param_grads, audio_grad, mel_grad = pullback(jnp.ones_like(objective))
        totals = jax.tree.map(lambda left, right: left + right, totals, param_grads)
        return (totals, (latent, log_det, objective / (CH * FRAMES), audio_grad, mel_grad))
    sums, per_crop = lax.scan(accumulate, start_sums, (crop_audio, crop_mel))
    latent, log_det, crop_loss, audio_grad, mel_grad = per_crop
    inv_grad, initial_projection_gradient, start_bias_grad, cond_grad, in_grad, in_bias_grad, res_grad, res_bias_grad, skip_grad, skip_bias_grad, end_grad, end_bias_grad = sums
    return (latent, log_det, crop_loss, audio_grad, mel_grad, inv_grad, initial_projection_gradient, start_bias_grad, cond_grad, in_grad, in_bias_grad, res_grad, res_bias_grad, skip_grad, skip_bias_grad, end_grad, end_bias_grad)
```

```python
import jax
import jax.numpy as jnp
from jax import lax
from jax.sharding import PartitionSpec as P

CH = 8
HALF = 4
MEL = 80
LAYERS = 8
HOP = 32
FRAMES = 2048
CONV = 1536
EXT = 1664
PACK = 1920

HIGH = lax.Precision.HIGHEST
F32 = jnp.float32
BF16 = jnp.bfloat16


def dot(a, b):
    return jnp.dot(a, b, preferred_element_type=F32)


def invert_small(matrix):
    size_of = matrix.shape[0]
    augmented = jnp.concatenate([matrix, jnp.eye(size_of, dtype=F32)], axis=1)
    log_total = F32(0.0)
    for column in range(size_of):
        pivot = augmented[column, column]
        log_total = log_total + jnp.log(pivot)
        pivot_row = augmented[column] / pivot
        factor = augmented[:, column]
        augmented = augmented - factor[:, None] * pivot_row[None, :]
        augmented = augmented.at[column].set(pivot_row)
    return (augmented[:, size_of:], log_total)


def split(values):
    high = values.astype(BF16)
    return high, (values - high.astype(F32)).astype(BF16)


def local(
    audio_clips,
    mel_frames,
    crop_offsets,
    inv_weight,
    initial_projection_weight,
    start_bias,
    cond_weight,
    in_weight,
    in_bias,
    res_weight,
    res_bias,
    skip_projection_weight,
    skip_output_bias,
    final_projection_weight,
    end_bias,
):
    shards = lax.axis_size("chan")
    shard = lax.axis_index("chan")
    rows = initial_projection_weight.shape[0]
    width = rows * shards
    frames = FRAMES // shards
    mel_count = frames // HOP
    up = [(i, i + 1) for i in range(shards - 1)]
    down = [(i + 1, i) for i in range(shards - 1)]

    offset = crop_offsets[0]
    audio = lax.dynamic_slice(audio_clips[0], (0, offset * HOP + shard * frames), (CH, frames)).T
    mel = lax.dynamic_slice(mel_frames[0], (0, offset + shard * mel_count), (MEL, mel_count)).T
    mixed = jnp.dot(audio, inv_weight.T, precision=HIGH)
    first, second = mixed[:, :HALF], mixed[:, HALF:]

    small = jnp.concatenate(
        [
            initial_projection_weight.T,
            start_bias[None],
            res_bias,
            final_projection_weight,
            skip_output_bias[None],
        ],
        axis=0,
    )
    small = lax.all_gather(small, "chan", axis=1, tiled=True)
    start_weight = small[:4]
    start = small[4]
    residual_bias = small[5:12]
    final_weight = small[12:20]
    skip_bias = small[20]
    fold_local = jnp.einsum(
        "ko,loi->lki", final_weight, skip_projection_weight.astype(F32), precision=HIGH
    )
    fold = lax.all_gather(fold_local, "chan", axis=2, tiled=True)
    fold_high, fold_low = split(fold)
    const = jnp.dot(final_weight, skip_bias, precision=HIGH) + end_bias

    bias_high, bias_low = split(in_bias)
    packed = jnp.concatenate(
        [
            in_weight.reshape(LAYERS, 2 * rows, CONV),
            jnp.concatenate(
                [
                    cond_weight,
                    bias_high[..., None],
                    bias_low[..., None],
                    jnp.zeros((LAYERS, 2, rows, EXT - CONV - MEL - 2), BF16),
                ],
                axis=-1,
            ).reshape(LAYERS, 2 * rows, EXT - CONV),
            jnp.pad(
                res_weight.reshape(LAYERS - 1, 2, width // 2, rows)
                .swapaxes(1, 2)
                .reshape(LAYERS - 1, width // 2, 2 * rows),
                ((0, 1), (0, 0), (0, 0)),
            ),
        ],
        axis=2,
    )
    weights = lax.all_gather(packed, "chan", axis=0, tiled=False)

    mel_part = jnp.concatenate(
        [
            jnp.repeat(mel, HOP, axis=0),
            jnp.ones((frames, 2), BF16),
            jnp.zeros((frames, EXT - CONV - MEL - 2), BF16),
        ],
        axis=1,
    )
    hidden = jnp.dot(first, start_weight, precision=HIGH) + start
    kept = []
    out = jnp.zeros((frames, CH), F32)
    for layer in range(LAYERS):
        d = 2**layer
        low = hidden.astype(BF16)
        before = lax.ppermute(low[frames - d :], "chan", up)
        after = lax.ppermute(low[:d], "chan", down)
        ext = jnp.concatenate(
            [
                jnp.concatenate([before, low[: frames - d]], axis=0),
                low,
                jnp.concatenate([low[d:], after], axis=0),
                mel_part,
            ],
            axis=1,
        )
        gated, dt, ds = [], [], []
        for s in range(shards):
            pre = dot(ext, weights[s, layer, :, :EXT].T)
            t = jnp.tanh(pre[:, :rows])
            g = jax.nn.sigmoid(pre[:, rows:])
            gated.append((t * g).astype(BF16))
            dt.append((g * (1.0 - t * t)).astype(BF16))
            ds.append((t * g * (1.0 - g)).astype(BF16))
        full = jnp.concatenate(gated, axis=1)
        kept.append((ext, gated, dt, ds))
        out = out + dot(full, fold_high[layer].T) + dot(full, fold_low[layer].T)
        if layer < LAYERS - 1:
            residual = jnp.concatenate(
                [
                    weights[:, layer, :, EXT : EXT + rows],
                    weights[:, layer, :, EXT + rows :],
                ],
                axis=1,
            )
            residual = jnp.moveaxis(residual, 0, 1).reshape(width, width)
            hidden = hidden + dot(full, residual.T) + residual_bias[layer]
    out = out + const
    log_scale, shift = out[:, :HALF], out[:, HALF:]
    scale = jnp.exp(log_scale)
    second_out = scale * second + shift
    latent = jnp.concatenate([first, second_out], axis=1)
    inverse, log_abs = invert_small(inv_weight)
    sums = lax.psum(jnp.stack([jnp.sum(log_scale), jnp.sum(latent * latent)]), "chan")
    log_det = sums[0] + FRAMES * log_abs
    crop_loss = (0.5 * sums[1] - log_det) / (CH * FRAMES)
    out_grad = jnp.concatenate([second_out * scale * second - 1.0, second_out], axis=1)
    og_high, og_low = split(out_grad)
    og_ext = jnp.concatenate([og_high, og_low, og_high], axis=1)
    og_pad = jnp.concatenate(
        [jnp.zeros((frames, 88), BF16), og_high, og_low, jnp.zeros((frames, 24), BF16)], axis=1
    )

    hidden_grad = jnp.zeros((frames, width), F32)
    mel_grad = jnp.zeros((frames, EXT - CONV), F32)
    grads = []
    res_bias_grads = []
    for layer in range(LAYERS - 1, -1, -1):
        d = 2**layer
        ext, gated, dt, ds = kept[layer]
        low = hidden_grad.astype(BF16)
        res_bias_grads.append(jnp.sum(low.astype(F32), axis=0))
        fold_ext = jnp.concatenate([fold_high[layer], fold_high[layer], fold_low[layer]], axis=0)
        back = jnp.zeros((frames, EXT), F32)
        parts = []
        for s in range(shards):
            w = weights[s, layer]
            residual = jnp.concatenate([w[:, EXT : EXT + rows], w[:, EXT + rows :]], axis=0)
            gated_back = dot(og_ext, fold_ext[:, s * rows : (s + 1) * rows])
            if layer < LAYERS - 1:
                gated_back = gated_back + dot(low, residual)
            pg = jnp.concatenate(
                [gated_back * dt[s].astype(F32), gated_back * ds[s].astype(F32)], axis=1
            ).astype(BF16)
            back = back + dot(pg, w[:, :EXT])
            top = dot(pg.T, ext)
            side = dot(gated[s].T, jnp.concatenate([low, og_pad], axis=1))
            extra = side[:, width:]
            extra = extra[:, :96] + jnp.pad(extra[:, 96:104], ((0, 0), (88, 0)))
            extra = jnp.pad(extra, ((0, rows), (0, 32)))
            top = top + jnp.pad(extra, ((0, 0), (CONV, 0)))
            res = jnp.concatenate([side[:, : width // 2], side[:, width // 2 : width]], axis=0)
            parts.append(jnp.concatenate([top, res], axis=1).astype(BF16))
        grads.append(jnp.stack(parts))
        b0, b1, b2 = back[:, :width], back[:, width : 2 * width], back[:, 2 * width : 3 * width]
        mel_grad = mel_grad + back[:, CONV:]
        from_next = lax.ppermute(b0[:d].astype(BF16), "chan", down).astype(F32)
        from_prev = lax.ppermute(b2[frames - d :].astype(BF16), "chan", up).astype(F32)
        hidden_grad = (
            hidden_grad
            + b1
            + jnp.concatenate([b0[d:], from_next], axis=0)
            + jnp.concatenate([from_prev, b2[: frames - d]], axis=0)
        )
    total = lax.psum_scatter(
        jnp.stack(grads[::-1], axis=1), "chan", scatter_dimension=0, tiled=False
    )
    total = lax.psum(total, "dp").astype(F32)

    first_back = first + jnp.dot(hidden_grad, start_weight.T, precision=HIGH)
    mixed_grad = jnp.concatenate([first_back, second_out * scale], axis=1)
    audio_grad = jnp.dot(mixed_grad, inv_weight, precision=HIGH)
    rows_out = jnp.concatenate(
        [
            jnp.dot(first.T, hidden_grad, precision=HIGH),
            jnp.sum(hidden_grad, axis=0)[None],
            jnp.stack(res_bias_grads[:0:-1]),
        ],
        axis=0,
    )
    tiny = jnp.concatenate(
        [
            jnp.dot(mixed_grad.T, audio, precision=HIGH).reshape(-1),
            jnp.sum(out_grad, axis=0),
        ]
    )
    rows_out, tiny = lax.psum((rows_out, tiny), ("dp", "chan"))
    mine = lax.dynamic_slice_in_dim(rows_out, shard * rows, rows, 1)
    crops = lax.axis_size("dp") * audio_clips.shape[0]
    inv_grad = tiny[:64].reshape(8, 8) - crops * FRAMES * inverse.T
    end_bias_grad = tiny[64:]
    per_frame = jnp.concatenate([latent, audio_grad], axis=1)
    per_frame = lax.all_gather(per_frame, "chan", axis=0, tiled=True).T
    mel_out = mel_grad.reshape(mel_count, HOP, EXT - CONV).sum(axis=1)[:, :MEL]
    mel_out = lax.all_gather(mel_out, "chan", axis=0, tiled=True).T

    cond_part = total[:, :, CONV:EXT].reshape(LAYERS, 2, rows, EXT - CONV)
    e = jnp.swapaxes(cond_part[:, 0, :, 88:96], 1, 2)
    skip_grad = jnp.einsum("ko,lki->loi", final_weight, e, precision=HIGH)
    end_partial = jnp.einsum(
        "lki,loi->ko", e, skip_projection_weight.astype(F32), precision=HIGH
    )
    end_grad = (
        lax.psum_scatter(end_partial, "chan", scatter_dimension=1, tiled=True)
        + end_bias_grad[:, None] * skip_output_bias[None]
    )
    res_part = total[: LAYERS - 1, :, EXT:].reshape(LAYERS - 1, 2, rows, width // 2)
    res_grad = jnp.swapaxes(res_part, 2, 3).reshape(LAYERS - 1, width, rows)
    return (
        per_frame[:CH][None],
        log_det[None],
        crop_loss[None],
        per_frame[CH:][None],
        mel_out[None],
        inv_grad,
        mine[:4].T,
        mine[4],
        cond_part[..., :MEL],
        total[:, :, :CONV].reshape(LAYERS, 2, rows, CONV),
        cond_part[..., MEL],
        res_grad,
        mine[5:12],
        skip_grad,
        jnp.dot(end_bias_grad, final_projection_weight, precision=HIGH),
        end_grad,
        end_bias_grad,
    )


def solution(mesh):
    in_specs = (
        P("dp", None, None),
        P("dp", None, None),
        P("dp"),
        P(),
        P("chan", None),
        P("chan"),
        P(None, None, "chan", None),
        P(None, None, "chan", None),
        P(None, None, "chan"),
        P(None, None, "chan"),
        P(None, "chan"),
        P(None, None, "chan"),
        P("chan"),
        P(None, "chan"),
        P(),
    )
    out_specs = (
        P("dp", None, None),
        P("dp"),
        P("dp"),
        P("dp", None, None),
        P("dp", None, None),
        P(),
        P("chan", None),
        P("chan"),
        P(None, None, "chan", None),
        P(None, None, "chan", None),
        P(None, None, "chan"),
        P(None, None, "chan"),
        P(None, "chan"),
        P(None, None, "chan"),
        P("chan"),
        P(None, "chan"),
        P(),
    )
    return jax.shard_map(local, mesh=mesh, in_specs=in_specs, out_specs=out_specs, check_vma=False)
```

```python
import functools

import jax
import jax.numpy as jnp
from jax import lax
from jax.experimental import pallas as pl
from jax.experimental.pallas import tpu as pltpu
from jax.sharding import PartitionSpec as P

CH = 8
HALF = 4
MEL = 80
LAYERS = 8
HOP = 32
FRAMES = 2048
WIDTH = 512
CONV = 1536
EXT = 1664
PACK = 1920
SHARDS = 4
ROWS = 128
BLOCK = FRAMES // SHARDS
PAD = 16
EDGE = 128

HIGH = lax.Precision.HIGHEST
F32 = jnp.float32
BF16 = jnp.bfloat16
MESH = pl.DeviceIdType.MESH
VMEM_LIMIT = 62 << 20


def dot(a, b):
    return jnp.dot(a, b, preferred_element_type=F32)


def dot_nt(a, b):
    return lax.dot_general(a, b, (((1,), (1,)), ((), ())), preferred_element_type=F32)


def dot_tn(a, b):
    return lax.dot_general(a, b, (((0,), (0,)), ((), ())), preferred_element_type=F32)


def when(cond):
    if cond is True:
        return lambda f: f()
    return pl.when(cond)


class Place:
    def __init__(self):
        self.dp = lax.axis_index("dp")
        self.chan = lax.axis_index("chan")
        self.core = self.chan % 2
        self.side = self.chan // 2
        self.bit = self.dp % 2

    def chan_device(self, chan):
        return (self.dp, chan)

    @property
    def core_shard(self):
        return self.side * 2 + 1 - self.core

    @property
    def far_shard(self):
        return (1 - self.side) * 2 + self.core

    @property
    def diag_shard(self):
        return (1 - self.side) * 2 + 1 - self.core

    def dp_bit(self, k):
        return (self.dp // 2**k) % 2

    def dp_device(self, k):
        return (self.dp + 2**k * (1 - 2 * self.dp_bit(k)), self.chan)


def greet(devices):
    barrier = pltpu.get_barrier_semaphore()
    for device in devices:
        pl.semaphore_signal(barrier, inc=1, device_id=device, device_id_type=MESH)
    pl.semaphore_wait(barrier, len(devices))


def remote(src, dst, send, recv, device):
    return pltpu.make_async_remote_copy(
        src_ref=src, dst_ref=dst, send_sem=send, recv_sem=recv, device_id=device, device_id_type=MESH
    )


def forward_kernel(
    packed, hidden0, mel, fold, res_bias,
    weights_out, ext_out, acts_out, out,
    weights, hid, ext, acts, top, bottom,
    send, recv, own_sem, keep_sem, ext_sem, acts_sem, top_send, top_recv, bottom_send, bottom_recv,
):
    me = Place()
    core_dev = me.chan_device(me.core_shard)
    far_dev = me.chan_device(me.far_shard)
    diag_dev = me.chan_device(me.diag_shard)
    pair_dev = me.dp_device(0)
    mine = pl.ds(pl.multiple_of(me.bit * ROWS, ROWS), ROWS)
    other = pl.ds(pl.multiple_of((1 - me.bit) * ROWS, ROWS), ROWS)
    has_prev = me.chan > 0
    has_next = me.chan < SHARDS - 1
    prev_dev = me.chan_device(jnp.maximum(me.chan - 1, 0))
    next_dev = me.chan_device(jnp.minimum(me.chan + 1, SHARDS - 1))

    @pl.when(jnp.logical_not(has_prev))
    def _():
        top[...] = jnp.zeros_like(top)

    @pl.when(jnp.logical_not(has_next))
    def _():
        bottom[...] = jnp.zeros_like(bottom)

    greet([core_dev, far_dev, diag_dev, pair_dev])

    def own_copy(l):
        return pltpu.make_async_copy(packed.at[l], weights.at[l, me.chan], own_sem.at[l])

    def to_core(l):
        return remote(packed.at[l], weights.at[l, me.chan], send.at[0, l], recv.at[0, l], core_dev)

    def to_far(l):
        return remote(
            packed.at[l, mine], weights.at[l, me.chan, mine], send.at[1, l], recv.at[1, l], far_dev
        )

    def to_pair(l):
        ref = weights.at[l, me.far_shard, mine]
        return remote(ref, ref, send.at[2, l], recv.at[2, l], pair_dev)

    def to_core_a(l):
        ref = weights.at[l, me.far_shard, mine]
        return remote(ref, ref, send.at[3, l], recv.at[3, l], core_dev)

    def to_core_b(l):
        ref = weights.at[l, me.far_shard, other]
        return remote(ref, ref, send.at[4, l], recv.at[4, l], core_dev)

    def issue(l):
        to_far(l).start()
        own_copy(l).start()
        to_core(l).start()

    def relay_far(l):
        to_far(l).wait_recv()
        to_pair(l).start()
        to_core_a(l).start()

    def relay_pair(l):
        to_pair(l).wait_recv()
        to_core_b(l).start()

    def arrive(l):
        own_copy(l).wait()
        to_core(l).wait_recv()
        to_core_a(l).wait_recv()
        to_core_b(l).wait_recv()

    issue(0)
    issue(1)

    hid[pl.ds(PAD, BLOCK), :] = hidden0[...]
    out[...] = jnp.zeros_like(out)
    for slot in range(2):
        ext[slot, :, CONV:] = mel[...]

    def ext_copy(l):
        return pltpu.make_async_copy(ext.at[l % 2], ext_out.at[l], ext_sem.at[l % 2])

    def acts_copy(l):
        return pltpu.make_async_copy(acts.at[l % 2], acts_out.at[l], acts_sem.at[l % 2])

    def keep_copy(l):
        return pltpu.make_async_copy(weights.at[l], weights_out.at[l], keep_sem.at[l])

    def to_next(l, rows):
        p = l % 2
        return remote(
            ext.at[p, pl.ds(BLOCK - rows, rows), pl.ds(WIDTH, WIDTH)],
            top.at[p, pl.ds(EDGE - rows, rows)],
            top_send.at[p], top_recv.at[p], next_dev,
        )

    def to_prev(l, rows):
        p = l % 2
        return remote(
            ext.at[p, pl.ds(0, rows), pl.ds(WIDTH, WIDTH)],
            bottom.at[p, pl.ds(0, rows)],
            bottom_send.at[p], bottom_recv.at[p], prev_dev,
        )

    def by_edge(l, f):
        pl.when(l <= 4)(lambda: f(PAD))
        pl.when(l > 4)(lambda: f(EDGE))

    def compute(l):
        p = l % 2

        @pl.when(l >= 2)
        def _():
            ext_copy(l - 2).wait()
            acts_copy(l - 2).wait()

        ext[p, :, WIDTH : 2 * WIDTH] = hid[pl.ds(PAD, BLOCK), :].astype(BF16)

        def start(rows):
            pl.when(has_next)(lambda: to_next(l, rows).start())
            pl.when(has_prev)(lambda: to_prev(l, rows).start())

        def finish(rows):
            @pl.when(has_next)
            def _():
                to_next(l, rows).wait_send()
                to_prev(l, rows).wait_recv()

            @pl.when(has_prev)
            def _():
                to_prev(l, rows).wait_send()
                to_next(l, rows).wait_recv()

        by_edge(l, start)
        by_edge(l, finish)
        hid[pl.ds(0, PAD), :] = top[p, pl.ds(EDGE - PAD, PAD), :].astype(F32)
        hid[pl.ds(PAD + BLOCK, PAD), :] = bottom[p, pl.ds(0, PAD), :].astype(F32)
        for layer in range(LAYERS):
            d = 2**layer

            @pl.when(l == layer)
            def _():
                if d < PAD:
                    ext[p, :, :WIDTH] = hid[pl.ds(PAD - d, BLOCK), :].astype(BF16)
                    ext[p, :, 2 * WIDTH : CONV] = hid[pl.ds(PAD + d, BLOCK), :].astype(BF16)
                else:
                    ext[p, :d, :WIDTH] = top[p, EDGE - d :, :]
                    ext[p, d:, :WIDTH] = ext[p, : BLOCK - d, WIDTH : 2 * WIDTH]
                    ext[p, BLOCK - d :, 2 * WIDTH : CONV] = bottom[p, :d, :]
                    ext[p, : BLOCK - d, 2 * WIDTH : CONV] = ext[p, d:, WIDTH : 2 * WIDTH]

        ext_copy(l).start()

        def one(s, carry):
            pre = dot_nt(ext[p], weights[l, s, :, :EXT])
            t = jnp.tanh(pre[:, :ROWS])
            g = 0.5 * jnp.tanh(0.5 * pre[:, ROWS:]) + 0.5
            tg = t * g
            acts[p, s, 0] = tg.astype(BF16)
            acts[p, s, 1] = (g - t * tg).astype(BF16)
            acts[p, s, 2] = (tg * (1.0 - g)).astype(BF16)
            return carry

        lax.fori_loop(0, SHARDS, one, 0)
        acts_copy(l).start()
        gated = jnp.concatenate([acts[p, s, 0] for s in range(SHARDS)], axis=1)
        out[...] += dot_nt(gated, fold[l])

        @pl.when(l < LAYERS - 1)
        def _():
            for h in range(2):
                res = jnp.concatenate(
                    [weights[l, s, :, EXT + h * ROWS : EXT + (h + 1) * ROWS] for s in range(SHARDS)], axis=1
                )
                cols = slice(h * 2 * ROWS, (h + 1) * 2 * ROWS)
                hid[pl.ds(PAD, BLOCK), cols] += dot_nt(gated, res) + res_bias[pl.ds(l, 1), cols]

    relay_far(0)

    def step(l, carry):
        pl.when(l + 2 < LAYERS)(lambda: issue(l + 2))
        pl.when(l + 1 < LAYERS)(lambda: relay_far(l + 1))
        relay_pair(l)
        arrive(l)
        keep_copy(l).start()
        compute(l)
        return carry

    lax.fori_loop(0, LAYERS, step, 0)
    for l in (LAYERS - 2, LAYERS - 1):
        ext_copy(l).wait()
        acts_copy(l).wait()

    def drain(l, carry):
        to_core(l).wait_send()
        to_far(l).wait_send()
        to_pair(l).wait_send()
        to_core_a(l).wait_send()
        to_core_b(l).wait_send()
        keep_copy(l).wait()
        return carry

    lax.fori_loop(0, LAYERS, drain, 0)


def run_forward(packed, hidden0, mel, fold, res_bias):
    vmem = pl.BlockSpec(memory_space=pltpu.VMEM)
    hbm = pl.BlockSpec(memory_space=pl.ANY)
    dma = pltpu.SemaphoreType.DMA
    return pl.pallas_call(
        forward_kernel,
        out_shape=(
            jax.ShapeDtypeStruct((LAYERS, SHARDS, 2 * ROWS, PACK), BF16),
            jax.ShapeDtypeStruct((LAYERS, BLOCK, EXT), BF16),
            jax.ShapeDtypeStruct((LAYERS, SHARDS, 3, BLOCK, ROWS), BF16),
            jax.ShapeDtypeStruct((BLOCK, 2 * CH), F32),
        ),
        in_specs=[hbm, vmem, vmem, vmem, vmem],
        out_specs=(hbm, hbm, hbm, vmem),
        scratch_shapes=[
            pltpu.VMEM((LAYERS, SHARDS, 2 * ROWS, PACK), BF16),
            pltpu.VMEM((PAD + BLOCK + PAD, WIDTH), F32),
            pltpu.VMEM((2, BLOCK, EXT), BF16),
            pltpu.VMEM((2, SHARDS, 3, BLOCK, ROWS), BF16),
            pltpu.VMEM((2, EDGE, WIDTH), BF16),
            pltpu.VMEM((2, EDGE, WIDTH), BF16),
            dma((5, LAYERS)), dma((5, LAYERS)), dma((LAYERS,)), dma((LAYERS,)), dma((2,)), dma((2,)),
            dma((2,)), dma((2,)), dma((2,)), dma((2,)),
        ],
        compiler_params=pltpu.CompilerParams(
            collective_id=0, has_side_effects=True, vmem_limit_bytes=VMEM_LIMIT
        ),
    )(packed, hidden0, mel, fold, res_bias)


def levels_of(dp_size):
    levels, rows, bit = [], 2 * ROWS, 0
    while 2**bit < dp_size:
        after = rows // 2 if rows > PAD else rows
        levels.append((bit, rows, after))
        rows, bit = after, bit + 1
    return levels


def backward_kernel(
    levels,
    weights, ext_in, acts_in, og, fold,
    total, grad_out, mel_out, bias_out,
    wbuf, abuf, ext, low, tap0, tap2, sums, from_core, from_far, edge_out, edge_in, *rest,
):
    level_bufs = rest[: len(levels)]
    (w_sem, a_sem, e_sem, core_send, core_recv, credit, far_send, far_recv,
     rs_send, rs_recv, ag_send, ag_recv, edge_send, edge_recv, out_sem) = rest[len(levels) :]
    me = Place()
    core_dev = me.chan_device(me.core_shard)
    far_dev = me.chan_device(me.far_shard)
    diag_dev = me.chan_device(me.diag_shard)
    has_prev = me.chan > 0
    has_next = me.chan < SHARDS - 1
    prev_dev = me.chan_device(jnp.maximum(me.chan - 1, 0))
    next_dev = me.chan_device(jnp.minimum(me.chan + 1, SHARDS - 1))
    edge_in[...] = jnp.zeros_like(edge_in)
    greet([core_dev, far_dev, diag_dev] + [me.dp_device(bit) for bit, _, _ in levels])

    def shard_of(j):
        core = jnp.where(j < 2, 1 - me.core, me.core)
        return (j % 2) * 2 + core

    def w_copy(q):
        l, s = LAYERS - 1 - q // SHARDS, shard_of(q % SHARDS)
        return pltpu.make_async_copy(weights.at[l, s], wbuf.at[q % 2], w_sem.at[q % 2])

    def a_copy(q):
        l, s = LAYERS - 1 - q // SHARDS, shard_of(q % SHARDS)
        return pltpu.make_async_copy(acts_in.at[l, s], abuf.at[q % 2], a_sem.at[q % 2])

    def e_copy(i):
        return pltpu.make_async_copy(ext_in.at[LAYERS - 1 - i], ext.at[i % 2], e_sem.at[i % 2])

    def kept(i, ys):
        return 4 + 2 * i + ys

    def to_core(i, ys):
        p = i % 2
        return remote(
            sums.at[2 * p + ys], from_core.at[2 * p + ys], core_send.at[p, ys], core_recv.at[p, ys], core_dev
        )

    def to_far(i):
        return remote(
            sums.at[kept(i, 1 - me.side)], from_far.at[i], far_send.at[i], far_recv.at[i], far_dev
        )

    def add_rows(i, base, rows, src, src_at):
        own = kept(i, me.side)
        chunk = min(rows, 32)

        def body(k, carry):
            at = pl.ds(pl.multiple_of(base + k * chunk, PAD), chunk)
            sums[own, at, :] = sums[own, at, :] + src[src_at, pl.ds(pl.multiple_of(k * chunk, PAD), chunk), :]
            return carry

        lax.fori_loop(0, rows // chunk, body, 0)

    def bases():
        base, got = 0, []
        for bit, rows, after in levels:
            got.append(base)
            if after < rows:
                base = base + me.dp_bit(bit) * after
        return got + [base]

    base_at = bases()

    def rs(k, i):
        bit, rows, after = levels[k]
        start = base_at[k]
        if after < rows:
            start = start + (1 - me.dp_bit(bit)) * after
        at = pl.ds(pl.multiple_of(start, PAD), after)
        return remote(
            sums.at[kept(i, me.side), at], level_bufs[k].at[i], rs_send.at[k, i], rs_recv.at[k, i],
            me.dp_device(bit),
        )

    def ag_out(k, i):
        bit, rows, after = levels[k]
        ref = total.at[LAYERS - 1 - i, pl.ds(pl.multiple_of(base_at[k + 1], PAD), after)]
        return remote(ref, ref, ag_send.at[k, i], ag_recv.at[k, i], me.dp_device(bit))

    def ag_in(k, i):
        bit, rows, after = levels[k]
        start = base_at[k] + (1 - me.dp_bit(bit)) * after
        ref = total.at[LAYERS - 1 - i, pl.ds(pl.multiple_of(start, PAD), after)]
        return remote(ref, ref, ag_send.at[k, i], ag_recv.at[k, i], me.dp_device(bit))

    halving = [k for k, (bit, rows, after) in enumerate(levels) if after < rows]

    def out_copy(i):
        at = pl.ds(pl.multiple_of(base_at[-1], PAD), levels[-1][2] if levels else 2 * ROWS)
        return pltpu.make_async_copy(
            sums.at[kept(i, me.side), at], total.at[LAYERS - 1 - i, at], out_sem.at[i]
        )

    def stage_core(i):
        p = i % 2
        for ys in (1 - me.side, me.side):
            to_core(i, ys).wait_recv()

            def body(k, carry):
                at = pl.ds(pl.multiple_of(k * 32, 32), 32)
                slot = kept(i, ys)
                sums[slot, at, :] = sums[slot, at, :] + from_core[2 * p + ys, at, :]
                return carry

            lax.fori_loop(0, 2 * ROWS // 32, body, 0)
            pl.semaphore_signal(credit.at[ys], inc=1, device_id=core_dev, device_id_type=MESH)
            if ys is not me.side:
                to_far(i).start()

    def stage_far(i):
        to_far(i).wait_recv()
        add_rows(i, 0, 2 * ROWS, from_far, i)
        rs(0, i).start()

    def ag_first(i):
        out_copy(i).start()
        out_copy(i).wait()
        if halving:
            ag_out(halving[-1], i).start()

    def stage_rs(k, i):
        bit, rows, after = levels[k]
        rs(k, i).wait_recv()
        if after == rows:
            rs(k, i).wait_send()
        add_rows(i, base_at[k + 1], after, level_bufs[k], i)
        if k + 1 < len(levels):
            rs(k + 1, i).start()
        else:
            ag_first(i)

    def stage_ag(n, i):
        k = halving[n]
        ag_in(k, i).wait_recv()
        if n > 0:
            ag_out(halving[n - 1], i).start()

    def to_prev(i, rows):
        p = i % 2
        return remote(
            edge_out.at[0, pl.ds(0, rows)], edge_in.at[p, 0, pl.ds(0, rows)],
            edge_send.at[0], edge_recv.at[p, 0], prev_dev,
        )

    def to_next(i, rows):
        p = i % 2
        return remote(
            edge_out.at[1, pl.ds(EDGE - rows, rows)], edge_in.at[p, 1, pl.ds(EDGE - rows, rows)],
            edge_send.at[1], edge_recv.at[p, 1], next_dev,
        )

    def by_edge(i, f):
        pl.when(i < 3)(lambda: f(EDGE))
        pl.when(i >= 3)(lambda: f(PAD))

    def compute(i):
        l = LAYERS - 1 - i
        p = i % 2
        pl.when(i + 1 < LAYERS)(lambda: e_copy(i + 1).start())
        now = grad_out[...].astype(BF16)
        low[:, :WIDTH] = now
        bias_out[pl.ds(l, 1), :] = jnp.sum(now.astype(F32), axis=0, keepdims=True)
        tap0[pl.ds(0, BLOCK), :] = jnp.zeros((BLOCK, WIDTH), F32)
        tap2[pl.ds(EDGE, BLOCK), :] = jnp.zeros((BLOCK, WIDTH), F32)
        e_copy(i).wait()

        def one(j, carry):
            q = i * SHARDS + j
            b = q % 2
            s = shard_of(j)
            pl.when(q + 1 < LAYERS * SHARDS)(lambda: w_copy(q + 1).start())
            pl.when(q + 1 < LAYERS * SHARDS)(lambda: a_copy(q + 1).start())

            @pl.when((j < 2) & (i >= 2))
            def _():
                to_core(i - 2, j).wait_send()

            w_copy(q).wait()
            a_copy(q).wait()
            slot = jnp.where(j < 2, 2 * p + j, kept(i, j - 2))
            gated = abuf[b, 0]
            res = jnp.concatenate([wbuf[b, :, EXT : EXT + ROWS], wbuf[b, :, EXT + ROWS :]], axis=0)
            back = dot(low[:, :WIDTH], res) + dot(low[:, WIDTH:], fold[l, s])
            pg = jnp.concatenate(
                [(back * abuf[b, 1].astype(F32)).astype(BF16), (back * abuf[b, 2].astype(F32)).astype(BF16)],
                axis=1,
            )
            tap0[pl.ds(0, BLOCK), :] += dot(pg, wbuf[b, :, :WIDTH])
            grad_out[...] += dot(pg, wbuf[b, :, WIDTH : 2 * WIDTH])
            tap2[pl.ds(EDGE, BLOCK), :] += dot(pg, wbuf[b, :, 2 * WIDTH : CONV])
            mel_out[...] += dot(pg, wbuf[b, :, CONV:EXT])
            for k in range(3):
                cols = slice(k * WIDTH, (k + 1) * WIDTH)
                sums[slot, :, cols] = dot_tn(pg, ext[p, :, cols]).astype(BF16)
            side = dot_tn(gated, low[...])
            extra = side[:, WIDTH:]
            extra = extra + pltpu.roll(extra, ROWS - CH, 1)
            lane = lax.broadcasted_iota(jnp.int32, (ROWS, ROWS), 1)
            extra = jnp.where((lane >= 88) & (lane < 96), extra, 0.0)
            top = dot_tn(pg, ext[p, :, CONV:])
            sums[slot, :ROWS, CONV:EXT] = (top[:ROWS] + extra).astype(BF16)
            sums[slot, ROWS:, CONV:EXT] = top[ROWS:].astype(BF16)
            sums[slot, :ROWS, EXT:] = side[:, : 2 * ROWS].astype(BF16)
            sums[slot, ROWS:, EXT:] = side[:, 2 * ROWS : WIDTH].astype(BF16)

            @pl.when(j < 2)
            def _():
                pl.when(i >= 2)(lambda: pl.semaphore_wait(credit.at[j], 1))
                to_core(i, j).start()

            return carry

        lax.fori_loop(0, SHARDS, one, 0)

        edge_out[0] = tap0[pl.ds(0, EDGE), :].astype(BF16)
        edge_out[1] = tap2[pl.ds(BLOCK, EDGE), :].astype(BF16)

        def start(rows):
            pl.when(has_next)(lambda: to_next(i, rows).start())
            pl.when(has_prev)(lambda: to_prev(i, rows).start())

        def finish(rows):
            @pl.when(has_next)
            def _():
                to_next(i, rows).wait_send()
                to_prev(i, rows).wait_recv()

            @pl.when(has_prev)
            def _():
                to_prev(i, rows).wait_send()
                to_next(i, rows).wait_recv()

        by_edge(i, start)
        by_edge(i, finish)
        tap0[pl.ds(BLOCK, EDGE), :] = edge_in[p, 0].astype(F32)
        tap2[pl.ds(0, EDGE), :] = edge_in[p, 1].astype(F32)
        for layer in range(LAYERS):
            d = 2**layer

            @pl.when(l == layer)
            def _():
                grad_out[...] += tap0[pl.ds(d, BLOCK), :] + tap2[pl.ds(EDGE - d, BLOCK), :]

    e_copy(0).start()
    w_copy(0).start()
    a_copy(0).start()
    grad_out[...] = jnp.zeros_like(grad_out)
    mel_out[...] = jnp.zeros_like(mel_out)
    low[:, WIDTH:] = og[...]

    stages = [stage_core, stage_far]
    stages += [functools.partial(stage_rs, k) for k in range(len(levels))]
    stages += [functools.partial(stage_ag, n) for n in range(len(halving) - 1, -1, -1)]

    def step(i, carry):
        for lag in range(len(stages) - 1, 0, -1):
            pl.when((i >= lag) & (i < LAYERS + lag))(functools.partial(stages[lag], i - lag))

        @pl.when(i < LAYERS)
        def _():
            compute(i)
            stage_core(i)

        return carry

    lax.fori_loop(0, LAYERS + len(stages) - 1, step, 0)

    for i in (LAYERS - 2, LAYERS - 1):
        for ys in range(2):
            to_core(i, ys).wait_send()
            pl.semaphore_wait(credit.at[ys], 1)

    def drain(i, carry):
        to_far(i).wait_send()
        for k, (bit, rows, after) in enumerate(levels):
            if after < rows:
                rs(k, i).wait_send()
                ag_out(k, i).wait_send()
        return carry

    lax.fori_loop(0, LAYERS, drain, 0)


def run_backward(dp_size, weights, ext, acts, og, fold):
    levels = levels_of(dp_size)
    vmem = pl.BlockSpec(memory_space=pltpu.VMEM)
    hbm = pl.BlockSpec(memory_space=pl.ANY)
    dma = pltpu.SemaphoreType.DMA
    block = (2 * ROWS, PACK)
    n = max(len(levels), 1)
    return pl.pallas_call(
        functools.partial(backward_kernel, levels),
        out_shape=(
            jax.ShapeDtypeStruct((LAYERS,) + block, BF16),
            jax.ShapeDtypeStruct((BLOCK, WIDTH), F32),
            jax.ShapeDtypeStruct((BLOCK, EXT - CONV), F32),
            jax.ShapeDtypeStruct((LAYERS, WIDTH), F32),
        ),
        in_specs=[hbm, hbm, hbm, vmem, vmem],
        out_specs=(hbm, vmem, vmem, vmem),
        scratch_shapes=[
            pltpu.VMEM((2,) + block, BF16),
            pltpu.VMEM((2, 3, BLOCK, ROWS), BF16),
            pltpu.VMEM((2, BLOCK, EXT), BF16),
            pltpu.VMEM((BLOCK, WIDTH + ROWS), BF16),
            pltpu.VMEM((BLOCK + EDGE, WIDTH), F32),
            pltpu.VMEM((EDGE + BLOCK, WIDTH), F32),
            pltpu.VMEM((4 + 2 * LAYERS,) + block, BF16),
            pltpu.VMEM((4,) + block, BF16),
            pltpu.VMEM((LAYERS,) + block, BF16),
            pltpu.VMEM((2, EDGE, WIDTH), BF16),
            pltpu.VMEM((2, 2, EDGE, WIDTH), BF16),
        ]
        + [pltpu.VMEM((LAYERS, after, PACK), BF16) for _, _, after in levels]
        + [
            dma((2,)), dma((2,)), dma((2,)), dma((2, 2)), dma((2, 2)), pltpu.SemaphoreType.REGULAR((2,)),
            dma((LAYERS,)), dma((LAYERS,)),
            dma((n, LAYERS)), dma((n, LAYERS)), dma((n, LAYERS)), dma((n, LAYERS)),
            dma((2,)), dma((2, 2)), dma((LAYERS,)),
        ],
        compiler_params=pltpu.CompilerParams(
            collective_id=1, has_side_effects=True, vmem_limit_bytes=VMEM_LIMIT
        ),
    )(weights, ext, acts, og, fold)


def invert_small(matrix):
    size_of = matrix.shape[0]
    augmented = jnp.concatenate([matrix, jnp.eye(size_of, dtype=F32)], axis=1)
    log_total = F32(0.0)
    for column in range(size_of):
        pivot = augmented[column, column]
        log_total = log_total + jnp.log(pivot)
        pivot_row = augmented[column] / pivot
        factor = augmented[:, column]
        augmented = augmented - factor[:, None] * pivot_row[None, :]
        augmented = augmented.at[column].set(pivot_row)
    return (augmented[:, size_of:], log_total)


def split(values):
    high = values.astype(BF16)
    return high, (values - high.astype(F32)).astype(BF16)


def local(
    audio_clips,
    mel_frames,
    crop_offsets,
    inv_weight,
    initial_projection_weight,
    start_bias,
    cond_weight,
    in_weight,
    in_bias,
    res_weight,
    res_bias,
    skip_projection_weight,
    skip_output_bias,
    final_projection_weight,
    end_bias,
):
    shards = lax.axis_size("chan")
    shard = lax.axis_index("chan")
    rows = initial_projection_weight.shape[0]
    width = rows * shards
    frames = FRAMES // shards
    mel_count = frames // HOP
    up = [(i, i + 1) for i in range(shards - 1)]
    down = [(i + 1, i) for i in range(shards - 1)]

    offset = crop_offsets[0]
    audio = lax.dynamic_slice(audio_clips[0], (0, offset * HOP + shard * frames), (CH, frames)).T
    mel = lax.dynamic_slice(mel_frames[0], (0, offset + shard * mel_count), (MEL, mel_count)).T
    mixed = jnp.dot(audio, inv_weight.T, precision=HIGH)
    first, second = mixed[:, :HALF], mixed[:, HALF:]

    small = jnp.concatenate(
        [
            initial_projection_weight.T,
            start_bias[None],
            res_bias,
            final_projection_weight,
            skip_output_bias[None],
        ],
        axis=0,
    )
    small = lax.all_gather(small, "chan", axis=1, tiled=True)
    start_weight = small[:4]
    start = small[4]
    residual_bias = small[5:12]
    final_weight = small[12:20]
    skip_bias = small[20]
    fold_local = jnp.einsum(
        "ko,loi->lki", final_weight, skip_projection_weight.astype(F32), precision=HIGH
    )
    fold = lax.all_gather(fold_local, "chan", axis=2, tiled=True)
    fold_high, fold_low = split(fold)
    const = jnp.dot(final_weight, skip_bias, precision=HIGH) + end_bias

    bias_high, bias_low = split(in_bias)
    packed = jnp.concatenate(
        [
            in_weight.reshape(LAYERS, 2 * rows, CONV),
            jnp.concatenate(
                [
                    cond_weight,
                    bias_high[..., None],
                    bias_low[..., None],
                    jnp.zeros((LAYERS, 2, rows, EXT - CONV - MEL - 2), BF16),
                ],
                axis=-1,
            ).reshape(LAYERS, 2 * rows, EXT - CONV),
            jnp.pad(
                res_weight.reshape(LAYERS - 1, 2, width // 2, rows)
                .swapaxes(1, 2)
                .reshape(LAYERS - 1, width // 2, 2 * rows),
                ((0, 1), (0, 0), (0, 0)),
            ),
        ],
        axis=2,
    )

    mel_part = jnp.concatenate(
        [
            jnp.repeat(mel, HOP, axis=0),
            jnp.ones((frames, 2), BF16),
            jnp.zeros((frames, EXT - CONV - MEL - 2), BF16),
        ],
        axis=1,
    )
    hidden = jnp.dot(first, start_weight, precision=HIGH) + start
    weights, ext, acts, out = run_forward(
        packed,
        hidden,
        mel_part,
        jnp.concatenate([fold_high, fold_low], axis=1),
        jnp.pad(residual_bias, ((0, 1), (0, 0))),
    )
    out = out[:, :CH] + out[:, CH:]
    out = out + const
    log_scale, shift = out[:, :HALF], out[:, HALF:]
    scale = jnp.exp(log_scale)
    second_out = scale * second + shift
    latent = jnp.concatenate([first, second_out], axis=1)
    inverse, log_abs = invert_small(inv_weight)
    sums = lax.psum(jnp.stack([jnp.sum(log_scale), jnp.sum(latent * latent)]), "chan")
    log_det = sums[0] + FRAMES * log_abs
    crop_loss = (0.5 * sums[1] - log_det) / (CH * FRAMES)
    out_grad = jnp.concatenate([second_out * scale * second - 1.0, second_out], axis=1)
    og_high, og_low = split(out_grad)
    og = jnp.concatenate(
        [jnp.zeros((frames, 88), BF16), og_high, og_low, og_high, jnp.zeros((frames, 16), BF16)], axis=1
    )
    fold_rows = jnp.pad(jnp.concatenate([fold_high, fold_high, fold_low], axis=1), ((0, 0), (88, 16), (0, 0)))
    fold_rows = fold_rows.reshape(LAYERS, rows, shards, rows).swapaxes(1, 2)
    total, hidden_grad, mel_grad, res_bias_grads = run_backward(
        lax.axis_size("dp"), weights, ext, acts, og, fold_rows
    )
    total = total.astype(F32)

    first_back = first + jnp.dot(hidden_grad, start_weight.T, precision=HIGH)
    mixed_grad = jnp.concatenate([first_back, second_out * scale], axis=1)
    audio_grad = jnp.dot(mixed_grad, inv_weight, precision=HIGH)
    rows_out = jnp.concatenate(
        [
            jnp.dot(first.T, hidden_grad, precision=HIGH),
            jnp.sum(hidden_grad, axis=0)[None],
            res_bias_grads[: LAYERS - 1],
        ],
        axis=0,
    )
    tiny = jnp.concatenate(
        [
            jnp.dot(mixed_grad.T, audio, precision=HIGH).reshape(-1),
            jnp.sum(out_grad, axis=0),
        ]
    )
    rows_out, tiny = lax.psum((rows_out, tiny), ("dp", "chan"))
    mine = lax.dynamic_slice_in_dim(rows_out, shard * rows, rows, 1)
    crops = lax.axis_size("dp") * audio_clips.shape[0]
    inv_grad = tiny[:64].reshape(8, 8) - crops * FRAMES * inverse.T
    end_bias_grad = tiny[64:]
    per_frame = jnp.concatenate([latent, audio_grad], axis=1)
    per_frame = lax.all_gather(per_frame, "chan", axis=0, tiled=True).T
    mel_out = mel_grad.reshape(mel_count, HOP, EXT - CONV).sum(axis=1)[:, :MEL]
    mel_out = lax.all_gather(mel_out, "chan", axis=0, tiled=True).T

    cond_part = total[:, :, CONV:EXT].reshape(LAYERS, 2, rows, EXT - CONV)
    e = jnp.swapaxes(cond_part[:, 0, :, 88:96], 1, 2)
    skip_grad = jnp.einsum("ko,lki->loi", final_weight, e, precision=HIGH)
    end_partial = jnp.einsum(
        "lki,loi->ko", e, skip_projection_weight.astype(F32), precision=HIGH
    )
    end_grad = (
        lax.psum_scatter(end_partial, "chan", scatter_dimension=1, tiled=True)
        + end_bias_grad[:, None] * skip_output_bias[None]
    )
    res_part = total[: LAYERS - 1, :, EXT:].reshape(LAYERS - 1, 2, rows, width // 2)
    res_grad = jnp.swapaxes(res_part, 2, 3).reshape(LAYERS - 1, width, rows)
    return (
        per_frame[:CH][None],
        log_det[None],
        crop_loss[None],
        per_frame[CH:][None],
        mel_out[None],
        inv_grad,
        mine[:4].T,
        mine[4],
        cond_part[..., :MEL],
        total[:, :, :CONV].reshape(LAYERS, 2, rows, CONV),
        cond_part[..., MEL],
        res_grad,
        mine[5:12],
        skip_grad,
        jnp.dot(end_bias_grad, final_projection_weight, precision=HIGH),
        end_grad,
        end_bias_grad,
    )


def solution(mesh):
    in_specs = (
        P("dp", None, None),
        P("dp", None, None),
        P("dp"),
        P(),
        P("chan", None),
        P("chan"),
        P(None, None, "chan", None),
        P(None, None, "chan", None),
        P(None, None, "chan"),
        P(None, None, "chan"),
        P(None, "chan"),
        P(None, None, "chan"),
        P("chan"),
        P(None, "chan"),
        P(),
    )
    out_specs = (
        P("dp", None, None),
        P("dp"),
        P("dp"),
        P("dp", None, None),
        P("dp", None, None),
        P(),
        P("chan", None),
        P("chan"),
        P(None, None, "chan", None),
        P(None, None, "chan", None),
        P(None, None, "chan"),
        P(None, None, "chan"),
        P(None, "chan"),
        P(None, None, "chan"),
        P("chan"),
        P(None, "chan"),
        P(),
    )
    return jax.shard_map(local, mesh=mesh, in_specs=in_specs, out_specs=out_specs, check_vma=False)
```

```python
import functools

import jax
import jax.numpy as jnp
from jax import lax
from jax.experimental import pallas as pl
from jax.experimental.pallas import tpu as pltpu
from jax.sharding import PartitionSpec as P

CH = 8
HALF = 4
MEL = 80
LAYERS = 8
HOP = 32
FRAMES = 2048
WIDTH = 512
CONV = 1536
EXT = 1664
PACK = 1920
SHARDS = 4
ROWS = 128
BLOCK = FRAMES // SHARDS
PAD = 16
EDGE = 128

HIGH = lax.Precision.HIGHEST
F32 = jnp.float32
BF16 = jnp.bfloat16
MESH = pl.DeviceIdType.MESH
VMEM_LIMIT = 62 << 20


def dot(a, b):
    return jnp.dot(a, b, preferred_element_type=F32)


def dot_nt(a, b):
    return lax.dot_general(a, b, (((1,), (1,)), ((), ())), preferred_element_type=F32)


def dot_tn(a, b):
    return lax.dot_general(a, b, (((0,), (0,)), ((), ())), preferred_element_type=F32)


def when(cond):
    if cond is True:
        return lambda f: f()
    return pl.when(cond)


class Place:
    def __init__(self):
        self.dp = lax.axis_index("dp")
        self.chan = lax.axis_index("chan")
        self.core = self.chan % 2
        self.side = self.chan // 2
        self.bit = self.dp % 2

    def chan_device(self, chan):
        return (self.dp, chan)

    @property
    def core_shard(self):
        return self.side * 2 + 1 - self.core

    @property
    def far_shard(self):
        return (1 - self.side) * 2 + self.core

    @property
    def diag_shard(self):
        return (1 - self.side) * 2 + 1 - self.core

    def dp_bit(self, k):
        return (self.dp // 2**k) % 2

    def dp_device(self, k):
        return (self.dp + 2**k * (1 - 2 * self.dp_bit(k)), self.chan)


def greet(devices):
    barrier = pltpu.get_barrier_semaphore()
    for device in devices:
        pl.semaphore_signal(barrier, inc=1, device_id=device, device_id_type=MESH)
    pl.semaphore_wait(barrier, len(devices))


def remote(src, dst, send, recv, device):
    return pltpu.make_async_remote_copy(
        src_ref=src, dst_ref=dst, send_sem=send, recv_sem=recv, device_id=device, device_id_type=MESH
    )


def levels_of(dp_size):
    levels, rows, bit = [], 2 * ROWS, 0
    while 2**bit < dp_size:
        after = rows // 2 if rows > PAD else rows
        levels.append((bit, rows, after))
        rows, bit = after, bit + 1
    return levels


ACROSS = pl.ds(0, 7 * ROWS)
ALONG = pl.ds(7 * ROWS, PACK - 7 * ROWS)
DEPTH = 4


def mesh_line(levels):
    return len(levels) == 3


def line_shapes():
    a, b = ACROSS.size, ALONG.size
    return [(2, ROWS, a), (ROWS, a), (ROWS // 2, a), (2 * ROWS, b), (ROWS, b), (ROWS // 2, b)]


class Lane:
    def __init__(self, buf, send, recv, credit, device):
        self.buf, self.send, self.recv, self.credit, self.device = buf, send, recv, credit, device

    def copy(self, i, src):
        d = i % DEPTH
        return remote(src, self.buf.at[d], self.send.at[d], self.recv.at[d], self.device)

    def start(self, i, src):
        @pl.when(i >= DEPTH)
        def _():
            self.copy(i, src).wait_send()
            pl.semaphore_wait(self.credit, 1)

        self.copy(i, src).start()

    def wait(self, i):
        d = i % DEPTH
        remote(self.buf.at[d], self.buf.at[d], self.send.at[d], self.recv.at[d], self.device).wait_recv()

    def free(self):
        pl.semaphore_signal(self.credit, inc=1, device_id=self.device, device_id_type=MESH)

    def finish(self):
        for d in range(DEPTH):
            ref = self.buf.at[d]
            remote(ref, ref, self.send.at[d], self.recv.at[d], self.device).wait_send()
            pl.semaphore_wait(self.credit, 1)


def split(values):
    high = values.astype(BF16).astype(F32)
    return high, values - high


def flow_kernel(
    levels,
    in_weight, cond_weight, res_weight, skip_weight, audio, mel, inv_weight, local_small, end_bias,
    total, weights_out, ext_out, acts_out, frames_out, mel_out, sums_out, inverse_out, log_out, small, end_out,
    mine_out, end_own_out,
    shared, hid, ext, acts, top, bottom, wbuf, low, low_t, tap0, tap2, grad, mel_sum, edge_out, edge_in,
    fold, keep, og_rows, out, small_in, end_in, *rest,
):
    line = mesh_line(levels)
    n_bufs = len(line_shapes()) if line else len(levels)
    level_bufs = rest[:n_bufs]
    (
        own_sem, send, recv, keep_sem, ext_sem, acts_sem,
        top_send, top_recv, bottom_send, bottom_recv,
        small_send, small_recv, fold_send, fold_recv,
        phase, w_sem, core_send, core_recv, credit, far_send, far_recv,
        rs_send, rs_recv, ag_send, ag_recv, out_sem, edge_send, edge_recv,
        sum_send, sum_recv, end_send, end_recv, frames_send, frames_recv, mel_send, mel_recv,
        lane_send, lane_recv, lane_credit, way_send, way_recv,
    ) = rest[n_bufs:]
    me = Place()
    core_dev = me.chan_device(me.core_shard)
    far_dev = me.chan_device(me.far_shard)
    diag_dev = me.chan_device(me.diag_shard)
    chan_devs = [core_dev, far_dev, diag_dev]
    has_prev = me.chan > 0
    has_next = me.chan < SHARDS - 1
    prev_dev = me.chan_device(jnp.maximum(me.chan - 1, 0))
    next_dev = me.chan_device(jnp.minimum(me.chan + 1, SHARDS - 1))

    quarter = ROWS // 2
    xb, zb = me.dp_bit(0), me.dp_bit(1)

    def quarter_at(x, z, first=0, rows=quarter):
        return pl.ds(pl.multiple_of((x * 2 + z) * quarter + first, 32), rows)

    half_quarter = quarter // 2

    def own_copies(l):
        dst = shared.at[l * SHARDS + me.chan]
        return [
            pltpu.make_async_copy(in_weight.at[l], dst.at[:, pl.ds(0, CONV)], own_sem.at[0, l]),
            pltpu.make_async_copy(cond_weight.at[l], dst.at[:, pl.ds(CONV, ROWS)], own_sem.at[1, l]),
        ]

    def res_copies(l):
        dst = shared.at[l * SHARDS + me.chan]
        return [
            pltpu.make_async_copy(
                res_weight.at[l, pl.ds(h * 2 * ROWS, 2 * ROWS)],
                dst.at[:, pl.ds(EXT + h * ROWS, ROWS)],
                own_sem.at[2 + h, l],
            )
            for h in range(2)
        ]

    def link(kind, l, shard, at, device):
        ref = shared.at[l * SHARDS + shard, at] if at is not None else shared.at[l * SHARDS + shard]
        return remote(ref, ref, send.at[kind, l], recv.at[kind, l], device)

    x_dev, z_dev = me.dp_device(0), me.dp_device(1)

    def far_a(l, shard):
        return link(0, l, shard, quarter_at(xb, zb), far_dev)

    def far_b(l, shard):
        return link(1, l, shard, quarter_at(1 - xb, 1 - zb, 0, half_quarter), far_dev)

    def x_a(l, x):
        return link(2, l, me.far_shard, quarter_at(x, zb), x_dev)

    def z_a(l, z):
        return link(3, l, me.far_shard, quarter_at(xb, z), z_dev)

    def x_b(l, x):
        return link(4, l, me.far_shard, quarter_at(x, 1 - zb, half_quarter, half_quarter), x_dev)

    def core_a(l, shard):
        return link(5, l, shard, None, core_dev)

    def core_b(l, shard):
        return link(6, l, shard, None, core_dev)

    def issue(l):
        for copy in own_copies(l):
            copy.wait()

        @pl.when(l < LAYERS - 1)
        def _():
            for copy in res_copies(l):
                copy.wait()

        far_a(l, me.chan).start()
        far_b(l, me.chan).start()
        core_a(l, me.chan).start()

    def relay_a(l):
        far_a(l, me.far_shard).wait_recv()
        x_a(l, xb).start()
        z_a(l, zb).start()
        pl.when(l + 1 < LAYERS)(lambda: issue(l + 1))

    def relay_b(l):
        z_a(l, 1 - zb).wait_recv()
        x_b(l, xb).start()

    def relay_c(l):
        far_b(l, me.far_shard).wait_recv()
        x_a(l, 1 - xb).wait_recv()
        x_b(l, 1 - xb).wait_recv()
        core_b(l, me.far_shard).start()

    def arrive(l):
        core_a(l, me.core_shard).wait_recv()
        core_b(l, me.diag_shard).wait_recv()

    shared[(LAYERS - 1) * SHARDS + me.chan, :, EXT:] = jnp.zeros((2 * ROWS, 2 * ROWS), BF16)

    def first_copies(l, carry):
        for copy in own_copies(l):
            copy.start()

        @pl.when(l < LAYERS - 1)
        def _():
            for copy in res_copies(l):
                copy.start()

        return carry

    lax.fori_loop(0, LAYERS, first_copies, 0)

    @pl.when(jnp.logical_not(has_prev))
    def _():
        top[...] = jnp.zeros_like(top)

    @pl.when(jnp.logical_not(has_next))
    def _():
        bottom[...] = jnp.zeros_like(bottom)

    edge_in[...] = jnp.zeros_like(edge_in)
    opp_dev = (6 + 2 * xb - me.dp, me.chan) if line else None
    greet(chan_devs + [me.dp_device(bit) for bit, _, _ in levels] + ([opp_dev] if line else []))

    def small_copy(k):
        return remote(local_small, small.at[me.chan], small_send.at[k], small_recv.at[k], chan_devs[k])

    def fold_copy(k):
        return remote(fold.at[me.chan], fold.at[me.chan], fold_send.at[k], fold_recv.at[k], chan_devs[k])

    issue(0)
    for k in range(3):
        small_copy(k).start()
    small[me.chan] = local_small[...]

    rows8 = lax.broadcasted_iota(jnp.int32, (CH, BLOCK), 0)
    mixed = jnp.zeros((CH, BLOCK), F32)
    for j in range(CH):
        mixed = mixed + inv_weight[:, j : j + 1] * audio[j : j + 1, :]
    first_ext = jnp.where(rows8 < HALF, mixed, jnp.where(rows8 == HALF, 1.0, 0.0))
    keep[0] = mixed
    keep[1] = first_ext
    for r in range(BLOCK // HOP):
        row = jnp.broadcast_to(mel[r : r + 1, :], (HOP, ROWS)).astype(BF16)
        for slot in range(2):
            ext[slot, pl.ds(r * HOP, HOP), CONV:] = row
    out[...] = jnp.zeros_like(out)
    for k in range(3):
        small_copy(k).wait_recv()

    def small_row(lo, hi):
        return jnp.concatenate([small[s, lo:hi, :] for s in range(SHARDS)], axis=1)

    start_ext = jnp.where(rows8 <= HALF, small_row(0, 8), 0.0)
    keep[2] = start_ext
    hid[pl.ds(PAD, BLOCK), :] = lax.dot_general(
        first_ext, start_ext, (((0,), (0,)), ((), ())), precision=HIGH, preferred_element_type=F32
    )
    final = small_row(16, 24)
    final_high, final_low = split(final)
    final_rows = jnp.concatenate([final_high, final_low], axis=0).astype(BF16)
    for l in range(LAYERS):
        both = dot(final_rows, skip_weight[l])
        high, rest_of = split(both[:CH] + both[CH:])
        fold[me.chan, l] = jnp.concatenate([high, rest_of, high, jnp.zeros_like(high)], axis=0).astype(BF16)
    for k in range(3):
        fold_copy(k).start()
    skip_bias = small_row(13, 14)
    const = jnp.sum(final * skip_bias, axis=1, keepdims=True) + end_bias[...]

    aug = jnp.concatenate(
        [
            inv_weight[...],
            jnp.where(
                lax.broadcasted_iota(jnp.int32, (CH, CH), 0) == lax.broadcasted_iota(jnp.int32, (CH, CH), 1), 1.0, 0.0
            ),
        ],
        axis=1,
    )
    aug_rows = lax.broadcasted_iota(jnp.int32, (CH, 2 * CH), 0)
    log_total = jnp.zeros((1, 1), F32)
    for c in range(CH):
        pivot = aug[c : c + 1, c : c + 1]
        log_total = log_total + jnp.log(pivot)
        pivot_row = aug[c : c + 1, :] / pivot
        aug = jnp.where(aug_rows == c, pivot_row, aug - aug[:, c : c + 1] * pivot_row)
    inverse_out[...] = aug
    log_out[...] = jnp.broadcast_to(log_total, log_out.shape)

    def ext_copy(l):
        return pltpu.make_async_copy(ext.at[l % 2], ext_out.at[l], ext_sem.at[l % 2])

    def acts_copy(l):
        return pltpu.make_async_copy(acts.at[l % 2], acts_out.at[l], acts_sem.at[l % 2])

    def keep_copy(l):
        return pltpu.make_async_copy(
            shared.at[pl.ds(l * SHARDS, SHARDS)], weights_out.at[l], keep_sem.at[l]
        )

    def to_next(l, rows):
        p = l % 2
        return remote(
            ext.at[p, pl.ds(BLOCK - rows, rows), pl.ds(WIDTH, WIDTH)],
            top.at[p, pl.ds(EDGE - rows, rows)],
            top_send.at[p], top_recv.at[p], next_dev,
        )

    def to_prev(l, rows):
        p = l % 2
        return remote(
            ext.at[p, pl.ds(0, rows), pl.ds(WIDTH, WIDTH)],
            bottom.at[p, pl.ds(0, rows)],
            bottom_send.at[p], bottom_recv.at[p], prev_dev,
        )

    def by_edge(l, f):
        pl.when(l <= 4)(lambda: f(PAD))
        pl.when(l > 4)(lambda: f(EDGE))

    def forward(l, carry):
        p = l % 2
        pl.when(l + 1 < LAYERS)(lambda: relay_a(l + 1))
        relay_c(l)
        arrive(l)
        keep_copy(l).start()

        @pl.when(l >= 2)
        def _():
            ext_copy(l - 2).wait()
            acts_copy(l - 2).wait()

        ext[p, :, WIDTH : 2 * WIDTH] = hid[pl.ds(PAD, BLOCK), :].astype(BF16)

        def start(rows):
            pl.when(has_next)(lambda: to_next(l, rows).start())
            pl.when(has_prev)(lambda: to_prev(l, rows).start())

        def finish(rows):
            @pl.when(has_next)
            def _():
                to_next(l, rows).wait_send()
                to_prev(l, rows).wait_recv()

            @pl.when(has_prev)
            def _():
                to_prev(l, rows).wait_send()
                to_next(l, rows).wait_recv()

        by_edge(l, start)
        by_edge(l, finish)
        hid[pl.ds(0, PAD), :] = top[p, pl.ds(EDGE - PAD, PAD), :].astype(F32)
        hid[pl.ds(PAD + BLOCK, PAD), :] = bottom[p, pl.ds(0, PAD), :].astype(F32)
        for layer in range(LAYERS):
            d = 2**layer

            @pl.when(l == layer)
            def _():
                if d < PAD:
                    ext[p, :, :WIDTH] = hid[pl.ds(PAD - d, BLOCK), :].astype(BF16)
                    ext[p, :, 2 * WIDTH : CONV] = hid[pl.ds(PAD + d, BLOCK), :].astype(BF16)
                else:
                    ext[p, :d, :WIDTH] = top[p, EDGE - d :, :]
                    ext[p, d:, :WIDTH] = ext[p, : BLOCK - d, WIDTH : 2 * WIDTH]
                    ext[p, BLOCK - d :, 2 * WIDTH : CONV] = bottom[p, :d, :]
                    ext[p, : BLOCK - d, 2 * WIDTH : CONV] = ext[p, d:, WIDTH : 2 * WIDTH]

        ext_copy(l).start()

        def one(s, carry):
            pre = dot_nt(ext[p], shared[l * SHARDS + s, :, :EXT])
            t = jnp.tanh(pre[:, :ROWS])
            g = 0.5 * jnp.tanh(0.5 * pre[:, ROWS:]) + 0.5
            tg = t * g
            acts[p, s, 0] = tg.astype(BF16)
            acts[p, s, 1] = (g - t * tg).astype(BF16)
            acts[p, s, 2] = (tg * (1.0 - g)).astype(BF16)
            pl.when((s == 1) & (l + 1 < LAYERS))(lambda: relay_b(l + 1))
            return carry

        lax.fori_loop(0, SHARDS, one, 0)
        acts_copy(l).start()

        @pl.when(l == 0)
        def _():
            for k in range(3):
                fold_copy(k).wait_recv()

        gated = jnp.concatenate([acts[p, s, 0] for s in range(SHARDS)], axis=1)
        out[...] += dot_nt(jnp.concatenate([fold[s, l, : 2 * CH, :] for s in range(SHARDS)], axis=1), gated)

        @pl.when(l < LAYERS - 1)
        def _():
            for h in range(2):
                res = jnp.concatenate(
                    [shared[l * SHARDS + s, :, EXT + h * ROWS : EXT + (h + 1) * ROWS] for s in range(SHARDS)], axis=1
                )
                bias = jnp.concatenate([small[s, pl.ds(5 + l, 1), :] for s in (2 * h, 2 * h + 1)], axis=1)
                cols = slice(h * 2 * ROWS, (h + 1) * 2 * ROWS)
                hid[pl.ds(PAD, BLOCK), cols] += dot_nt(gated, res) + bias

        return carry

    relay_a(0)
    relay_b(0)
    lax.fori_loop(0, LAYERS, forward, 0)

    both = out[...]
    output = both[:CH] + both[CH:] + const
    log_scale, shift = output[:HALF], output[HALF:]
    scale = jnp.exp(log_scale)
    mixed = keep[0]
    second = mixed[HALF:]
    second_out = scale * second + shift
    mine = pl.ds(pl.multiple_of(me.chan * BLOCK, BLOCK), BLOCK)
    frames_out[0:CH, mine] = jnp.concatenate([mixed[:HALF], second_out], axis=0)
    frames_out[2 * CH : 3 * CH, mine] = jnp.concatenate([log_scale, jnp.zeros_like(log_scale)], axis=0)
    out_grad = jnp.concatenate([second_out * scale * second - 1.0, second_out], axis=0)
    keep[3] = jnp.concatenate([jnp.zeros_like(scale), second_out * scale], axis=0)
    og_high, og_low = split(out_grad)
    og_rows[...] = jnp.concatenate([og_high, og_low], axis=0).astype(BF16)
    og_stack = jnp.concatenate([og_high, og_high, og_low, jnp.zeros((ROWS - 3 * CH, BLOCK), F32)], axis=0)
    low[:, WIDTH:] = og_stack.T.astype(BF16)
    end_sum = jnp.sum(out_grad, axis=1, keepdims=True)
    grad[...] = jnp.zeros_like(grad)
    mel_sum[...] = jnp.zeros_like(mel_sum)

    def drain_forward(l, carry):
        far_a(l, me.chan).wait_send()
        far_b(l, me.chan).wait_send()
        x_a(l, xb).wait_send()
        z_a(l, zb).wait_send()
        x_b(l, xb).wait_send()
        core_a(l, me.chan).wait_send()
        core_b(l, me.far_shard).wait_send()
        keep_copy(l).wait()
        return carry

    lax.fori_loop(0, LAYERS, drain_forward, 0)
    for l in (LAYERS - 2, LAYERS - 1):
        ext_copy(l).wait()
        acts_copy(l).wait()
    for k in range(3):
        small_copy(k).wait_send()
        fold_copy(k).wait_send()
    pl.semaphore_signal(phase.at[0], inc=1, device_id=core_dev, device_id_type=MESH)
    pl.semaphore_signal(phase.at[1], inc=1, device_id=far_dev, device_id_type=MESH)

    def shard_of(j):
        core = jnp.where(j < 2, 1 - me.core, me.core)
        return (j % 2) * 2 + core

    def w_copy(q):
        l, s = LAYERS - 1 - q // SHARDS, shard_of(q % SHARDS)
        return pltpu.make_async_copy(weights_out.at[l, s], wbuf.at[q % 2], w_sem.at[q % 2])

    def ext_back(l):
        return pltpu.make_async_copy(ext_out.at[l], ext.at[l % 2], ext_sem.at[l % 2])

    def acts_back(l):
        return pltpu.make_async_copy(acts_out.at[l], acts.at[l % 2], acts_sem.at[l % 2])

    def kept(i, ys):
        return 4 + 2 * i + ys

    def got_core(i, ys):
        return 20 + 2 * (i % 2) + ys

    def to_core(i, ys):
        p = i % 2
        return remote(
            shared.at[2 * p + ys], shared.at[got_core(i, ys)], core_send.at[p, ys], core_recv.at[p, ys], core_dev
        )

    def to_far(i):
        return remote(shared.at[kept(i, 1 - me.side)], shared.at[24 + i], far_send.at[i], far_recv.at[i], far_dev)

    def add_rows(block, base, rows, src, src_at):
        chunk = min(rows, 32)

        def body(k, carry):
            at = pl.ds(pl.multiple_of(base + k * chunk, PAD), chunk)
            shared[block, at, :] = shared[block, at, :] + src[src_at, pl.ds(pl.multiple_of(k * chunk, PAD), chunk), :]
            return carry

        lax.fori_loop(0, rows // chunk, body, 0)

    base_at = [0]
    for bit, rows, after in levels:
        base_at.append(base_at[-1] + (me.dp_bit(bit) * after if after < rows else 0))

    def rs(k, i):
        bit, rows, after = levels[k]
        first = base_at[k] + ((1 - me.dp_bit(bit)) * after if after < rows else 0)
        at = pl.ds(pl.multiple_of(first, PAD), after)
        return remote(
            shared.at[kept(i, me.side), at], level_bufs[k].at[i], rs_send.at[k, i], rs_recv.at[k, i], me.dp_device(bit)
        )

    def ag(k, i, arriving):
        bit, rows, after = levels[k]
        first = base_at[k] + (1 - me.dp_bit(bit)) * after if arriving else base_at[k + 1]
        ref = total.at[LAYERS - 1 - i, pl.ds(pl.multiple_of(first, PAD), after)]
        return remote(ref, ref, ag_send.at[k, i], ag_recv.at[k, i], me.dp_device(bit))

    halving = [k for k, (bit, rows, after) in enumerate(levels) if after < rows]

    def out_copy(i):
        at = pl.ds(pl.multiple_of(base_at[-1], PAD), levels[-1][2])
        return pltpu.make_async_copy(shared.at[kept(i, me.side), at], total.at[LAYERS - 1 - i, at], out_sem.at[0, i])

    def stage_core(i):
        for ys in (1 - me.side, me.side):
            to_core(i, ys).wait_recv()
            add_rows(kept(i, ys), 0, 2 * ROWS, shared, got_core(i, ys))
            pl.semaphore_signal(credit.at[ys], inc=1, device_id=core_dev, device_id_type=MESH)
            if ys is not me.side:
                pl.when(i == 0)(lambda: pl.semaphore_wait(phase.at[1], 1))
                if not line:
                    to_far(i).start()
        if line:
            start_ways(i)

    def stage_far(i):
        to_far(i).wait_recv()
        add_rows(kept(i, me.side), 0, 2 * ROWS, shared, 24 + i)
        rs(0, i).start()

    def stage_rs(k, i):
        bit, rows, after = levels[k]
        rs(k, i).wait_recv()
        if after == rows:
            rs(k, i).wait_send()
        add_rows(kept(i, me.side), base_at[k + 1], after, level_bufs[k], i)
        if k + 1 < len(levels):
            rs(k + 1, i).start()
        else:
            out_copy(i).start()
            out_copy(i).wait()
            ag(halving[-1], i, False).start()

    def stage_ag(n, i):
        ag(halving[n], i, True).wait_recv()
        if n > 0:
            ag(halving[n - 1], i, False).start()

    def add_block(block, base, rows, cols, src, src_base=0):
        chunk = min(rows, 64)

        def body(k, carry):
            at = pl.ds(pl.multiple_of(base + k * chunk, 64), chunk)
            got = src[pl.ds(pl.multiple_of(src_base + k * chunk, 64), chunk), :]
            shared[block, at, cols] = shared[block, at, cols] + got
            return carry

        lax.fori_loop(0, rows // chunk, body, 0)

    def rows_at(first, rows):
        return pl.ds(pl.multiple_of(first, 64), rows)

    if line:
        zc = me.dp // 2
        inner = (zc == 1) | (zc == 2)
        edge = jnp.logical_not(inner)
        hb = jnp.where(zc == 2, 1, 0)
        lane_devs = [x_dev, z_dev, opp_dev, z_dev, opp_dev, x_dev]
        lanes = [
            Lane(level_bufs[k], lane_send.at[k], lane_recv.at[k], lane_credit.at[k], lane_devs[k]) for k in range(6)
        ]
        qx, q1, q2, r1, r2, rx = lanes
        half = ROWS
        mine_x, mine_x2 = xb * half, xb * half + hb * (half // 2)
        r_base, r_base2 = hb * half, hb * half + xb * (half // 2)

        def far_way(k, i, rows, cols):
            return remote(
                shared.at[kept(i, 1 - me.side), rows, cols], shared.at[24 + i, rows, cols],
                way_send.at[k, i], way_recv.at[k, i], far_dev,
            )

        def far_q(i):
            return far_way(0, i, rows_at(mine_x, half), ACROSS)

        def far_r(i):
            return far_way(1, i, pl.ds(0, 2 * ROWS), ALONG)

        def total_way(k, i, rows, cols, device, src=None):
            ref = total.at[LAYERS - 1 - i, rows, cols]
            return remote(ref if src is None else src, ref, way_send.at[k, i], way_recv.at[k, i], device)

        def own_part(k, i, rows, cols):
            return pltpu.make_async_copy(
                shared.at[kept(i, me.side), rows, cols], total.at[LAYERS - 1 - i, rows, cols], out_sem.at[k, i]
            )

        def q_inner(i, b):
            rows = rows_at(mine_x + b * (half // 2), half // 2)
            return total_way(2, i, rows, ACROSS, opp_dev, shared.at[kept(i, me.side), rows, ACROSS])

        def q_edge(i):
            return total_way(3, i, rows_at(mine_x, half), ACROSS, z_dev)

        def q_x(i, x):
            return total_way(4, i, rows_at(x * half, half), ACROSS, x_dev)

        def r_x(i, x):
            rows = rows_at(r_base + x * (half // 2), half // 2)
            return total_way(5, i, rows, ALONG, x_dev, shared.at[kept(i, me.side), rows, ALONG])

        def r_inner(i, b):
            return total_way(6, i, rows_at(b * half, half), ALONG, opp_dev)

        def r_edge(i):
            return total_way(7, i, pl.ds(0, 2 * ROWS), ALONG, z_dev)

        def q_out(i):
            return own_part(0, i, rows_at(mine_x2, half // 2), ACROSS)

        def r_out(i):
            return own_part(1, i, rows_at(r_base2, half // 2), ALONG)

        def own_ref(i, first, rows, cols):
            return shared.at[kept(i, me.side), rows_at(first, rows), cols]

        def start_ways(i):
            far_r(i).start()
            qx.start(i, shared.at[pl.ds(kept(i, 0), 2), rows_at((1 - xb) * half, half), ACROSS])

        def q_stage1(i):
            qx.wait(i)
            for ys in (1 - me.side, me.side):
                add_block(kept(i, ys), mine_x, half, ACROSS, qx.buf.at[i % DEPTH, ys])
                if ys is not me.side:
                    far_q(i).start()
            qx.free()

        def r_stage1(i):
            far_r(i).wait_recv()
            add_block(kept(i, me.side), 0, 2 * ROWS, ALONG, shared.at[24 + i, :, ALONG])
            pl.when(edge)(lambda: r1.start(i, own_ref(i, 0, 2 * ROWS, ALONG)))

        def q_stage2(i):
            far_q(i).wait_recv()
            add_block(kept(i, me.side), mine_x, half, ACROSS, shared.at[24 + i, :, ACROSS], mine_x)
            pl.when(edge)(lambda: q1.start(i, own_ref(i, mine_x, half, ACROSS)))

        def r_stage2(i):
            @pl.when(inner)
            def _():
                r1.wait(i)
                add_block(kept(i, me.side), 0, 2 * ROWS, ALONG, r1.buf.at[i % DEPTH])
                r1.free()
                r2.start(i, own_ref(i, (1 - hb) * half, half, ALONG))

        def q_stage3(i):
            @pl.when(inner)
            def _():
                q1.wait(i)
                add_block(kept(i, me.side), mine_x, half, ACROSS, q1.buf.at[i % DEPTH])
                q1.free()
                q2.start(i, own_ref(i, mine_x + (1 - hb) * (half // 2), half // 2, ACROSS))

        def r_stage3(i):
            @pl.when(inner)
            def _():
                r2.wait(i)
                add_block(kept(i, me.side), r_base, half, ALONG, r2.buf.at[i % DEPTH])
                r2.free()
                rx.start(i, own_ref(i, r_base + (1 - xb) * (half // 2), half // 2, ALONG))

        def q_stage4(i):
            @pl.when(inner)
            def _():
                q2.wait(i)
                add_block(kept(i, me.side), mine_x2, half // 2, ACROSS, q2.buf.at[i % DEPTH])
                q2.free()
                q_inner(i, hb).start()
                q_out(i).start()

        def r_stage4(i):
            @pl.when(inner)
            def _():
                rx.wait(i)
                add_block(kept(i, me.side), r_base2, half // 2, ALONG, rx.buf.at[i % DEPTH])
                rx.free()
                r_x(i, xb).start()
                r_out(i).start()

        def q_stage5(i):
            @pl.when(inner)
            def _():
                q_out(i).wait()
                q_inner(i, 1 - hb).wait_recv()
                q_edge(i).start()
                q_x(i, xb).start()

        def r_stage5(i):
            @pl.when(inner)
            def _():
                r_out(i).wait()
                r_x(i, 1 - xb).wait_recv()
                r_inner(i, hb).start()

        def q_stage6(i):
            @pl.when(edge)
            def _():
                q_edge(i).wait_recv()
                q_x(i, xb).start()

        def r_stage6(i):
            @pl.when(inner)
            def _():
                r_inner(i, 1 - hb).wait_recv()
                r_edge(i).start()

        def q_stage7(i):
            q_x(i, 1 - xb).wait_recv()

        def r_stage7(i):
            pl.when(edge)(lambda: r_edge(i).wait_recv())

        def drain_ways(i, carry):
            far_q(i).wait_send()
            far_r(i).wait_send()
            q_x(i, xb).wait_send()

            @pl.when(inner)
            def _():
                q_inner(i, hb).wait_send()
                q_edge(i).wait_send()
                r_x(i, xb).wait_send()
                r_inner(i, hb).wait_send()
                r_edge(i).wait_send()

            return carry

        def finish_lanes():
            qx.finish()

            @pl.when(edge)
            def _():
                q1.finish()
                r1.finish()

            @pl.when(inner)
            def _():
                q2.finish()
                r2.finish()
                rx.finish()

        line_stages = [
            [q_stage1, r_stage1], [q_stage2, r_stage2], [q_stage3, r_stage3], [q_stage4, r_stage4],
            [q_stage5, r_stage5], [q_stage6, r_stage6], [q_stage7, r_stage7],
        ]

    def back_prev(i, rows):
        return remote(
            edge_out.at[0, pl.ds(0, rows)], edge_in.at[i % 2, 0, pl.ds(0, rows)],
            edge_send.at[0], edge_recv.at[i % 2, 0], prev_dev,
        )

    def back_next(i, rows):
        return remote(
            edge_out.at[1, pl.ds(EDGE - rows, rows)], edge_in.at[i % 2, 1, pl.ds(EDGE - rows, rows)],
            edge_send.at[1], edge_recv.at[i % 2, 1], next_dev,
        )

    def backward(i):
        l = LAYERS - 1 - i
        p = l % 2
        now = grad[...].astype(BF16)
        low[:, :WIDTH] = now
        low_t[...] = now.T
        sums_out[pl.ds(72 + l, 1), :] = jnp.sum(now.astype(F32), axis=0, keepdims=True)
        tap0[pl.ds(0, BLOCK), :] = jnp.zeros((BLOCK, WIDTH), F32)
        tap2[pl.ds(EDGE, BLOCK), :] = jnp.zeros((BLOCK, WIDTH), F32)

        @pl.when(i >= 2)
        def _():
            ext_back(l).wait()
            acts_back(l).wait()

        def one(j, carry):
            q = i * SHARDS + j
            b = q % 2
            s = shard_of(j)
            pl.when(q + 1 < LAYERS * SHARDS)(lambda: w_copy(q + 1).start())

            @pl.when((j < 2) & (i >= 2))
            def _():
                to_core(i - 2, j).wait_send()

            w_copy(q).wait()
            slot = jnp.where(j < 2, 2 * (i % 2) + j, kept(i, j - 2))
            gated = acts[p, s, 0]
            res = jnp.concatenate([wbuf[b, :, EXT : EXT + ROWS], wbuf[b, :, EXT + ROWS :]], axis=0)
            back = dot(low[:, :WIDTH], res) + dot(low[:, WIDTH : WIDTH + 4 * CH], fold[s, l])
            pg = jnp.concatenate(
                [(back * acts[p, s, 1].astype(F32)).astype(BF16), (back * acts[p, s, 2].astype(F32)).astype(BF16)],
                axis=1,
            )
            tap0[pl.ds(0, BLOCK), :] += dot(pg, wbuf[b, :, :WIDTH])
            grad[...] += dot(pg, wbuf[b, :, WIDTH : 2 * WIDTH])
            tap2[pl.ds(EDGE, BLOCK), :] += dot(pg, wbuf[b, :, 2 * WIDTH : CONV])
            mel_sum[...] += dot(pg, wbuf[b, :, CONV:EXT])
            for k in range(3):
                cols = slice(k * WIDTH, (k + 1) * WIDTH)
                shared[slot, :, cols] = dot_tn(pg, ext[p, :, cols]).astype(BF16)
            shared[slot, :, CONV:EXT] = dot_tn(pg, ext[p, :, CONV:]).astype(BF16)
            side = dot(low_t[...], gated).astype(BF16)
            shared[slot, :, EXT : EXT + ROWS] = side[: 2 * ROWS]
            shared[slot, :, EXT + ROWS :] = side[2 * ROWS :]
            e = dot(og_rows[...], gated)
            sums_out[pl.ds(pl.multiple_of(l * CH, CH), CH), pl.ds(pl.multiple_of(s * ROWS, ROWS), ROWS)] = e[:CH] + e[CH:]

            @pl.when(j < 2)
            def _():
                pl.when(q == 0)(lambda: pl.semaphore_wait(phase.at[0], 1))
                pl.when(i >= 2)(lambda: pl.semaphore_wait(credit.at[j], 1))
                to_core(i, j).start()

            return carry

        lax.fori_loop(0, SHARDS, one, 0)

        @pl.when(l >= 2)
        def _():
            ext_back(l - 2).start()
            acts_back(l - 2).start()

        edge_out[0] = tap0[pl.ds(0, EDGE), :].astype(BF16)
        edge_out[1] = tap2[pl.ds(BLOCK, EDGE), :].astype(BF16)

        def start(rows):
            pl.when(has_next)(lambda: back_next(i, rows).start())
            pl.when(has_prev)(lambda: back_prev(i, rows).start())

        def finish(rows):
            @pl.when(has_next)
            def _():
                back_next(i, rows).wait_send()
                back_prev(i, rows).wait_recv()

            @pl.when(has_prev)
            def _():
                back_prev(i, rows).wait_send()
                back_next(i, rows).wait_recv()

        by_edge(l, start)
        by_edge(l, finish)
        tap0[pl.ds(BLOCK, EDGE), :] = edge_in[i % 2, 0].astype(F32)
        tap2[pl.ds(0, EDGE), :] = edge_in[i % 2, 1].astype(F32)
        for layer in range(LAYERS):
            d = 2**layer

            @pl.when(l == layer)
            def _():
                grad[...] += tap0[pl.ds(d, BLOCK), :] + tap2[pl.ds(EDGE - d, BLOCK), :]

    sum_devs = [core_dev, far_dev] + [me.dp_device(bit) for bit, _, _ in levels]

    def sum_copy(k):
        return remote(sums_out, small_in.at[k], sum_send.at[k], sum_recv.at[k], sum_devs[k])

    def end_copy(k):
        return remote(end_out, end_in.at[k], end_send.at[k], end_recv.at[k], sum_devs[k])

    def frames_copy(k):
        ref = frames_out.at[:, mine]
        return remote(ref, ref, frames_send.at[k], frames_recv.at[k], chan_devs[k])

    mel_rows = BLOCK // HOP

    def mel_copy(k):
        ref = mel_out.at[pl.ds(pl.multiple_of(me.chan * mel_rows, mel_rows), mel_rows)]
        return remote(ref, ref, mel_send.at[k], mel_recv.at[k], chan_devs[k])

    def last(values, other, dims):
        return lax.dot_general(values, other, (dims, ((), ())), precision=HIGH, preferred_element_type=F32)

    def finish_frames():
        hidden_grad = grad[...]
        sums_out[64:72, :] = last(keep[1], hidden_grad, ((1,), (0,)))
        mixed = keep[0]
        first_back = last(keep[2], hidden_grad, ((1,), (1,)))
        rows = lax.broadcasted_iota(jnp.int32, (CH, BLOCK), 0)
        mixed_grad = jnp.where(rows < HALF, mixed + first_back, keep[3])
        frames_out[CH : 2 * CH, mine] = last(inv_weight[...], mixed_grad, ((0,), (0,)))
        inv_part = last(mixed_grad, audio[...], ((1,), (1,)))
        sums_out[80:88, :] = jnp.concatenate([inv_part, end_sum, jnp.zeros((CH, WIDTH - CH - 1), F32)], axis=1)
        mel_out[pl.ds(pl.multiple_of(me.chan * mel_rows, mel_rows), mel_rows), :] = jnp.sum(
            mel_sum[...].reshape(mel_rows, HOP, ROWS), axis=1
        )
        for k in range(3):
            frames_copy(k).start()
            mel_copy(k).start()
        sum_copy(0).start()

    def sum_stage(k):
        sum_copy(k).wait_recv()
        sum_copy(k).wait_send()
        sums_out[...] = sums_out[...] + small_in[k]
        if k + 1 < len(sum_devs):
            sum_copy(k + 1).start()
            return
        e = sums_out[0:64, pl.ds(pl.multiple_of(me.chan * ROWS, ROWS), ROWS)]
        e_high, e_low = split(e)
        end = jnp.zeros((2 * CH, WIDTH), F32)
        for l in range(LAYERS):
            part = slice(l * CH, (l + 1) * CH)
            end = end + dot_nt(jnp.concatenate([e_high[part], e_low[part]], axis=0).astype(BF16), skip_weight[l])
        end_out[...] = end[:CH] + end[CH:]
        end_copy(0).start()

    def end_stage(k):
        end_copy(k).wait_recv()
        end_copy(k).wait_send()
        end_out[...] = end_out[...] + end_in[k]
        if k == 0:
            end_copy(1).start()

    small_stages = [finish_frames]
    small_stages += [functools.partial(sum_stage, k) for k in range(len(sum_devs))]
    small_stages += [functools.partial(end_stage, k) for k in range(2)]

    if line:
        stages = [[stage_core]] + line_stages
    else:
        stages = [[stage_core], [stage_far]]
        stages += [[functools.partial(stage_rs, k)] for k in range(len(levels))]
        stages += [[functools.partial(stage_ag, n)] for n in range(len(halving) - 1, -1, -1)]
    steps = LAYERS - 1 + max(len(stages), len(small_stages))

    w_copy(0).start()

    def step(i, carry):
        @pl.when(i < LAYERS)
        def _():
            backward(i)
            stage_core(i)

        for k, stage in enumerate(small_stages):
            pl.when(i == LAYERS - 1 + k)(stage)
        for lag in range(len(stages) - 1, 0, -1):

            @pl.when((i >= lag) & (i < LAYERS + lag))
            def _():
                for stage in stages[lag]:
                    stage(i - lag)

        return carry

    lax.fori_loop(0, steps, step, 0)

    for i in (LAYERS - 2, LAYERS - 1):
        for ys in range(2):
            to_core(i, ys).wait_send()
            pl.semaphore_wait(credit.at[ys], 1)

    def drain(i, carry):
        to_far(i).wait_send()
        for k, (bit, rows, after) in enumerate(levels):
            if after < rows:
                rs(k, i).wait_send()
                ag(k, i, False).wait_send()
        return carry

    if line:
        lax.fori_loop(0, LAYERS, drain_ways, 0)
        finish_lanes()
    else:
        lax.fori_loop(0, LAYERS, drain, 0)
    for k, shard in enumerate([me.core_shard, me.far_shard, me.diag_shard]):
        frames_copy(k).wait_send()
        mel_copy(k).wait_send()
        frames_copy(k).wait_recv()
        mel_copy(k).wait_recv()
    own_lanes = pl.ds(pl.multiple_of(me.chan * ROWS, ROWS), ROWS)
    mine_out[...] = sums_out[:, own_lanes]
    end_own_out[...] = end_out[:, own_lanes]


def run_flow(dp_size, *args):
    levels = levels_of(dp_size)
    vmem = pl.BlockSpec(memory_space=pltpu.VMEM)
    hbm = pl.BlockSpec(memory_space=pl.ANY)
    dma = pltpu.SemaphoreType.DMA
    regular = pltpu.SemaphoreType.REGULAR
    block = (2 * ROWS, PACK)
    n = len(levels)
    return pl.pallas_call(
        functools.partial(flow_kernel, levels),
        out_shape=(
            jax.ShapeDtypeStruct((LAYERS,) + block, BF16),
            jax.ShapeDtypeStruct((LAYERS, SHARDS) + block, BF16),
            jax.ShapeDtypeStruct((LAYERS, BLOCK, EXT), BF16),
            jax.ShapeDtypeStruct((LAYERS, SHARDS, 3, BLOCK, ROWS), BF16),
            jax.ShapeDtypeStruct((3 * CH, FRAMES), F32),
            jax.ShapeDtypeStruct((FRAMES // HOP, ROWS), F32),
            jax.ShapeDtypeStruct((88, WIDTH), F32),
            jax.ShapeDtypeStruct((CH, 2 * CH), F32),
            jax.ShapeDtypeStruct((CH, ROWS), F32),
            jax.ShapeDtypeStruct((SHARDS, 24, ROWS), F32),
            jax.ShapeDtypeStruct((CH, WIDTH), F32),
            jax.ShapeDtypeStruct((88, ROWS), F32),
            jax.ShapeDtypeStruct((CH, ROWS), F32),
        ),
        in_specs=[hbm] * 3 + [vmem] * 6,
        out_specs=tuple([hbm] * 4 + [vmem] * 9),
        scratch_shapes=[
            pltpu.VMEM((LAYERS * SHARDS,) + block, BF16),
            pltpu.VMEM((PAD + BLOCK + PAD, WIDTH), F32),
            pltpu.VMEM((2, BLOCK, EXT), BF16),
            pltpu.VMEM((2, SHARDS, 3, BLOCK, ROWS), BF16),
            pltpu.VMEM((2, EDGE, WIDTH), BF16),
            pltpu.VMEM((2, EDGE, WIDTH), BF16),
            pltpu.VMEM((2,) + block, BF16),
            pltpu.VMEM((BLOCK, WIDTH + ROWS), BF16),
            pltpu.VMEM((WIDTH, BLOCK), BF16),
            pltpu.VMEM((BLOCK + EDGE, WIDTH), F32),
            pltpu.VMEM((EDGE + BLOCK, WIDTH), F32),
            pltpu.VMEM((BLOCK, WIDTH), F32),
            pltpu.VMEM((BLOCK, ROWS), F32),
            pltpu.VMEM((2, EDGE, WIDTH), BF16),
            pltpu.VMEM((2, 2, EDGE, WIDTH), BF16),
            pltpu.VMEM((SHARDS, LAYERS, 4 * CH, ROWS), BF16),
            pltpu.VMEM((4, CH, BLOCK), F32),
            pltpu.VMEM((2 * CH, BLOCK), BF16),
            pltpu.VMEM((2 * CH, BLOCK), F32),
            pltpu.VMEM((n + 2, 88, WIDTH), F32),
            pltpu.VMEM((2, CH, WIDTH), F32),
        ]
        + (
            [pltpu.VMEM((DEPTH,) + shape, BF16) for shape in line_shapes()]
            if mesh_line(levels)
            else [pltpu.VMEM((LAYERS, after, PACK), BF16) for _, _, after in levels]
        )
        + [
            dma((4, LAYERS)), dma((7, LAYERS)), dma((7, LAYERS)), dma((LAYERS,)), dma((2,)), dma((2,)),
            dma((2,)), dma((2,)), dma((2,)), dma((2,)),
            dma((3,)), dma((3,)), dma((3,)), dma((3,)),
            regular((2,)), dma((2,)), dma((2, 2)), dma((2, 2)), regular((2,)), dma((LAYERS,)), dma((LAYERS,)),
            dma((n, LAYERS)), dma((n, LAYERS)), dma((n, LAYERS)), dma((n, LAYERS)), dma((2, LAYERS)),
            dma((2,)), dma((2, 2)),
            dma((n + 2,)), dma((n + 2,)), dma((2,)), dma((2,)), dma((3,)), dma((3,)), dma((3,)), dma((3,)),
            dma((6, DEPTH)), dma((6, DEPTH)), regular((6,)), dma((8, LAYERS)), dma((8, LAYERS)),
        ],
        compiler_params=pltpu.CompilerParams(
            collective_id=0, has_side_effects=True, vmem_limit_bytes=VMEM_LIMIT
        ),
    )(*args)


def prepare_kernel(
    offset, clip, mel_frames, cond_weight, in_bias, start_weight, start_bias, res_bias, skip_bias, final, end_bias,
    audio, mel, cond_ext, local_small, end_column,
):
    chan = lax.axis_index("chan")
    first = offset[0] * HOP + chan * BLOCK
    length = clip.shape[2]
    audio[...] = pltpu.roll(clip[0], lax.rem(length - first, length), 1)[:, :BLOCK]
    mel_rows = BLOCK // HOP
    clip_rows = mel_frames.shape[1]
    frames = jnp.concatenate([mel_frames[0].astype(F32), jnp.ones((clip_rows, ROWS - MEL), F32)], axis=1)
    frames = pltpu.roll(frames, lax.rem(clip_rows - offset[0] - chan * mel_rows, clip_rows), 0)[:mel_rows]
    lane = lax.broadcasted_iota(jnp.int32, (mel_rows, ROWS), 1)
    mel[...] = jnp.where(lane < MEL + 2, frames, 0.0)
    for l in range(LAYERS):
        high, rest = split(in_bias[l])
        for g in range(2):
            part = jnp.concatenate(
                [
                    cond_weight[l, g].astype(F32),
                    high[g : g + 1],
                    rest[g : g + 1],
                    jnp.zeros((ROWS - MEL - 2, ROWS), F32),
                ],
                axis=0,
            )
            cond_ext[l, g * ROWS : (g + 1) * ROWS, :] = part.T.astype(BF16)
    local_small[...] = jnp.concatenate(
        [
            start_weight[...],
            start_bias[...],
            res_bias[...],
            jnp.zeros((1, ROWS), F32),
            skip_bias[...],
            jnp.zeros((2, ROWS), F32),
            final[...],
        ],
        axis=0,
    )
    row = jnp.concatenate([end_bias[...], jnp.zeros((1, ROWS - CH), F32)], axis=1)
    end_column[...] = jnp.broadcast_to(row, (ROWS, ROWS)).T[:CH, :1]


def run_prepare(*args):
    vmem = pl.BlockSpec(memory_space=pltpu.VMEM)
    return pl.pallas_call(
        prepare_kernel,
        out_shape=(
            jax.ShapeDtypeStruct((CH, BLOCK), F32),
            jax.ShapeDtypeStruct((BLOCK // HOP, ROWS), F32),
            jax.ShapeDtypeStruct((LAYERS, 2 * ROWS, ROWS), BF16),
            jax.ShapeDtypeStruct((24, ROWS), F32),
            jax.ShapeDtypeStruct((CH, 1), F32),
        ),
        in_specs=[pl.BlockSpec(memory_space=pltpu.SMEM)] + [vmem] * 10,
        out_specs=tuple([vmem] * 5),
    )(*args)


def finish_kernel(
    crops, total, sums, mine, small, frames, mel_in, inverse, log_abs, end_in, final_own, skip_bias,
    latent, log_det, loss, audio_grad, mel_grad, inv_grad, start_grad, start_bias_grad, cond_grad, in_grad,
    bias_grad, res_grad, res_bias_grad, skip_grad, skip_bias_grad, end_grad, end_bias_grad,
):
    l = pl.program_id(0)
    for g in range(2):
        rows = slice(g * ROWS, (g + 1) * ROWS)
        in_grad[0, g] = total[0, rows, :CONV].astype(F32)
        cond = total[0, rows, CONV:EXT].astype(F32)
        cond = cond.T
        cond_grad[0, g] = cond[:MEL]
        bias_grad[0, g : g + 1, :] = cond[MEL : MEL + 1]

    @pl.when(l < LAYERS - 1)
    def _():
        res_grad[0, : 2 * ROWS] = total[0, :, EXT : EXT + ROWS].astype(F32)
        res_grad[0, 2 * ROWS :] = total[0, :, EXT + ROWS :].astype(F32)

    final = jnp.concatenate([small[s, 16:24, :] for s in range(SHARDS)], axis=1)
    skip_grad[0] = lax.dot_general(
        final, mine[pl.ds(pl.multiple_of(l * CH, CH), CH), :], (((0,), (0,)), ((), ())),
        precision=HIGH, preferred_element_type=F32,
    )

    @pl.when(l == 0)
    def _():
        z = frames[:CH]
        latent[0] = z
        audio_grad[0] = frames[CH : 2 * CH]
        mel_grad[0] = mel_in[:, :MEL]
        log_scale = frames[2 * CH : 2 * CH + HALF]
        det = jnp.sum(jnp.sum(log_scale, axis=1, keepdims=True), axis=0, keepdims=True) + FRAMES * log_abs[:1, :1]
        squares = jnp.sum(jnp.sum(z * z, axis=1, keepdims=True), axis=0, keepdims=True)
        log_det[...] = det
        loss[...] = (0.5 * squares - det) / (CH * FRAMES)
        tiny = sums[80:88, :ROWS]
        inv_grad[...] = tiny[:, :CH] - crops * FRAMES * inverse[:, CH:].T
        end_column = tiny[:, CH : CH + 1]
        end_bias_grad[...] = jnp.broadcast_to(end_column, (CH, ROWS)).T[:1, :]
        start_grad[...] = mine[64:68, :]
        start_bias_grad[...] = mine[68:69, :]
        res_bias_grad[...] = mine[72:79, :]
        skip_bias_grad[...] = jnp.sum(end_column * final_own[...], axis=0, keepdims=True)
        end_grad[...] = end_in[...] + end_column * skip_bias[...]


def run_finish(crops, total, *args):
    def whole(shape):
        return pl.BlockSpec(shape, lambda l: (0,) * len(shape))

    outs = [
        ((1, CH, FRAMES), None),
        ((1, 1), None),
        ((1, 1), None),
        ((1, CH, FRAMES), None),
        ((1, FRAMES // HOP, MEL), None),
        ((CH, CH), None),
        ((HALF, ROWS), None),
        ((1, ROWS), None),
        ((LAYERS, 2, MEL, ROWS), pl.BlockSpec((1, 2, MEL, ROWS), lambda l: (l, 0, 0, 0))),
        ((LAYERS, 2, ROWS, CONV), pl.BlockSpec((1, 2, ROWS, CONV), lambda l: (l, 0, 0, 0))),
        ((LAYERS, 2, ROWS), pl.BlockSpec((1, 2, ROWS), lambda l: (l, 0, 0))),
        (
            (LAYERS - 1, WIDTH, ROWS),
            pl.BlockSpec((1, WIDTH, ROWS), lambda l: (jnp.minimum(l, LAYERS - 2), 0, 0)),
        ),
        ((LAYERS - 1, ROWS), None),
        ((LAYERS, WIDTH, ROWS), pl.BlockSpec((1, WIDTH, ROWS), lambda l: (l, 0, 0))),
        ((1, ROWS), None),
        ((CH, ROWS), None),
        ((1, CH), None),
    ]
    return pl.pallas_call(
        functools.partial(finish_kernel, crops),
        grid=(LAYERS,),
        out_shape=tuple(jax.ShapeDtypeStruct(shape, F32) for shape, _ in outs),
        in_specs=[pl.BlockSpec((1, 2 * ROWS, PACK), lambda l: (l, 0, 0))] + [whole(a.shape) for a in args],
        out_specs=tuple(spec or whole(shape) for shape, spec in outs),
    )(total, *args)


def local(
    audio_clips,
    mel_frames,
    crop_offsets,
    inv_weight,
    initial_projection_weight,
    start_bias,
    cond_weight,
    in_weight,
    in_bias,
    res_weight,
    res_bias,
    skip_projection_weight,
    skip_output_bias,
    final_projection_weight,
    end_bias,
):
    skip_bias = skip_output_bias[None]
    audio, mel, cond_ext, local_small, end_column = run_prepare(
        crop_offsets,
        audio_clips,
        jnp.swapaxes(mel_frames, 1, 2),
        jnp.swapaxes(cond_weight, 2, 3),
        in_bias,
        initial_projection_weight.T,
        start_bias[None],
        res_bias,
        skip_bias,
        final_projection_weight,
        end_bias[None],
    )
    total, _, _, _, frames, mel_grad, sums, inverse, log_abs, small, _, mine, end_own = run_flow(
        lax.axis_size("dp"),
        in_weight.reshape(LAYERS, 2 * ROWS, CONV),
        cond_ext,
        res_weight,
        skip_projection_weight,
        audio,
        mel,
        inv_weight,
        local_small,
        end_column,
    )
    crops = lax.axis_size("dp") * audio_clips.shape[0]
    outs = list(
        run_finish(
            crops, total, sums, mine, small, frames, mel_grad, inverse, log_abs, end_own,
            final_projection_weight, skip_bias,
        )
    )
    for k, shape in ((1, (1,)), (2, (1,)), (7, (ROWS,)), (14, (ROWS,)), (16, (CH,))):
        outs[k] = outs[k].reshape(shape)
    outs[4] = jnp.swapaxes(outs[4], 1, 2)
    outs[6] = outs[6].T
    outs[8] = jnp.swapaxes(outs[8], 2, 3)
    return tuple(outs)


def solution(mesh):
    in_specs = (
        P("dp", None, None),
        P("dp", None, None),
        P("dp"),
        P(),
        P("chan", None),
        P("chan"),
        P(None, None, "chan", None),
        P(None, None, "chan", None),
        P(None, None, "chan"),
        P(None, None, "chan"),
        P(None, "chan"),
        P(None, None, "chan"),
        P("chan"),
        P(None, "chan"),
        P(),
    )
    out_specs = (
        P("dp", None, None),
        P("dp"),
        P("dp"),
        P("dp", None, None),
        P("dp", None, None),
        P(),
        P("chan", None),
        P("chan"),
        P(None, None, "chan", None),
        P(None, None, "chan", None),
        P(None, None, "chan"),
        P(None, None, "chan"),
        P(None, "chan"),
        P(None, None, "chan"),
        P("chan"),
        P(None, "chan"),
        P(),
    )
    return jax.shard_map(local, mesh=mesh, in_specs=in_specs, out_specs=out_specs, check_vma=False)
```

```python
import functools

import jax
import jax.numpy as jnp
from jax import lax
from jax.experimental import pallas as pl
from jax.experimental.pallas import tpu as pltpu
from jax.sharding import PartitionSpec as P

CH = 8
HALF = 4
MEL = 80
LAYERS = 8
HOP = 32
FRAMES = 2048
WIDTH = 512
CONV = 1536
EXT = 1664
PACK = 1920
SHARDS = 4
ROWS = 128
BLOCK = FRAMES // SHARDS
PAD = 16
EDGE = 128

HIGH = lax.Precision.HIGHEST
F32 = jnp.float32
BF16 = jnp.bfloat16
MESH = pl.DeviceIdType.MESH
VMEM_LIMIT = 62 << 20


def dot(a, b):
    return jnp.dot(a, b, preferred_element_type=F32)


def dot_nt(a, b):
    return lax.dot_general(a, b, (((1,), (1,)), ((), ())), preferred_element_type=F32)


def dot_tn(a, b):
    return lax.dot_general(a, b, (((0,), (0,)), ((), ())), preferred_element_type=F32)


def when(cond):
    if cond is True:
        return lambda f: f()
    return pl.when(cond)


class Place:
    def __init__(self):
        self.dp = lax.axis_index("dp")
        self.chan = lax.axis_index("chan")
        self.core = self.chan % 2
        self.side = self.chan // 2
        self.bit = self.dp % 2

    def chan_device(self, chan):
        return (self.dp, chan)

    @property
    def core_shard(self):
        return self.side * 2 + 1 - self.core

    @property
    def far_shard(self):
        return (1 - self.side) * 2 + self.core

    @property
    def diag_shard(self):
        return (1 - self.side) * 2 + 1 - self.core

    def dp_bit(self, k):
        return (self.dp // 2**k) % 2

    def dp_device(self, k):
        return (self.dp + 2**k * (1 - 2 * self.dp_bit(k)), self.chan)


def greet(devices):
    barrier = pltpu.get_barrier_semaphore()
    for device in devices:
        pl.semaphore_signal(barrier, inc=1, device_id=device, device_id_type=MESH)
    pl.semaphore_wait(barrier, len(devices))


def remote(src, dst, send, recv, device):
    return pltpu.make_async_remote_copy(
        src_ref=src, dst_ref=dst, send_sem=send, recv_sem=recv, device_id=device, device_id_type=MESH
    )


def levels_of(dp_size):
    levels, rows, bit = [], 2 * ROWS, 0
    while 2**bit < dp_size:
        after = rows // 2 if rows > PAD else rows
        levels.append((bit, rows, after))
        rows, bit = after, bit + 1
    return levels


ACROSS = pl.ds(0, 6 * ROWS)
ALONG = pl.ds(6 * ROWS, PACK - 6 * ROWS)
DEPTH = 4


def mesh_line(levels):
    return len(levels) == 3


def line_shapes():
    a, b = ACROSS.size, ALONG.size
    return [(2, ROWS // 2, a), (ROWS // 2, a), (ROWS // 4, a), (ROWS, b), (ROWS // 2, b), (ROWS // 4, b)]


class Lane:
    def __init__(self, buf, send, recv, credit, device):
        self.buf, self.send, self.recv, self.credit, self.device = buf, send, recv, credit, device

    def copy(self, i, src):
        d = i % DEPTH
        return remote(src, self.buf.at[d], self.send.at[d], self.recv.at[d], self.device)

    def start(self, i, src):
        @pl.when(i >= DEPTH)
        def _():
            self.copy(i, src).wait_send()
            pl.semaphore_wait(self.credit, 1)

        self.copy(i, src).start()

    def wait(self, i):
        d = i % DEPTH
        remote(self.buf.at[d], self.buf.at[d], self.send.at[d], self.recv.at[d], self.device).wait_recv()

    def free(self):
        pl.semaphore_signal(self.credit, inc=1, device_id=self.device, device_id_type=MESH)

    def finish(self):
        for d in range(DEPTH):
            ref = self.buf.at[d]
            remote(ref, ref, self.send.at[d], self.recv.at[d], self.device).wait_send()
            pl.semaphore_wait(self.credit, 1)


def split(values):
    high = values.astype(BF16).astype(F32)
    return high, values - high


def flow_kernel(
    levels,
    in_weight, cond_weight, res_weight, skip_weight, audio, mel, inv_weight, local_small, end_bias,
    total, weights_out, ext_out, acts_out, frames_out, mel_out, sums_out, inverse_out, log_out, small, end_out,
    mine_out, end_own_out,
    shared, hid, ext, acts, top, bottom, wbuf, low, low_t, tap0, tap2, grad, mel_sum, edge_out, edge_in,
    fold, keep, og_rows, out, small_in, end_in, *rest,
):
    line = mesh_line(levels)
    n_bufs = len(line_shapes()) if line else len(levels)
    level_bufs = rest[:n_bufs]
    (
        own_sem, send, recv, keep_sem, ext_sem, acts_sem,
        top_send, top_recv, bottom_send, bottom_recv,
        small_send, small_recv, fold_send, fold_recv,
        phase, w_sem, core_send, core_recv, credit, far_send, far_recv,
        rs_send, rs_recv, ag_send, ag_recv, out_sem, edge_send, edge_recv,
        sum_send, sum_recv, end_send, end_recv, frames_send, frames_recv, mel_send, mel_recv,
        lane_send, lane_recv, lane_credit, way_send, way_recv,
    ) = rest[n_bufs:]
    me = Place()
    core_dev = me.chan_device(me.core_shard)
    far_dev = me.chan_device(me.far_shard)
    diag_dev = me.chan_device(me.diag_shard)
    chan_devs = [core_dev, far_dev, diag_dev]
    has_prev = me.chan > 0
    has_next = me.chan < SHARDS - 1
    prev_dev = me.chan_device(jnp.maximum(me.chan - 1, 0))
    next_dev = me.chan_device(jnp.minimum(me.chan + 1, SHARDS - 1))

    quarter = ROWS // 2
    xb, zb = me.dp_bit(0), me.dp_bit(1)

    def quarter_at(x, z, first=0, rows=quarter):
        return pl.ds(pl.multiple_of((x * 2 + z) * quarter + first, 32), rows)

    half_quarter = quarter // 2

    def own_copies(l):
        dst = shared.at[l * SHARDS + me.chan]
        return [
            pltpu.make_async_copy(in_weight.at[l], dst.at[:, pl.ds(0, CONV)], own_sem.at[0, l]),
            pltpu.make_async_copy(cond_weight.at[l], dst.at[:, pl.ds(CONV, ROWS)], own_sem.at[1, l]),
        ]

    def res_copies(l):
        dst = shared.at[l * SHARDS + me.chan]
        return [
            pltpu.make_async_copy(
                res_weight.at[l, pl.ds(h * 2 * ROWS, 2 * ROWS)],
                dst.at[:, pl.ds(EXT + h * ROWS, ROWS)],
                own_sem.at[2 + h, l],
            )
            for h in range(2)
        ]

    def link(kind, l, shard, at, device):
        ref = shared.at[l * SHARDS + shard, at] if at is not None else shared.at[l * SHARDS + shard]
        return remote(ref, ref, send.at[kind, l], recv.at[kind, l], device)

    x_dev, z_dev = me.dp_device(0), me.dp_device(1)

    def far_a(l, shard):
        return link(0, l, shard, quarter_at(xb, zb), far_dev)

    def far_b(l, shard):
        return link(1, l, shard, quarter_at(1 - xb, 1 - zb, 0, half_quarter), far_dev)

    def x_a(l, x):
        return link(2, l, me.far_shard, quarter_at(x, zb), x_dev)

    def z_a(l, z):
        return link(3, l, me.far_shard, quarter_at(xb, z), z_dev)

    def x_b(l, x):
        return link(4, l, me.far_shard, quarter_at(x, 1 - zb, half_quarter, half_quarter), x_dev)

    def core_a(l, shard):
        return link(5, l, shard, None, core_dev)

    def core_b(l, shard):
        return link(6, l, shard, None, core_dev)

    def issue(l):
        for copy in own_copies(l):
            copy.wait()

        @pl.when(l < LAYERS - 1)
        def _():
            for copy in res_copies(l):
                copy.wait()

        far_a(l, me.chan).start()
        far_b(l, me.chan).start()
        core_a(l, me.chan).start()

    def relay_a(l):
        far_a(l, me.far_shard).wait_recv()
        x_a(l, xb).start()
        z_a(l, zb).start()

    def relay_b(l):
        z_a(l, 1 - zb).wait_recv()
        x_b(l, xb).start()

    def relay_c(l):
        far_b(l, me.far_shard).wait_recv()
        x_a(l, 1 - xb).wait_recv()
        x_b(l, 1 - xb).wait_recv()
        core_b(l, me.far_shard).start()

    def arrive(l):
        core_a(l, me.core_shard).wait_recv()
        core_b(l, me.diag_shard).wait_recv()

    shared[(LAYERS - 1) * SHARDS + me.chan, :, EXT:] = jnp.zeros((2 * ROWS, 2 * ROWS), BF16)

    def first_copies(l, carry):
        for copy in own_copies(l):
            copy.start()

        @pl.when(l < LAYERS - 1)
        def _():
            for copy in res_copies(l):
                copy.start()

        return carry

    lax.fori_loop(0, LAYERS, first_copies, 0)

    @pl.when(jnp.logical_not(has_prev))
    def _():
        top[...] = jnp.zeros_like(top)

    @pl.when(jnp.logical_not(has_next))
    def _():
        bottom[...] = jnp.zeros_like(bottom)

    edge_in[...] = jnp.zeros_like(edge_in)
    opp_dev = (6 + 2 * xb - me.dp, me.chan) if line else None
    greet(chan_devs + [me.dp_device(bit) for bit, _, _ in levels] + ([opp_dev] if line else []))

    def small_copy(k):
        return remote(local_small, small.at[me.chan], small_send.at[k], small_recv.at[k], chan_devs[k])

    def fold_copy(k):
        return remote(fold.at[me.chan], fold.at[me.chan], fold_send.at[k], fold_recv.at[k], chan_devs[k])

    issue(0)
    for k in range(3):
        small_copy(k).start()
    small[me.chan] = local_small[...]

    rows8 = lax.broadcasted_iota(jnp.int32, (CH, BLOCK), 0)
    mixed = jnp.zeros((CH, BLOCK), F32)
    for j in range(CH):
        mixed = mixed + inv_weight[:, j : j + 1] * audio[j : j + 1, :]
    first_ext = jnp.where(rows8 < HALF, mixed, jnp.where(rows8 == HALF, 1.0, 0.0))
    keep[0] = mixed
    keep[1] = first_ext
    for r in range(BLOCK // HOP):
        row = jnp.broadcast_to(mel[r : r + 1, :], (HOP, ROWS)).astype(BF16)
        for slot in range(2):
            ext[slot, pl.ds(r * HOP, HOP), CONV:] = row
    out[...] = jnp.zeros_like(out)
    for k in range(3):
        small_copy(k).wait_recv()

    def small_row(lo, hi):
        return jnp.concatenate([small[s, lo:hi, :] for s in range(SHARDS)], axis=1)

    start_ext = jnp.where(rows8 <= HALF, small_row(0, 8), 0.0)
    keep[2] = start_ext
    hid[pl.ds(PAD, BLOCK), :] = lax.dot_general(
        first_ext, start_ext, (((0,), (0,)), ((), ())), precision=HIGH, preferred_element_type=F32
    )
    relay_a(0)
    issue(1)
    final = small_row(16, 24)
    final_high, final_low = split(final)
    final_rows = jnp.concatenate([final_high, final_low], axis=0).astype(BF16)
    for l in range(LAYERS):
        both = dot(final_rows, skip_weight[l])
        high, rest_of = split(both[:CH] + both[CH:])
        fold[me.chan, l] = jnp.concatenate([high, rest_of, high, jnp.zeros_like(high)], axis=0).astype(BF16)
    for k in range(3):
        fold_copy(k).start()
    skip_bias = small_row(13, 14)
    const = jnp.sum(final * skip_bias, axis=1, keepdims=True) + end_bias[...]

    relay_b(0)
    aug = jnp.concatenate(
        [
            inv_weight[...],
            jnp.where(
                lax.broadcasted_iota(jnp.int32, (CH, CH), 0) == lax.broadcasted_iota(jnp.int32, (CH, CH), 1), 1.0, 0.0
            ),
        ],
        axis=1,
    )
    aug_rows = lax.broadcasted_iota(jnp.int32, (CH, 2 * CH), 0)
    log_total = jnp.zeros((1, 1), F32)
    for c in range(CH):
        pivot = aug[c : c + 1, c : c + 1]
        log_total = log_total + jnp.log(pivot)
        pivot_row = aug[c : c + 1, :] / pivot
        aug = jnp.where(aug_rows == c, pivot_row, aug - aug[:, c : c + 1] * pivot_row)
    inverse_out[...] = aug
    log_out[...] = jnp.broadcast_to(log_total, log_out.shape)
    relay_a(1)
    issue(2)
    relay_c(0)
    relay_b(1)

    def ext_copy(l):
        return pltpu.make_async_copy(ext.at[l % 2], ext_out.at[l], ext_sem.at[l % 2])

    def acts_copy(l):
        return pltpu.make_async_copy(acts.at[l % 2], acts_out.at[l], acts_sem.at[l % 2])

    def keep_copy(l):
        return pltpu.make_async_copy(
            shared.at[pl.ds(l * SHARDS, SHARDS)], weights_out.at[l], keep_sem.at[l]
        )

    def to_next(l, rows):
        p = l % 2
        return remote(
            ext.at[p, pl.ds(BLOCK - rows, rows), pl.ds(WIDTH, WIDTH)],
            top.at[p, pl.ds(EDGE - rows, rows)],
            top_send.at[p], top_recv.at[p], next_dev,
        )

    def to_prev(l, rows):
        p = l % 2
        return remote(
            ext.at[p, pl.ds(0, rows), pl.ds(WIDTH, WIDTH)],
            bottom.at[p, pl.ds(0, rows)],
            bottom_send.at[p], bottom_recv.at[p], prev_dev,
        )

    def by_edge(l, f):
        pl.when(l <= 4)(lambda: f(PAD))
        pl.when(l > 4)(lambda: f(EDGE))

    def forward(l, carry):
        p = l % 2
        pl.when(l + 2 < LAYERS)(lambda: relay_a(l + 2))
        arrive(l)
        pl.when(l < LAYERS - 1)(lambda: keep_copy(l).start())

        @pl.when(l >= 2)
        def _():
            ext_copy(l - 2).wait()
            acts_copy(l - 2).wait()

        ext[p, :, WIDTH : 2 * WIDTH] = hid[pl.ds(PAD, BLOCK), :].astype(BF16)

        def start(rows):
            pl.when(has_next)(lambda: to_next(l, rows).start())
            pl.when(has_prev)(lambda: to_prev(l, rows).start())

        def finish(rows):
            @pl.when(has_next)
            def _():
                to_next(l, rows).wait_send()
                to_prev(l, rows).wait_recv()

            @pl.when(has_prev)
            def _():
                to_prev(l, rows).wait_send()
                to_next(l, rows).wait_recv()

        by_edge(l, start)
        pl.when(l + 3 < LAYERS)(lambda: issue(l + 3))
        by_edge(l, finish)
        hid[pl.ds(0, PAD), :] = top[p, pl.ds(EDGE - PAD, PAD), :].astype(F32)
        hid[pl.ds(PAD + BLOCK, PAD), :] = bottom[p, pl.ds(0, PAD), :].astype(F32)
        for layer in range(LAYERS):
            d = 2**layer

            @pl.when(l == layer)
            def _():
                if d < PAD:
                    ext[p, :, :WIDTH] = hid[pl.ds(PAD - d, BLOCK), :].astype(BF16)
                    ext[p, :, 2 * WIDTH : CONV] = hid[pl.ds(PAD + d, BLOCK), :].astype(BF16)
                else:
                    ext[p, :d, :WIDTH] = top[p, EDGE - d :, :]
                    ext[p, d:, :WIDTH] = ext[p, : BLOCK - d, WIDTH : 2 * WIDTH]
                    ext[p, BLOCK - d :, 2 * WIDTH : CONV] = bottom[p, :d, :]
                    ext[p, : BLOCK - d, 2 * WIDTH : CONV] = ext[p, d:, WIDTH : 2 * WIDTH]

        ext_copy(l).start()

        def one(s, carry):
            pre = dot_nt(ext[p], shared[l * SHARDS + s, :, :EXT])
            t = jnp.tanh(pre[:, :ROWS])
            g = 0.5 * jnp.tanh(0.5 * pre[:, ROWS:]) + 0.5
            tg = t * g
            acts[p, s, 0] = tg.astype(BF16)
            acts[p, s, 1] = (g - t * tg).astype(BF16)
            acts[p, s, 2] = (tg * (1.0 - g)).astype(BF16)
            return carry

        lax.fori_loop(0, SHARDS, one, 0)
        acts_copy(l).start()

        @pl.when(l == 0)
        def _():
            for k in range(3):
                fold_copy(k).wait_recv()

        gated = jnp.concatenate([acts[p, s, 0] for s in range(SHARDS)], axis=1)
        out[...] += dot_nt(jnp.concatenate([fold[s, l, : 2 * CH, :] for s in range(SHARDS)], axis=1), gated)

        @pl.when(l < LAYERS - 1)
        def _():
            for h in range(2):
                res = jnp.concatenate(
                    [shared[l * SHARDS + s, :, EXT + h * ROWS : EXT + (h + 1) * ROWS] for s in range(SHARDS)], axis=1
                )
                bias = jnp.concatenate([small[s, pl.ds(5 + l, 1), :] for s in (2 * h, 2 * h + 1)], axis=1)
                cols = slice(h * 2 * ROWS, (h + 1) * 2 * ROWS)
                hid[pl.ds(PAD, BLOCK), cols] += dot_nt(gated, res) + bias

        pl.when(l + 1 < LAYERS)(lambda: relay_c(l + 1))
        pl.when(l + 2 < LAYERS)(lambda: relay_b(l + 2))
        return carry

    lax.fori_loop(0, LAYERS, forward, 0)

    both = out[...]
    output = both[:CH] + both[CH:] + const
    log_scale, shift = output[:HALF], output[HALF:]
    scale = jnp.exp(log_scale)
    mixed = keep[0]
    second = mixed[HALF:]
    second_out = scale * second + shift
    mine = pl.ds(pl.multiple_of(me.chan * BLOCK, BLOCK), BLOCK)
    frames_out[0:CH, mine] = jnp.concatenate([mixed[:HALF], second_out], axis=0)
    frames_out[2 * CH : 3 * CH, mine] = jnp.concatenate([log_scale, jnp.zeros_like(log_scale)], axis=0)
    out_grad = jnp.concatenate([second_out * scale * second - 1.0, second_out], axis=0)
    keep[3] = jnp.concatenate([jnp.zeros_like(scale), second_out * scale], axis=0)
    og_high, og_low = split(out_grad)
    og_rows[...] = jnp.concatenate([og_high, og_low], axis=0).astype(BF16)
    og_stack = jnp.concatenate([og_high, og_high, og_low, jnp.zeros((ROWS - 3 * CH, BLOCK), F32)], axis=0)
    low[:, WIDTH:] = og_stack.T.astype(BF16)
    end_sum = jnp.sum(out_grad, axis=1, keepdims=True)
    grad[...] = jnp.zeros_like(grad)
    mel_sum[...] = jnp.zeros_like(mel_sum)

    def drain_forward(l, carry):
        far_a(l, me.chan).wait_send()
        far_b(l, me.chan).wait_send()
        x_a(l, xb).wait_send()
        z_a(l, zb).wait_send()
        x_b(l, xb).wait_send()
        core_a(l, me.chan).wait_send()
        core_b(l, me.far_shard).wait_send()
        pl.when(l < LAYERS - 1)(lambda: keep_copy(l).wait())
        return carry

    lax.fori_loop(0, LAYERS, drain_forward, 0)
    for l in (LAYERS - 2, LAYERS - 1):
        ext_copy(l).wait()
        acts_copy(l).wait()
    for k in range(3):
        small_copy(k).wait_send()
        fold_copy(k).wait_send()
    pl.semaphore_signal(phase.at[0], inc=1, device_id=core_dev, device_id_type=MESH)
    pl.semaphore_signal(phase.at[1], inc=1, device_id=far_dev, device_id_type=MESH)

    def shard_of(j):
        core = jnp.where(j < 2, 1 - me.core, me.core)
        return (j % 2) * 2 + core

    def w_copy(q):
        l, s = LAYERS - 1 - q // SHARDS, shard_of(q % SHARDS)
        return pltpu.make_async_copy(weights_out.at[l, s], wbuf.at[q % 2], w_sem.at[q % 2])

    def w_start(q):
        s = shard_of(q % SHARDS)
        here = pltpu.make_async_copy(shared.at[(LAYERS - 1) * SHARDS + s], wbuf.at[q % 2], w_sem.at[q % 2])
        pl.when(q < SHARDS)(lambda: here.start())
        pl.when(q >= SHARDS)(lambda: w_copy(q).start())

    def ext_back(l):
        return pltpu.make_async_copy(ext_out.at[l], ext.at[l % 2], ext_sem.at[l % 2])

    def acts_back(l):
        return pltpu.make_async_copy(acts_out.at[l], acts.at[l % 2], acts_sem.at[l % 2])

    def kept(i, ys):
        return 4 + 2 * i + ys

    def got_core(i, ys):
        return 20 + 2 * (i % 2) + ys

    def to_core(i, ys):
        p = i % 2
        return remote(
            shared.at[2 * p + ys], shared.at[got_core(i, ys)], core_send.at[p, ys], core_recv.at[p, ys], core_dev
        )

    def to_far(i):
        return remote(shared.at[kept(i, 1 - me.side)], shared.at[24 + i], far_send.at[i], far_recv.at[i], far_dev)

    def add_rows(block, base, rows, src, src_at):
        chunk = min(rows, 32)

        def body(k, carry):
            at = pl.ds(pl.multiple_of(base + k * chunk, PAD), chunk)
            shared[block, at, :] = shared[block, at, :] + src[src_at, pl.ds(pl.multiple_of(k * chunk, PAD), chunk), :]
            return carry

        lax.fori_loop(0, rows // chunk, body, 0)

    base_at = [0]
    for bit, rows, after in levels:
        base_at.append(base_at[-1] + (me.dp_bit(bit) * after if after < rows else 0))

    def rs(k, i):
        bit, rows, after = levels[k]
        first = base_at[k] + ((1 - me.dp_bit(bit)) * after if after < rows else 0)
        at = pl.ds(pl.multiple_of(first, PAD), after)
        return remote(
            shared.at[kept(i, me.side), at], level_bufs[k].at[i], rs_send.at[k, i], rs_recv.at[k, i], me.dp_device(bit)
        )

    def ag(k, i, arriving):
        bit, rows, after = levels[k]
        first = base_at[k] + (1 - me.dp_bit(bit)) * after if arriving else base_at[k + 1]
        ref = total.at[LAYERS - 1 - i, pl.ds(pl.multiple_of(first, PAD), after)]
        return remote(ref, ref, ag_send.at[k, i], ag_recv.at[k, i], me.dp_device(bit))

    halving = [k for k, (bit, rows, after) in enumerate(levels) if after < rows]

    def out_copy(i):
        at = pl.ds(pl.multiple_of(base_at[-1], PAD), levels[-1][2])
        return pltpu.make_async_copy(shared.at[kept(i, me.side), at], total.at[LAYERS - 1 - i, at], out_sem.at[0, i])

    def stage_core(i):
        for ys in (1 - me.side, me.side):
            to_core(i, ys).wait_recv()
            add_rows(kept(i, ys), 0, 2 * ROWS, shared, got_core(i, ys))
            pl.semaphore_signal(credit.at[ys], inc=1, device_id=core_dev, device_id_type=MESH)
            if ys is not me.side:
                pl.when(i == 0)(lambda: pl.semaphore_wait(phase.at[1], 1))
                if not line:
                    to_far(i).start()

    def stage_far(i):
        to_far(i).wait_recv()
        add_rows(kept(i, me.side), 0, 2 * ROWS, shared, 24 + i)
        rs(0, i).start()

    def stage_rs(k, i):
        bit, rows, after = levels[k]
        rs(k, i).wait_recv()
        if after == rows:
            rs(k, i).wait_send()
        add_rows(kept(i, me.side), base_at[k + 1], after, level_bufs[k], i)
        if k + 1 < len(levels):
            rs(k + 1, i).start()
        else:
            out_copy(i).start()
            out_copy(i).wait()
            ag(halving[-1], i, False).start()

    def stage_ag(n, i):
        ag(halving[n], i, True).wait_recv()
        if n > 0:
            ag(halving[n - 1], i, False).start()

    def add_block(block, base, rows, cols, src, src_base=0):
        chunk = min(rows, 64)

        def body(k, carry):
            at = pl.ds(pl.multiple_of(base + k * chunk, 32), chunk)
            got = src[pl.ds(pl.multiple_of(src_base + k * chunk, 32), chunk), :]
            shared[block, at, cols] = shared[block, at, cols] + got
            return carry

        lax.fori_loop(0, rows // chunk, body, 0)

    def rows_at(first, rows):
        return pl.ds(pl.multiple_of(first, 32), rows)

    if line:
        zc = me.dp // 2
        inner = (zc == 1) | (zc == 2)
        edge = jnp.logical_not(inner)
        hb = jnp.where(zc == 2, 1, 0)
        lane_devs = [x_dev, z_dev, opp_dev, z_dev, opp_dev, x_dev]
        lanes = [
            Lane(level_bufs[k], lane_send.at[k], lane_recv.at[k], lane_credit.at[k], lane_devs[k]) for k in range(6)
        ]
        qx, q1, q2, r1, r2, rx = lanes
        wide, half, small_half = ROWS, ROWS // 2, ROWS // 4

        def q_rows(u, x):
            return x * wide + u % 2 * half

        def r_rows(u):
            return u % 2 * wide

        def far_way(k, u, rows, cols):
            i = u // 2
            return remote(
                shared.at[kept(i, 1 - me.side), rows, cols], shared.at[24 + i, rows, cols],
                way_send.at[k, u], way_recv.at[k, u], far_dev,
            )

        def far_q(u):
            return far_way(0, u, rows_at(q_rows(u, xb), half), ACROSS)

        def far_r(u):
            return far_way(1, u, rows_at(r_rows(u), wide), ALONG)

        def own_ref(u, first, rows, cols):
            return shared.at[kept(u // 2, me.side), rows_at(first, rows), cols]

        def total_ref(u, first, rows, cols):
            return total.at[LAYERS - 1 - u // 2, rows_at(first, rows), cols]

        def way(k, u, src, dst, device):
            return remote(src, dst, way_send.at[k, u], way_recv.at[k, u], device)

        def q_inner(u, b):
            at = (u, q_rows(u, xb) + b * small_half, small_half, ACROSS)
            return way(2, u, own_ref(*at), total_ref(*at), opp_dev)

        def q_edge(u):
            ref = total_ref(u, q_rows(u, xb), half, ACROSS)
            return way(3, u, ref, ref, z_dev)

        def q_x(u, x):
            ref = total_ref(u, q_rows(u, x), half, ACROSS)
            return way(4, u, ref, ref, x_dev)

        def r_x(u, x):
            at = (u, r_rows(u) + hb * half + x * small_half, small_half, ALONG)
            return way(5, u, own_ref(*at), total_ref(*at), x_dev)

        def r_inner(u, b):
            ref = total_ref(u, r_rows(u) + b * half, half, ALONG)
            return way(6, u, ref, ref, opp_dev)

        def r_edge(u):
            ref = total_ref(u, r_rows(u), wide, ALONG)
            return way(7, u, ref, ref, z_dev)

        def q_out(u):
            at = (u, q_rows(u, xb) + hb * small_half, small_half, ACROSS)
            return pltpu.make_async_copy(own_ref(*at), total_ref(*at), out_sem.at[0, u])

        def r_out(u):
            at = (u, r_rows(u) + hb * half + xb * small_half, small_half, ALONG)
            return pltpu.make_async_copy(own_ref(*at), total_ref(*at), out_sem.at[1, u])

        def start_ways(u):
            far_r(u).start()
            qx.start(u, shared.at[pl.ds(kept(u // 2, 0), 2), rows_at(q_rows(u, 1 - xb), half), ACROSS])

        def q_stage1(u):
            qx.wait(u)
            for ys in (1 - me.side, me.side):
                add_block(kept(u // 2, ys), q_rows(u, xb), half, ACROSS, qx.buf.at[u % DEPTH, ys])
                if ys is not me.side:
                    far_q(u).start()
            qx.free()

        def r_stage1(u):
            far_r(u).wait_recv()
            add_block(kept(u // 2, me.side), r_rows(u), wide, ALONG, shared.at[24 + u // 2, :, ALONG], r_rows(u))
            pl.when(edge)(lambda: r1.start(u, own_ref(u, r_rows(u), wide, ALONG)))

        def q_stage2(u):
            far_q(u).wait_recv()
            first = q_rows(u, xb)
            add_block(kept(u // 2, me.side), first, half, ACROSS, shared.at[24 + u // 2, :, ACROSS], first)
            pl.when(edge)(lambda: q1.start(u, own_ref(u, first, half, ACROSS)))

        def r_stage2(u):
            @pl.when(inner)
            def _():
                r1.wait(u)
                add_block(kept(u // 2, me.side), r_rows(u), wide, ALONG, r1.buf.at[u % DEPTH])
                r1.free()
                r2.start(u, own_ref(u, r_rows(u) + (1 - hb) * half, half, ALONG))

        def q_stage3(u):
            @pl.when(inner)
            def _():
                first = q_rows(u, xb)
                q1.wait(u)
                add_block(kept(u // 2, me.side), first, half, ACROSS, q1.buf.at[u % DEPTH])
                q1.free()
                q2.start(u, own_ref(u, first + (1 - hb) * small_half, small_half, ACROSS))

        def r_stage3(u):
            @pl.when(inner)
            def _():
                first = r_rows(u) + hb * half
                r2.wait(u)
                add_block(kept(u // 2, me.side), first, half, ALONG, r2.buf.at[u % DEPTH])
                r2.free()
                rx.start(u, own_ref(u, first + (1 - xb) * small_half, small_half, ALONG))

        def q_stage4(u):
            @pl.when(inner)
            def _():
                q2.wait(u)
                first = q_rows(u, xb) + hb * small_half
                add_block(kept(u // 2, me.side), first, small_half, ACROSS, q2.buf.at[u % DEPTH])
                q2.free()
                q_inner(u, hb).start()
                q_out(u).start()

        def r_stage4(u):
            @pl.when(inner)
            def _():
                rx.wait(u)
                first = r_rows(u) + hb * half + xb * small_half
                add_block(kept(u // 2, me.side), first, small_half, ALONG, rx.buf.at[u % DEPTH])
                rx.free()
                r_x(u, xb).start()
                r_out(u).start()

        def q_stage5(u):
            @pl.when(inner)
            def _():
                q_out(u).wait()
                q_inner(u, 1 - hb).wait_recv()
                q_edge(u).start()
                q_x(u, xb).start()

        def r_stage5(u):
            @pl.when(inner)
            def _():
                r_out(u).wait()
                r_x(u, 1 - xb).wait_recv()
                r_inner(u, hb).start()

        def q_stage6(u):
            @pl.when(edge)
            def _():
                q_edge(u).wait_recv()
                q_x(u, xb).start()

        def r_stage6(u):
            @pl.when(inner)
            def _():
                r_inner(u, 1 - hb).wait_recv()
                r_edge(u).start()

        def q_stage7(u):
            q_x(u, 1 - xb).wait_recv()

        def r_stage7(u):
            pl.when(edge)(lambda: r_edge(u).wait_recv())

        def drain_ways(u, carry):
            far_q(u).wait_send()
            far_r(u).wait_send()
            q_x(u, xb).wait_send()

            @pl.when(inner)
            def _():
                q_inner(u, hb).wait_send()
                q_edge(u).wait_send()
                r_x(u, xb).wait_send()
                r_inner(u, hb).wait_send()
                r_edge(u).wait_send()

            return carry

        def finish_lanes():
            qx.finish()

            @pl.when(edge)
            def _():
                q1.finish()
                r1.finish()

            @pl.when(inner)
            def _():
                q2.finish()
                r2.finish()
                rx.finish()

        line_stages = [
            [q_stage1, r_stage1], [q_stage2, r_stage2], [q_stage3, r_stage3], [q_stage4, r_stage4],
            [q_stage5, r_stage5], [q_stage6, r_stage6], [q_stage7, r_stage7],
        ]

    def back_prev(i, rows):
        return remote(
            edge_out.at[0, pl.ds(0, rows)], edge_in.at[i % 2, 0, pl.ds(0, rows)],
            edge_send.at[0], edge_recv.at[i % 2, 0], prev_dev,
        )

    def back_next(i, rows):
        return remote(
            edge_out.at[1, pl.ds(EDGE - rows, rows)], edge_in.at[i % 2, 1, pl.ds(EDGE - rows, rows)],
            edge_send.at[1], edge_recv.at[i % 2, 1], next_dev,
        )

    def back_edge(i, f):
        by_edge(LAYERS - 1 - i, f)

    def apply_edges(i):
        def finish(rows):
            @pl.when(has_next)
            def _():
                back_next(i, rows).wait_send()
                back_prev(i, rows).wait_recv()

            @pl.when(has_prev)
            def _():
                back_prev(i, rows).wait_send()
                back_next(i, rows).wait_recv()

        back_edge(i, finish)
        tap0[pl.ds(BLOCK, EDGE), :] = edge_in[i % 2, 0].astype(F32)
        tap2[pl.ds(0, EDGE), :] = edge_in[i % 2, 1].astype(F32)
        for layer in range(LAYERS):
            d = 2**layer

            @pl.when(LAYERS - 1 - i == layer)
            def _():
                grad[...] += tap0[pl.ds(d, BLOCK), :] + tap2[pl.ds(EDGE - d, BLOCK), :]

    def backward_open(i):
        l = LAYERS - 1 - i
        pl.when(i > 0)(lambda: apply_edges(i - 1))
        now = grad[...].astype(BF16)
        low[:, :WIDTH] = now
        low_t[...] = now.T
        sums_out[pl.ds(72 + l, 1), :] = jnp.sum(now.astype(F32), axis=0, keepdims=True)
        tap0[pl.ds(0, BLOCK), :] = jnp.zeros((BLOCK, WIDTH), F32)
        tap2[pl.ds(EDGE, BLOCK), :] = jnp.zeros((BLOCK, WIDTH), F32)

        @pl.when(i >= 2)
        def _():
            ext_back(l).wait()
            acts_back(l).wait()

    def backward_shards(i, h):
        l = LAYERS - 1 - i
        p = l % 2

        def one(k, carry):
            j = 2 * h + k
            q = i * SHARDS + j
            b = q % 2
            s = shard_of(j)
            pl.when(q + 1 < LAYERS * SHARDS)(lambda: w_start(q + 1))

            @pl.when((j < 2) & (i >= 2))
            def _():
                to_core(i - 2, j).wait_send()

            w_copy(q).wait()
            slot = jnp.where(j < 2, 2 * (i % 2) + j, kept(i, j - 2))
            gated = acts[p, s, 0]
            res = jnp.concatenate([wbuf[b, :, EXT : EXT + ROWS], wbuf[b, :, EXT + ROWS :]], axis=0)
            back = dot(low[:, :WIDTH], res) + dot(low[:, WIDTH : WIDTH + 4 * CH], fold[s, l])
            pg = jnp.concatenate(
                [(back * acts[p, s, 1].astype(F32)).astype(BF16), (back * acts[p, s, 2].astype(F32)).astype(BF16)],
                axis=1,
            )
            tap0[pl.ds(0, BLOCK), :] += dot(pg, wbuf[b, :, :WIDTH])
            grad[...] += dot(pg, wbuf[b, :, WIDTH : 2 * WIDTH])
            tap2[pl.ds(EDGE, BLOCK), :] += dot(pg, wbuf[b, :, 2 * WIDTH : CONV])
            mel_sum[...] += dot(pg, wbuf[b, :, CONV:EXT])
            for k in range(3):
                cols = slice(k * WIDTH, (k + 1) * WIDTH)
                shared[slot, :, cols] = dot_tn(pg, ext[p, :, cols]).astype(BF16)
            shared[slot, :, CONV:EXT] = dot_tn(pg, ext[p, :, CONV:]).astype(BF16)
            side = dot(low_t[...], gated).astype(BF16)
            shared[slot, :, EXT : EXT + ROWS] = side[: 2 * ROWS]
            shared[slot, :, EXT + ROWS :] = side[2 * ROWS :]
            e = dot(og_rows[...], gated)
            sums_out[pl.ds(pl.multiple_of(l * CH, CH), CH), pl.ds(pl.multiple_of(s * ROWS, ROWS), ROWS)] = e[:CH] + e[CH:]

            @pl.when(j < 2)
            def _():
                pl.when(q == 0)(lambda: pl.semaphore_wait(phase.at[0], 1))
                pl.when(i >= 2)(lambda: pl.semaphore_wait(credit.at[j], 1))
                to_core(i, j).start()

            return carry

        lax.fori_loop(0, 2, one, 0)

    def backward_close(i):
        l = LAYERS - 1 - i

        @pl.when(l >= 2)
        def _():
            ext_back(l - 2).start()
            acts_back(l - 2).start()

        edge_out[0] = tap0[pl.ds(0, EDGE), :].astype(BF16)
        edge_out[1] = tap2[pl.ds(BLOCK, EDGE), :].astype(BF16)

        def start(rows):
            pl.when(has_next)(lambda: back_next(i, rows).start())
            pl.when(has_prev)(lambda: back_prev(i, rows).start())

        back_edge(i, start)

    sum_devs = [core_dev, far_dev] + [me.dp_device(bit) for bit, _, _ in levels]

    def sum_copy(k):
        return remote(sums_out, small_in.at[k], sum_send.at[k], sum_recv.at[k], sum_devs[k])

    def end_copy(k):
        return remote(end_out, end_in.at[k], end_send.at[k], end_recv.at[k], sum_devs[k])

    def frames_copy(k):
        ref = frames_out.at[:, mine]
        return remote(ref, ref, frames_send.at[k], frames_recv.at[k], chan_devs[k])

    mel_rows = BLOCK // HOP

    def mel_copy(k):
        ref = mel_out.at[pl.ds(pl.multiple_of(me.chan * mel_rows, mel_rows), mel_rows)]
        return remote(ref, ref, mel_send.at[k], mel_recv.at[k], chan_devs[k])

    def last(values, other, dims):
        return lax.dot_general(values, other, (dims, ((), ())), precision=HIGH, preferred_element_type=F32)

    def finish_frames():
        apply_edges(LAYERS - 1)
        hidden_grad = grad[...]
        sums_out[64:72, :] = last(keep[1], hidden_grad, ((1,), (0,)))
        mixed = keep[0]
        first_back = last(keep[2], hidden_grad, ((1,), (1,)))
        rows = lax.broadcasted_iota(jnp.int32, (CH, BLOCK), 0)
        mixed_grad = jnp.where(rows < HALF, mixed + first_back, keep[3])
        frames_out[CH : 2 * CH, mine] = last(inv_weight[...], mixed_grad, ((0,), (0,)))
        inv_part = last(mixed_grad, audio[...], ((1,), (1,)))
        sums_out[80:88, :] = jnp.concatenate([inv_part, end_sum, jnp.zeros((CH, WIDTH - CH - 1), F32)], axis=1)
        mel_out[pl.ds(pl.multiple_of(me.chan * mel_rows, mel_rows), mel_rows), :] = jnp.sum(
            mel_sum[...].reshape(mel_rows, HOP, ROWS), axis=1
        )
        for k in range(3):
            frames_copy(k).start()
            mel_copy(k).start()
        sum_copy(0).start()

    def sum_stage(k):
        sum_copy(k).wait_recv()
        sum_copy(k).wait_send()
        sums_out[...] = sums_out[...] + small_in[k]
        if k + 1 < len(sum_devs):
            sum_copy(k + 1).start()
            return
        e = sums_out[0:64, pl.ds(pl.multiple_of(me.chan * ROWS, ROWS), ROWS)]
        e_high, e_low = split(e)
        end = jnp.zeros((2 * CH, WIDTH), F32)
        for l in range(LAYERS):
            part = slice(l * CH, (l + 1) * CH)
            end = end + dot_nt(jnp.concatenate([e_high[part], e_low[part]], axis=0).astype(BF16), skip_weight[l])
        end_out[...] = end[:CH] + end[CH:]
        end_copy(0).start()

    def end_stage(k):
        end_copy(k).wait_recv()
        end_copy(k).wait_send()
        end_out[...] = end_out[...] + end_in[k]
        if k == 0:
            end_copy(1).start()

    small_stages = [finish_frames]
    small_stages += [functools.partial(sum_stage, k) for k in range(len(sum_devs))]
    small_stages += [functools.partial(end_stage, k) for k in range(2)]

    if line:
        stages = [[stage_core]] + line_stages
    else:
        stages = [[stage_core], [stage_far]]
        stages += [[functools.partial(stage_rs, k)] for k in range(len(levels))]
        stages += [[functools.partial(stage_ag, n)] for n in range(len(halving) - 1, -1, -1)]
    if line:
        steps = 2 * LAYERS + max(len(stages), len(small_stages))
    else:
        steps = 2 * LAYERS + max(2 * len(stages) - 2, len(small_stages))

    w_start(0)

    def step(v, carry):
        i, h = v // 2, v % 2

        @pl.when(v < 2 * LAYERS)
        def _():
            pl.when(h == 0)(lambda: backward_open(i))
            backward_shards(i, h)

            @pl.when(h == 1)
            def _():
                backward_close(i)
                stage_core(i)

        for k, stage in enumerate(small_stages):
            pl.when(v == 2 * LAYERS + k)(stage)
        if line:
            pl.when((v >= 1) & (v <= 2 * LAYERS))(lambda: start_ways(v - 1))
        for lag in range(len(stages) - 1, 0, -1):
            at = v - 1 - lag if line else i - lag
            count = 2 * LAYERS if line else LAYERS
            now = (at >= 0) & (at < count)

            @pl.when(now if line else now & (h == 1))
            def _():
                for stage in stages[lag]:
                    stage(at)

        return carry

    lax.fori_loop(0, steps, step, 0)

    for i in (LAYERS - 2, LAYERS - 1):
        for ys in range(2):
            to_core(i, ys).wait_send()
            pl.semaphore_wait(credit.at[ys], 1)

    def drain(i, carry):
        to_far(i).wait_send()
        for k, (bit, rows, after) in enumerate(levels):
            if after < rows:
                rs(k, i).wait_send()
                ag(k, i, False).wait_send()
        return carry

    if line:
        lax.fori_loop(0, 2 * LAYERS, drain_ways, 0)
        finish_lanes()
    else:
        lax.fori_loop(0, LAYERS, drain, 0)
    for k, shard in enumerate([me.core_shard, me.far_shard, me.diag_shard]):
        frames_copy(k).wait_send()
        mel_copy(k).wait_send()
        frames_copy(k).wait_recv()
        mel_copy(k).wait_recv()
    own_lanes = pl.ds(pl.multiple_of(me.chan * ROWS, ROWS), ROWS)
    mine_out[...] = sums_out[:, own_lanes]
    end_own_out[...] = end_out[:, own_lanes]


def run_flow(dp_size, *args):
    levels = levels_of(dp_size)
    vmem = pl.BlockSpec(memory_space=pltpu.VMEM)
    hbm = pl.BlockSpec(memory_space=pl.ANY)
    dma = pltpu.SemaphoreType.DMA
    regular = pltpu.SemaphoreType.REGULAR
    block = (2 * ROWS, PACK)
    n = len(levels)
    return pl.pallas_call(
        functools.partial(flow_kernel, levels),
        out_shape=(
            jax.ShapeDtypeStruct((LAYERS,) + block, BF16),
            jax.ShapeDtypeStruct((LAYERS, SHARDS) + block, BF16),
            jax.ShapeDtypeStruct((LAYERS, BLOCK, EXT), BF16),
            jax.ShapeDtypeStruct((LAYERS, SHARDS, 3, BLOCK, ROWS), BF16),
            jax.ShapeDtypeStruct((3 * CH, FRAMES), F32),
            jax.ShapeDtypeStruct((FRAMES // HOP, ROWS), F32),
            jax.ShapeDtypeStruct((88, WIDTH), F32),
            jax.ShapeDtypeStruct((CH, 2 * CH), F32),
            jax.ShapeDtypeStruct((CH, ROWS), F32),
            jax.ShapeDtypeStruct((SHARDS, 24, ROWS), F32),
            jax.ShapeDtypeStruct((CH, WIDTH), F32),
            jax.ShapeDtypeStruct((88, ROWS), F32),
            jax.ShapeDtypeStruct((CH, ROWS), F32),
        ),
        in_specs=[hbm] * 3 + [vmem] * 6,
        out_specs=tuple([hbm] * 4 + [vmem] * 9),
        scratch_shapes=[
            pltpu.VMEM((LAYERS * SHARDS,) + block, BF16),
            pltpu.VMEM((PAD + BLOCK + PAD, WIDTH), F32),
            pltpu.VMEM((2, BLOCK, EXT), BF16),
            pltpu.VMEM((2, SHARDS, 3, BLOCK, ROWS), BF16),
            pltpu.VMEM((2, EDGE, WIDTH), BF16),
            pltpu.VMEM((2, EDGE, WIDTH), BF16),
            pltpu.VMEM((2,) + block, BF16),
            pltpu.VMEM((BLOCK, WIDTH + ROWS), BF16),
            pltpu.VMEM((WIDTH, BLOCK), BF16),
            pltpu.VMEM((BLOCK + EDGE, WIDTH), F32),
            pltpu.VMEM((EDGE + BLOCK, WIDTH), F32),
            pltpu.VMEM((BLOCK, WIDTH), F32),
            pltpu.VMEM((BLOCK, ROWS), F32),
            pltpu.VMEM((2, EDGE, WIDTH), BF16),
            pltpu.VMEM((2, 2, EDGE, WIDTH), BF16),
            pltpu.VMEM((SHARDS, LAYERS, 4 * CH, ROWS), BF16),
            pltpu.VMEM((4, CH, BLOCK), F32),
            pltpu.VMEM((2 * CH, BLOCK), BF16),
            pltpu.VMEM((2 * CH, BLOCK), F32),
            pltpu.VMEM((n + 2, 88, WIDTH), F32),
            pltpu.VMEM((2, CH, WIDTH), F32),
        ]
        + (
            [pltpu.VMEM((DEPTH,) + shape, BF16) for shape in line_shapes()]
            if mesh_line(levels)
            else [pltpu.VMEM((LAYERS, after, PACK), BF16) for _, _, after in levels]
        )
        + [
            dma((4, LAYERS)), dma((7, LAYERS)), dma((7, LAYERS)), dma((LAYERS,)), dma((2,)), dma((2,)),
            dma((2,)), dma((2,)), dma((2,)), dma((2,)),
            dma((3,)), dma((3,)), dma((3,)), dma((3,)),
            regular((2,)), dma((2,)), dma((2, 2)), dma((2, 2)), regular((2,)), dma((LAYERS,)), dma((LAYERS,)),
            dma((n, LAYERS)), dma((n, LAYERS)), dma((n, LAYERS)), dma((n, LAYERS)), dma((2, 2 * LAYERS)),
            dma((2,)), dma((2, 2)),
            dma((n + 2,)), dma((n + 2,)), dma((2,)), dma((2,)), dma((3,)), dma((3,)), dma((3,)), dma((3,)),
            dma((6, DEPTH)), dma((6, DEPTH)), regular((6,)), dma((8, 2 * LAYERS)), dma((8, 2 * LAYERS)),
        ],
        compiler_params=pltpu.CompilerParams(
            collective_id=0, has_side_effects=True, vmem_limit_bytes=VMEM_LIMIT
        ),
    )(*args)


def prepare_kernel(
    offset, clip, mel_frames, cond_weight, in_bias, start_weight, start_bias, res_bias, skip_bias, final, end_bias,
    audio, mel, cond_ext, local_small, end_column,
):
    chan = lax.axis_index("chan")
    first = offset[0] * HOP + chan * BLOCK
    length = clip.shape[2]
    audio[...] = pltpu.roll(clip[0], lax.rem(length - first, length), 1)[:, :BLOCK]
    mel_rows = BLOCK // HOP
    clip_rows = mel_frames.shape[1]
    frames = jnp.concatenate([mel_frames[0].astype(F32), jnp.ones((clip_rows, ROWS - MEL), F32)], axis=1)
    frames = pltpu.roll(frames, lax.rem(clip_rows - offset[0] - chan * mel_rows, clip_rows), 0)[:mel_rows]
    lane = lax.broadcasted_iota(jnp.int32, (mel_rows, ROWS), 1)
    mel[...] = jnp.where(lane < MEL + 2, frames, 0.0)
    for l in range(LAYERS):
        high, rest = split(in_bias[l])
        for g in range(2):
            part = jnp.concatenate(
                [
                    cond_weight[l, g].astype(F32),
                    high[g : g + 1],
                    rest[g : g + 1],
                    jnp.zeros((ROWS - MEL - 2, ROWS), F32),
                ],
                axis=0,
            )
            cond_ext[l, g * ROWS : (g + 1) * ROWS, :] = part.T.astype(BF16)
    local_small[...] = jnp.concatenate(
        [
            start_weight[...],
            start_bias[...],
            res_bias[...],
            jnp.zeros((1, ROWS), F32),
            skip_bias[...],
            jnp.zeros((2, ROWS), F32),
            final[...],
        ],
        axis=0,
    )
    row = jnp.concatenate([end_bias[...], jnp.zeros((1, ROWS - CH), F32)], axis=1)
    end_column[...] = jnp.broadcast_to(row, (ROWS, ROWS)).T[:CH, :1]


def run_prepare(*args):
    vmem = pl.BlockSpec(memory_space=pltpu.VMEM)
    return pl.pallas_call(
        prepare_kernel,
        out_shape=(
            jax.ShapeDtypeStruct((CH, BLOCK), F32),
            jax.ShapeDtypeStruct((BLOCK // HOP, ROWS), F32),
            jax.ShapeDtypeStruct((LAYERS, 2 * ROWS, ROWS), BF16),
            jax.ShapeDtypeStruct((24, ROWS), F32),
            jax.ShapeDtypeStruct((CH, 1), F32),
        ),
        in_specs=[pl.BlockSpec(memory_space=pltpu.SMEM)] + [vmem] * 10,
        out_specs=tuple([vmem] * 5),
    )(*args)


def finish_kernel(
    crops, total, sums, mine, small, frames, mel_in, inverse, log_abs, end_in, final_own, skip_bias,
    latent, log_det, loss, audio_grad, mel_grad, inv_grad, start_grad, start_bias_grad, cond_grad, in_grad,
    bias_grad, res_grad, res_bias_grad, skip_grad, skip_bias_grad, end_grad, end_bias_grad,
):
    l = pl.program_id(0)
    for g in range(2):
        rows = slice(g * ROWS, (g + 1) * ROWS)
        in_grad[0, g] = total[0, rows, :CONV].astype(F32)
        cond = total[0, rows, CONV:EXT].astype(F32)
        cond = cond.T
        cond_grad[0, g] = cond[:MEL]
        bias_grad[0, g : g + 1, :] = cond[MEL : MEL + 1]

    @pl.when(l < LAYERS - 1)
    def _():
        res_grad[0, : 2 * ROWS] = total[0, :, EXT : EXT + ROWS].astype(F32)
        res_grad[0, 2 * ROWS :] = total[0, :, EXT + ROWS :].astype(F32)

    final = jnp.concatenate([small[s, 16:24, :] for s in range(SHARDS)], axis=1)
    skip_grad[0] = lax.dot_general(
        final, mine[pl.ds(pl.multiple_of(l * CH, CH), CH), :], (((0,), (0,)), ((), ())),
        precision=HIGH, preferred_element_type=F32,
    )

    @pl.when(l == 0)
    def _():
        z = frames[:CH]
        latent[0] = z
        audio_grad[0] = frames[CH : 2 * CH]
        mel_grad[0] = mel_in[:, :MEL]
        log_scale = frames[2 * CH : 2 * CH + HALF]
        det = jnp.sum(jnp.sum(log_scale, axis=1, keepdims=True), axis=0, keepdims=True) + FRAMES * log_abs[:1, :1]
        squares = jnp.sum(jnp.sum(z * z, axis=1, keepdims=True), axis=0, keepdims=True)
        log_det[...] = det
        loss[...] = (0.5 * squares - det) / (CH * FRAMES)
        tiny = sums[80:88, :ROWS]
        inv_grad[...] = tiny[:, :CH] - crops * FRAMES * inverse[:, CH:].T
        end_column = tiny[:, CH : CH + 1]
        end_bias_grad[...] = jnp.broadcast_to(end_column, (CH, ROWS)).T[:1, :]
        start_grad[...] = mine[64:68, :]
        start_bias_grad[...] = mine[68:69, :]
        res_bias_grad[...] = mine[72:79, :]
        skip_bias_grad[...] = jnp.sum(end_column * final_own[...], axis=0, keepdims=True)
        end_grad[...] = end_in[...] + end_column * skip_bias[...]


def run_finish(crops, total, *args):
    def whole(shape):
        return pl.BlockSpec(shape, lambda l: (0,) * len(shape))

    outs = [
        ((1, CH, FRAMES), None),
        ((1, 1), None),
        ((1, 1), None),
        ((1, CH, FRAMES), None),
        ((1, FRAMES // HOP, MEL), None),
        ((CH, CH), None),
        ((HALF, ROWS), None),
        ((1, ROWS), None),
        ((LAYERS, 2, MEL, ROWS), pl.BlockSpec((1, 2, MEL, ROWS), lambda l: (l, 0, 0, 0))),
        ((LAYERS, 2, ROWS, CONV), pl.BlockSpec((1, 2, ROWS, CONV), lambda l: (l, 0, 0, 0))),
        ((LAYERS, 2, ROWS), pl.BlockSpec((1, 2, ROWS), lambda l: (l, 0, 0))),
        (
            (LAYERS - 1, WIDTH, ROWS),
            pl.BlockSpec((1, WIDTH, ROWS), lambda l: (jnp.minimum(l, LAYERS - 2), 0, 0)),
        ),
        ((LAYERS - 1, ROWS), None),
        ((LAYERS, WIDTH, ROWS), pl.BlockSpec((1, WIDTH, ROWS), lambda l: (l, 0, 0))),
        ((1, ROWS), None),
        ((CH, ROWS), None),
        ((1, CH), None),
    ]
    return pl.pallas_call(
        functools.partial(finish_kernel, crops),
        grid=(LAYERS,),
        out_shape=tuple(jax.ShapeDtypeStruct(shape, F32) for shape, _ in outs),
        in_specs=[pl.BlockSpec((1, 2 * ROWS, PACK), lambda l: (l, 0, 0))] + [whole(a.shape) for a in args],
        out_specs=tuple(spec or whole(shape) for shape, spec in outs),
    )(total, *args)


def local(
    audio_clips,
    mel_frames,
    crop_offsets,
    inv_weight,
    initial_projection_weight,
    start_bias,
    cond_weight,
    in_weight,
    in_bias,
    res_weight,
    res_bias,
    skip_projection_weight,
    skip_output_bias,
    final_projection_weight,
    end_bias,
):
    skip_bias = skip_output_bias[None]
    audio, mel, cond_ext, local_small, end_column = run_prepare(
        crop_offsets,
        audio_clips,
        jnp.swapaxes(mel_frames, 1, 2),
        jnp.swapaxes(cond_weight, 2, 3),
        in_bias,
        initial_projection_weight.T,
        start_bias[None],
        res_bias,
        skip_bias,
        final_projection_weight,
        end_bias[None],
    )
    total, _, _, _, frames, mel_grad, sums, inverse, log_abs, small, _, mine, end_own = run_flow(
        lax.axis_size("dp"),
        in_weight.reshape(LAYERS, 2 * ROWS, CONV),
        cond_ext,
        res_weight,
        skip_projection_weight,
        audio,
        mel,
        inv_weight,
        local_small,
        end_column,
    )
    crops = lax.axis_size("dp") * audio_clips.shape[0]
    outs = list(
        run_finish(
            crops, total, sums, mine, small, frames, mel_grad, inverse, log_abs, end_own,
            final_projection_weight, skip_bias,
        )
    )
    for k, shape in ((1, (1,)), (2, (1,)), (7, (ROWS,)), (14, (ROWS,)), (16, (CH,))):
        outs[k] = outs[k].reshape(shape)
    outs[4] = jnp.swapaxes(outs[4], 1, 2)
    outs[6] = outs[6].T
    outs[8] = jnp.swapaxes(outs[8], 2, 3)
    return tuple(outs)


def solution(mesh):
    in_specs = (
        P("dp", None, None),
        P("dp", None, None),
        P("dp"),
        P(),
        P("chan", None),
        P("chan"),
        P(None, None, "chan", None),
        P(None, None, "chan", None),
        P(None, None, "chan"),
        P(None, None, "chan"),
        P(None, "chan"),
        P(None, None, "chan"),
        P("chan"),
        P(None, "chan"),
        P(),
    )
    out_specs = (
        P("dp", None, None),
        P("dp"),
        P("dp"),
        P("dp", None, None),
        P("dp", None, None),
        P(),
        P("chan", None),
        P("chan"),
        P(None, None, "chan", None),
        P(None, None, "chan", None),
        P(None, None, "chan"),
        P(None, None, "chan"),
        P(None, "chan"),
        P(None, None, "chan"),
        P("chan"),
        P(None, "chan"),
        P(),
    )
    return jax.shard_map(local, mesh=mesh, in_specs=in_specs, out_specs=out_specs, check_vma=False)
```

```python
import functools

import jax
import jax.numpy as jnp
from jax import lax
from jax.experimental import pallas as pl
from jax.experimental.pallas import tpu as pltpu
from jax.sharding import PartitionSpec as P

CH = 8
HALF = 4
MEL = 80
LAYERS = 8
HOP = 32
FRAMES = 2048
WIDTH = 512
CONV = 1536
EXT = 1664
PACK = 1920
SHARDS = 4
ROWS = 128
BLOCK = FRAMES // SHARDS
PAD = 16
EDGE = 128

HIGH = lax.Precision.HIGHEST
F32 = jnp.float32
BF16 = jnp.bfloat16
MESH = pl.DeviceIdType.MESH
VMEM_LIMIT = 62 << 20


def dot(a, b):
    return jnp.dot(a, b, preferred_element_type=F32)


def dot_nt(a, b):
    return lax.dot_general(a, b, (((1,), (1,)), ((), ())), preferred_element_type=F32)


def dot_tn(a, b):
    return lax.dot_general(a, b, (((0,), (0,)), ((), ())), preferred_element_type=F32)


def when(cond):
    if cond is True:
        return lambda f: f()
    return pl.when(cond)


class Place:
    def __init__(self):
        self.dp = lax.axis_index("dp")
        self.chan = lax.axis_index("chan")
        self.core = self.chan % 2
        self.side = self.chan // 2
        self.bit = self.dp % 2

    def chan_device(self, chan):
        return (self.dp, chan)

    @property
    def core_shard(self):
        return self.side * 2 + 1 - self.core

    @property
    def far_shard(self):
        return (1 - self.side) * 2 + self.core

    @property
    def diag_shard(self):
        return (1 - self.side) * 2 + 1 - self.core

    def dp_bit(self, k):
        return (self.dp // 2**k) % 2

    def dp_device(self, k):
        return (self.dp + 2**k * (1 - 2 * self.dp_bit(k)), self.chan)


def greet(devices):
    barrier = pltpu.get_barrier_semaphore()
    for device in devices:
        pl.semaphore_signal(barrier, inc=1, device_id=device, device_id_type=MESH)
    pl.semaphore_wait(barrier, len(devices))


def remote(src, dst, send, recv, device):
    return pltpu.make_async_remote_copy(
        src_ref=src, dst_ref=dst, send_sem=send, recv_sem=recv, device_id=device, device_id_type=MESH
    )


def levels_of(dp_size):
    levels, rows, bit = [], 2 * ROWS, 0
    while 2**bit < dp_size:
        after = rows // 2 if rows > PAD else rows
        levels.append((bit, rows, after))
        rows, bit = after, bit + 1
    return levels


ACROSS = pl.ds(0, 6 * ROWS)
ALONG = pl.ds(6 * ROWS, PACK - 6 * ROWS)
DEPTH = 8
ACROSS_LAGS = (0, 1, 3, 3, 4, 5, 7, 20)
ALONG_LAGS = (0, 1, 2, 3, 4, 5, 6, 21)
ORDER = 'q5 r6 q4 r5 q2 q1 r1 r4 r7 q7 q6 r3 q3 r2'


def mesh_line(levels):
    return len(levels) == 3


def line_shapes():
    a, b = ACROSS.size, ALONG.size
    return [(2, ROWS // 2, a), (ROWS // 2, a), (ROWS // 4, a), (ROWS, b), (ROWS // 2, b), (ROWS // 4, b)]


class Lane:
    def __init__(self, buf, send, recv, credit, device):
        self.buf, self.send, self.recv, self.credit, self.device = buf, send, recv, credit, device

    def copy(self, i, src):
        d = i % DEPTH
        return remote(src, self.buf.at[d], self.send.at[d], self.recv.at[d], self.device)

    def start(self, i, src):
        @pl.when(i >= DEPTH)
        def _():
            self.copy(i, src).wait_send()
            pl.semaphore_wait(self.credit, 1)

        self.copy(i, src).start()

    def wait(self, i):
        d = i % DEPTH
        remote(self.buf.at[d], self.buf.at[d], self.send.at[d], self.recv.at[d], self.device).wait_recv()

    def free(self):
        pl.semaphore_signal(self.credit, inc=1, device_id=self.device, device_id_type=MESH)

    def finish(self):
        for d in range(DEPTH):
            ref = self.buf.at[d]
            remote(ref, ref, self.send.at[d], self.recv.at[d], self.device).wait_send()
            pl.semaphore_wait(self.credit, 1)


def split(values):
    high = values.astype(BF16).astype(F32)
    return high, values - high


def flow_kernel(
    levels,
    in_weight, cond_weight, res_weight, skip_weight, audio, mel, inv_weight, local_small, end_bias,
    total, weights_out, ext_out, acts_out, frames_out, mel_out, sums_out, inverse_out, log_out, small, end_out,
    mine_out, end_own_out,
    shared, hid, ext, acts, top, bottom, wbuf, low, low_t, tap0, tap2, grad, mel_sum, edge_out, edge_in,
    fold, keep, og_rows, out, small_in, end_in, *rest,
):
    line = mesh_line(levels)
    n_bufs = len(line_shapes()) if line else len(levels)
    level_bufs = rest[:n_bufs]
    (
        own_sem, send, recv, keep_sem, ext_sem, acts_sem,
        top_send, top_recv, bottom_send, bottom_recv,
        small_send, small_recv, fold_send, fold_recv,
        phase, w_sem, core_send, core_recv, credit, far_send, far_recv,
        rs_send, rs_recv, ag_send, ag_recv, out_sem, edge_send, edge_recv,
        sum_send, sum_recv, end_send, end_recv, frames_send, frames_recv, mel_send, mel_recv,
        lane_send, lane_recv, lane_credit, way_send, way_recv,
    ) = rest[n_bufs:]
    me = Place()
    core_dev = me.chan_device(me.core_shard)
    far_dev = me.chan_device(me.far_shard)
    diag_dev = me.chan_device(me.diag_shard)
    chan_devs = [core_dev, far_dev, diag_dev]
    has_prev = me.chan > 0
    has_next = me.chan < SHARDS - 1
    prev_dev = me.chan_device(jnp.maximum(me.chan - 1, 0))
    next_dev = me.chan_device(jnp.minimum(me.chan + 1, SHARDS - 1))

    quarter = ROWS // 2
    xb, zb = me.dp_bit(0), me.dp_bit(1)

    def quarter_at(x, z, first=0, rows=quarter):
        return pl.ds(pl.multiple_of((x * 2 + z) * quarter + first, 32), rows)

    half_quarter = quarter // 2

    def own_copies(l):
        dst = shared.at[l * SHARDS + me.chan]
        return [
            pltpu.make_async_copy(in_weight.at[l], dst.at[:, pl.ds(0, CONV)], own_sem.at[0, l]),
            pltpu.make_async_copy(cond_weight.at[l], dst.at[:, pl.ds(CONV, ROWS)], own_sem.at[1, l]),
        ]

    def res_copies(l):
        dst = shared.at[l * SHARDS + me.chan]
        return [
            pltpu.make_async_copy(
                res_weight.at[l, pl.ds(h * 2 * ROWS, 2 * ROWS)],
                dst.at[:, pl.ds(EXT + h * ROWS, ROWS)],
                own_sem.at[2 + h, l],
            )
            for h in range(2)
        ]

    def link(kind, l, shard, at, device):
        ref = shared.at[l * SHARDS + shard, at] if at is not None else shared.at[l * SHARDS + shard]
        return remote(ref, ref, send.at[kind, l], recv.at[kind, l], device)

    x_dev, z_dev = me.dp_device(0), me.dp_device(1)

    def far_a(l, shard):
        return link(0, l, shard, quarter_at(xb, zb), far_dev)

    def far_b(l, shard):
        return link(1, l, shard, quarter_at(1 - xb, 1 - zb, 0, half_quarter), far_dev)

    def x_a(l, x):
        return link(2, l, me.far_shard, quarter_at(x, zb), x_dev)

    def z_a(l, z):
        return link(3, l, me.far_shard, quarter_at(xb, z), z_dev)

    def x_b(l, x):
        return link(4, l, me.far_shard, quarter_at(x, 1 - zb, half_quarter, half_quarter), x_dev)

    def core_a(l, shard):
        return link(5, l, shard, None, core_dev)

    def core_b(l, shard):
        return link(6, l, shard, None, core_dev)

    def issue(l):
        for copy in own_copies(l):
            copy.wait()

        @pl.when(l < LAYERS - 1)
        def _():
            for copy in res_copies(l):
                copy.wait()

        far_a(l, me.chan).start()
        far_b(l, me.chan).start()
        core_a(l, me.chan).start()

    def relay_a(l):
        far_a(l, me.far_shard).wait_recv()
        x_a(l, xb).start()
        z_a(l, zb).start()

    def relay_b(l):
        z_a(l, 1 - zb).wait_recv()
        x_b(l, xb).start()

    def relay_c(l):
        far_b(l, me.far_shard).wait_recv()
        x_a(l, 1 - xb).wait_recv()
        x_b(l, 1 - xb).wait_recv()
        core_b(l, me.far_shard).start()

    def arrive(l):
        core_a(l, me.core_shard).wait_recv()
        core_b(l, me.diag_shard).wait_recv()

    shared[(LAYERS - 1) * SHARDS + me.chan, :, EXT:] = jnp.zeros((2 * ROWS, 2 * ROWS), BF16)

    def first_copies(l, carry):
        for copy in own_copies(l):
            copy.start()

        @pl.when(l < LAYERS - 1)
        def _():
            for copy in res_copies(l):
                copy.start()

        return carry

    lax.fori_loop(0, LAYERS, first_copies, 0)

    @pl.when(jnp.logical_not(has_prev))
    def _():
        top[...] = jnp.zeros_like(top)

    @pl.when(jnp.logical_not(has_next))
    def _():
        bottom[...] = jnp.zeros_like(bottom)

    edge_in[...] = jnp.zeros_like(edge_in)
    opp_dev = (6 + 2 * xb - me.dp, me.chan) if line else None
    greet(chan_devs + [me.dp_device(bit) for bit, _, _ in levels] + ([opp_dev] if line else []))

    def small_copy(k):
        return remote(local_small, small.at[me.chan], small_send.at[k], small_recv.at[k], chan_devs[k])

    def fold_copy(k):
        return remote(fold.at[me.chan], fold.at[me.chan], fold_send.at[k], fold_recv.at[k], chan_devs[k])

    issue(0)
    for k in range(3):
        small_copy(k).start()
    small[me.chan] = local_small[...]

    rows8 = lax.broadcasted_iota(jnp.int32, (CH, BLOCK), 0)
    mixed = jnp.zeros((CH, BLOCK), F32)
    for j in range(CH):
        mixed = mixed + inv_weight[:, j : j + 1] * audio[j : j + 1, :]
    first_ext = jnp.where(rows8 < HALF, mixed, jnp.where(rows8 == HALF, 1.0, 0.0))
    keep[0] = mixed
    keep[1] = first_ext
    for r in range(BLOCK // HOP):
        row = jnp.broadcast_to(mel[r : r + 1, :], (HOP, ROWS)).astype(BF16)
        for slot in range(2):
            ext[slot, pl.ds(r * HOP, HOP), CONV:] = row
    out[...] = jnp.zeros_like(out)
    for k in range(3):
        small_copy(k).wait_recv()

    def small_row(lo, hi):
        return jnp.concatenate([small[s, lo:hi, :] for s in range(SHARDS)], axis=1)

    start_ext = jnp.where(rows8 <= HALF, small_row(0, 8), 0.0)
    keep[2] = start_ext
    hid[pl.ds(PAD, BLOCK), :] = lax.dot_general(
        first_ext, start_ext, (((0,), (0,)), ((), ())), precision=HIGH, preferred_element_type=F32
    )
    relay_a(0)
    issue(1)
    final = small_row(16, 24)
    final_high, final_low = split(final)
    final_rows = jnp.concatenate([final_high, final_low], axis=0).astype(BF16)
    for l in range(LAYERS):
        both = dot(final_rows, skip_weight[l])
        high, rest_of = split(both[:CH] + both[CH:])
        fold[me.chan, l] = jnp.concatenate([high, rest_of, high, jnp.zeros_like(high)], axis=0).astype(BF16)
    for k in range(3):
        fold_copy(k).start()
    skip_bias = small_row(13, 14)
    const = jnp.sum(final * skip_bias, axis=1, keepdims=True) + end_bias[...]

    relay_b(0)
    aug = jnp.concatenate(
        [
            inv_weight[...],
            jnp.where(
                lax.broadcasted_iota(jnp.int32, (CH, CH), 0) == lax.broadcasted_iota(jnp.int32, (CH, CH), 1), 1.0, 0.0
            ),
        ],
        axis=1,
    )
    aug_rows = lax.broadcasted_iota(jnp.int32, (CH, 2 * CH), 0)
    log_total = jnp.zeros((1, 1), F32)
    for c in range(CH):
        pivot = aug[c : c + 1, c : c + 1]
        log_total = log_total + jnp.log(pivot)
        pivot_row = aug[c : c + 1, :] / pivot
        aug = jnp.where(aug_rows == c, pivot_row, aug - aug[:, c : c + 1] * pivot_row)
    inverse_out[...] = aug
    log_out[...] = jnp.broadcast_to(log_total, log_out.shape)
    relay_a(1)
    issue(2)
    relay_c(0)
    relay_b(1)

    def ext_copy(l):
        return pltpu.make_async_copy(ext.at[l % 2], ext_out.at[l], ext_sem.at[l % 2])

    def acts_copy(l):
        return pltpu.make_async_copy(acts.at[l % 2], acts_out.at[l], acts_sem.at[l % 2])

    def keep_copy(l):
        return pltpu.make_async_copy(
            shared.at[pl.ds(l * SHARDS, SHARDS)], weights_out.at[l], keep_sem.at[l]
        )

    def to_next(l, rows):
        p = l % 2
        return remote(
            ext.at[p, pl.ds(BLOCK - rows, rows), pl.ds(WIDTH, WIDTH)],
            top.at[p, pl.ds(EDGE - rows, rows)],
            top_send.at[p], top_recv.at[p], next_dev,
        )

    def to_prev(l, rows):
        p = l % 2
        return remote(
            ext.at[p, pl.ds(0, rows), pl.ds(WIDTH, WIDTH)],
            bottom.at[p, pl.ds(0, rows)],
            bottom_send.at[p], bottom_recv.at[p], prev_dev,
        )

    def by_edge(l, f):
        pl.when(l <= 4)(lambda: f(PAD))
        pl.when(l > 4)(lambda: f(EDGE))

    def forward(l, carry):
        p = l % 2
        pl.when(l + 2 < LAYERS)(lambda: relay_a(l + 2))
        arrive(l)
        pl.when(l < LAYERS - 1)(lambda: keep_copy(l).start())

        @pl.when(l >= 2)
        def _():
            ext_copy(l - 2).wait()
            acts_copy(l - 2).wait()

        spilled = l < LAYERS - 2
        ext[p, :, WIDTH : 2 * WIDTH] = hid[pl.ds(PAD, BLOCK), :].astype(BF16)

        def start(rows):
            pl.when(has_next)(lambda: to_next(l, rows).start())
            pl.when(has_prev)(lambda: to_prev(l, rows).start())

        def finish(rows):
            @pl.when(has_next)
            def _():
                to_next(l, rows).wait_send()
                to_prev(l, rows).wait_recv()

            @pl.when(has_prev)
            def _():
                to_prev(l, rows).wait_send()
                to_next(l, rows).wait_recv()

        by_edge(l, start)
        pl.when(l + 3 < LAYERS)(lambda: issue(l + 3))
        by_edge(l, finish)
        hid[pl.ds(0, PAD), :] = top[p, pl.ds(EDGE - PAD, PAD), :].astype(F32)
        hid[pl.ds(PAD + BLOCK, PAD), :] = bottom[p, pl.ds(0, PAD), :].astype(F32)
        for layer in range(LAYERS):
            d = 2**layer

            @pl.when(l == layer)
            def _():
                if d < PAD:
                    ext[p, :, :WIDTH] = hid[pl.ds(PAD - d, BLOCK), :].astype(BF16)
                    ext[p, :, 2 * WIDTH : CONV] = hid[pl.ds(PAD + d, BLOCK), :].astype(BF16)
                else:
                    ext[p, :d, :WIDTH] = top[p, EDGE - d :, :]
                    ext[p, d:, :WIDTH] = ext[p, : BLOCK - d, WIDTH : 2 * WIDTH]
                    ext[p, BLOCK - d :, 2 * WIDTH : CONV] = bottom[p, :d, :]
                    ext[p, : BLOCK - d, 2 * WIDTH : CONV] = ext[p, d:, WIDTH : 2 * WIDTH]

        pl.when(spilled)(lambda: ext_copy(l).start())

        def one(s, carry):
            pre = dot_nt(ext[p], shared[l * SHARDS + s, :, :EXT])
            t = jnp.tanh(pre[:, :ROWS])
            g = 0.5 * jnp.tanh(0.5 * pre[:, ROWS:]) + 0.5
            tg = t * g
            acts[p, s, 0] = tg.astype(BF16)
            acts[p, s, 1] = (g - t * tg).astype(BF16)
            acts[p, s, 2] = (tg * (1.0 - g)).astype(BF16)
            return carry

        lax.fori_loop(0, SHARDS, one, 0)
        pl.when(spilled)(lambda: acts_copy(l).start())

        @pl.when(l == 0)
        def _():
            for k in range(3):
                fold_copy(k).wait_recv()

        gated = jnp.concatenate([acts[p, s, 0] for s in range(SHARDS)], axis=1)
        out[...] += dot_nt(jnp.concatenate([fold[s, l, : 2 * CH, :] for s in range(SHARDS)], axis=1), gated)

        @pl.when(l < LAYERS - 1)
        def _():
            for h in range(2):
                res = jnp.concatenate(
                    [shared[l * SHARDS + s, :, EXT + h * ROWS : EXT + (h + 1) * ROWS] for s in range(SHARDS)], axis=1
                )
                bias = jnp.concatenate([small[s, pl.ds(5 + l, 1), :] for s in (2 * h, 2 * h + 1)], axis=1)
                cols = slice(h * 2 * ROWS, (h + 1) * 2 * ROWS)
                hid[pl.ds(PAD, BLOCK), cols] += dot_nt(gated, res) + bias

        pl.when(l + 1 < LAYERS)(lambda: relay_c(l + 1))
        pl.when(l + 2 < LAYERS)(lambda: relay_b(l + 2))
        return carry

    lax.fori_loop(0, LAYERS, forward, 0)

    both = out[...]
    output = both[:CH] + both[CH:] + const
    log_scale, shift = output[:HALF], output[HALF:]
    scale = jnp.exp(log_scale)
    mixed = keep[0]
    second = mixed[HALF:]
    second_out = scale * second + shift
    mine = pl.ds(pl.multiple_of(me.chan * BLOCK, BLOCK), BLOCK)
    frames_out[0:CH, mine] = jnp.concatenate([mixed[:HALF], second_out], axis=0)
    frames_out[2 * CH : 3 * CH, mine] = jnp.concatenate([log_scale, jnp.zeros_like(log_scale)], axis=0)
    out_grad = jnp.concatenate([second_out * scale * second - 1.0, second_out], axis=0)
    keep[3] = jnp.concatenate([jnp.zeros_like(scale), second_out * scale], axis=0)
    og_high, og_low = split(out_grad)
    og_rows[...] = jnp.concatenate([og_high, og_low], axis=0).astype(BF16)
    og_stack = jnp.concatenate([og_high, og_high, og_low, jnp.zeros((ROWS - 3 * CH, BLOCK), F32)], axis=0)
    low[:, WIDTH:] = og_stack.T.astype(BF16)
    end_sum = jnp.sum(out_grad, axis=1, keepdims=True)
    grad[...] = jnp.zeros_like(grad)
    mel_sum[...] = jnp.zeros_like(mel_sum)

    def drain_forward(l, carry):
        far_a(l, me.chan).wait_send()
        far_b(l, me.chan).wait_send()
        x_a(l, xb).wait_send()
        z_a(l, zb).wait_send()
        x_b(l, xb).wait_send()
        core_a(l, me.chan).wait_send()
        core_b(l, me.far_shard).wait_send()
        pl.when(l < LAYERS - 1)(lambda: keep_copy(l).wait())
        return carry

    lax.fori_loop(0, LAYERS, drain_forward, 0)
    for k in range(3):
        small_copy(k).wait_send()
        fold_copy(k).wait_send()
    pl.semaphore_signal(phase.at[0], inc=1, device_id=core_dev, device_id_type=MESH)
    pl.semaphore_signal(phase.at[1], inc=1, device_id=far_dev, device_id_type=MESH)

    def side_of(j):
        return jnp.where(j < 2, 1 - me.side, me.side)

    def shard_of(j):
        return side_of(j) * 2 + jnp.where(j % 2 == 0, 1 - me.core, me.core)

    def w_copy(q):
        l, s = LAYERS - 1 - q // SHARDS, shard_of(q % SHARDS)
        return pltpu.make_async_copy(weights_out.at[l, s], wbuf.at[q % 2], w_sem.at[q % 2])

    def w_start(q):
        s = shard_of(q % SHARDS)
        here = pltpu.make_async_copy(shared.at[(LAYERS - 1) * SHARDS + s], wbuf.at[q % 2], w_sem.at[q % 2])
        pl.when(q < SHARDS)(lambda: here.start())
        pl.when(q >= SHARDS)(lambda: w_copy(q).start())

    def ext_back(l):
        return pltpu.make_async_copy(ext_out.at[l], ext.at[l % 2], ext_sem.at[l % 2])

    def acts_back(l):
        return pltpu.make_async_copy(acts_out.at[l], acts.at[l % 2], acts_sem.at[l % 2])

    def kept(i, ys):
        return 4 + 2 * i + ys

    def got_core(i, ys):
        return 20 + 2 * (i % 2) + ys

    def to_core(i, ys):
        p = i % 2
        return remote(
            shared.at[2 * p + ys], shared.at[got_core(i, ys)], core_send.at[p, ys], core_recv.at[p, ys], core_dev
        )

    def to_far(i):
        return remote(shared.at[kept(i, 1 - me.side)], shared.at[24 + i], far_send.at[i], far_recv.at[i], far_dev)

    def add_rows(block, base, rows, src, src_at):
        chunk = min(rows, 32)

        def body(k, carry):
            at = pl.ds(pl.multiple_of(base + k * chunk, PAD), chunk)
            shared[block, at, :] = shared[block, at, :] + src[src_at, pl.ds(pl.multiple_of(k * chunk, PAD), chunk), :]
            return carry

        lax.fori_loop(0, rows // chunk, body, 0)

    base_at = [0]
    for bit, rows, after in levels:
        base_at.append(base_at[-1] + (me.dp_bit(bit) * after if after < rows else 0))

    def rs(k, i):
        bit, rows, after = levels[k]
        first = base_at[k] + ((1 - me.dp_bit(bit)) * after if after < rows else 0)
        at = pl.ds(pl.multiple_of(first, PAD), after)
        return remote(
            shared.at[kept(i, me.side), at], level_bufs[k].at[i], rs_send.at[k, i], rs_recv.at[k, i], me.dp_device(bit)
        )

    def ag(k, i, arriving):
        bit, rows, after = levels[k]
        first = base_at[k] + (1 - me.dp_bit(bit)) * after if arriving else base_at[k + 1]
        ref = total.at[LAYERS - 1 - i, pl.ds(pl.multiple_of(first, PAD), after)]
        return remote(ref, ref, ag_send.at[k, i], ag_recv.at[k, i], me.dp_device(bit))

    halving = [k for k, (bit, rows, after) in enumerate(levels) if after < rows]

    def out_copy(i):
        at = pl.ds(pl.multiple_of(base_at[-1], PAD), levels[-1][2])
        return pltpu.make_async_copy(shared.at[kept(i, me.side), at], total.at[LAYERS - 1 - i, at], out_sem.at[0, i])

    def core_block(i, ys):
        to_core(i, ys).wait_recv()
        add_rows(kept(i, ys), 0, 2 * ROWS, shared, got_core(i, ys))
        pl.semaphore_signal(credit.at[ys], inc=1, device_id=core_dev, device_id_type=MESH)

    def far_block(i):
        core_block(i, 1 - me.side)
        pl.when(i == 0)(lambda: pl.semaphore_wait(phase.at[1], 1))
        if not line:
            to_far(i).start()

    def stage_far(i):
        to_far(i).wait_recv()
        add_rows(kept(i, me.side), 0, 2 * ROWS, shared, 24 + i)
        rs(0, i).start()

    def stage_rs(k, i):
        bit, rows, after = levels[k]
        rs(k, i).wait_recv()
        if after == rows:
            rs(k, i).wait_send()
        add_rows(kept(i, me.side), base_at[k + 1], after, level_bufs[k], i)
        if k + 1 < len(levels):
            rs(k + 1, i).start()
        else:
            out_copy(i).start()
            out_copy(i).wait()
            ag(halving[-1], i, False).start()

    def stage_ag(n, i):
        ag(halving[n], i, True).wait_recv()
        if n > 0:
            ag(halving[n - 1], i, False).start()

    def add_block(block, base, rows, cols, src, src_base=0):
        chunk = min(rows, 64)

        def body(k, carry):
            at = pl.ds(pl.multiple_of(base + k * chunk, 32), chunk)
            got = src[pl.ds(pl.multiple_of(src_base + k * chunk, 32), chunk), :]
            shared[block, at, cols] = shared[block, at, cols] + got
            return carry

        lax.fori_loop(0, rows // chunk, body, 0)

    def rows_at(first, rows):
        return pl.ds(pl.multiple_of(first, 32), rows)

    if line:
        zc = me.dp // 2
        inner = (zc == 1) | (zc == 2)
        edge = jnp.logical_not(inner)
        hb = jnp.where(zc == 2, 1, 0)
        lane_devs = [x_dev, z_dev, opp_dev, z_dev, opp_dev, x_dev]
        lanes = [
            Lane(level_bufs[k], lane_send.at[k], lane_recv.at[k], lane_credit.at[k], lane_devs[k]) for k in range(6)
        ]
        qx, q1, q2, r1, r2, rx = lanes
        wide, half, small_half = ROWS, ROWS // 2, ROWS // 4

        def q_rows(u, x):
            return x * wide + u % 2 * half

        def r_rows(u):
            return u % 2 * wide

        def far_way(k, u, rows, cols):
            i = u // 2
            return remote(
                shared.at[kept(i, 1 - me.side), rows, cols], shared.at[24 + i, rows, cols],
                way_send.at[k, u], way_recv.at[k, u], far_dev,
            )

        def far_q(u):
            return far_way(0, u, rows_at(q_rows(u, xb), half), ACROSS)

        def far_r(u):
            return far_way(1, u, rows_at(r_rows(u), wide), ALONG)

        def own_ref(u, first, rows, cols):
            return shared.at[kept(u // 2, me.side), rows_at(first, rows), cols]

        def total_ref(u, first, rows, cols):
            return total.at[LAYERS - 1 - u // 2, rows_at(first, rows), cols]

        def way(k, u, src, dst, device):
            return remote(src, dst, way_send.at[k, u], way_recv.at[k, u], device)

        def q_inner(u, b):
            at = (u, q_rows(u, xb) + b * small_half, small_half, ACROSS)
            return way(2, u, own_ref(*at), total_ref(*at), opp_dev)

        def q_edge(u):
            ref = total_ref(u, q_rows(u, xb), half, ACROSS)
            return way(3, u, ref, ref, z_dev)

        def q_x(u, x):
            ref = total_ref(u, q_rows(u, x), half, ACROSS)
            return way(4, u, ref, ref, x_dev)

        def r_x(u, x):
            at = (u, r_rows(u) + hb * half + x * small_half, small_half, ALONG)
            return way(5, u, own_ref(*at), total_ref(*at), x_dev)

        def r_inner(u, b):
            ref = total_ref(u, r_rows(u) + b * half, half, ALONG)
            return way(6, u, ref, ref, opp_dev)

        def r_edge(u):
            ref = total_ref(u, r_rows(u), wide, ALONG)
            return way(7, u, ref, ref, z_dev)

        def q_out(u):
            at = (u, q_rows(u, xb) + hb * small_half, small_half, ACROSS)
            return pltpu.make_async_copy(own_ref(*at), total_ref(*at), out_sem.at[0, u])

        def r_out(u):
            at = (u, r_rows(u) + hb * half + xb * small_half, small_half, ALONG)
            return pltpu.make_async_copy(own_ref(*at), total_ref(*at), out_sem.at[1, u])

        def start_q(u):
            qx.start(u, shared.at[pl.ds(kept(u // 2, 0), 2), rows_at(q_rows(u, 1 - xb), half), ACROSS])

        def q_stage1(u):
            qx.wait(u)
            for ys in (1 - me.side, me.side):
                add_block(kept(u // 2, ys), q_rows(u, xb), half, ACROSS, qx.buf.at[u % DEPTH, ys])
                if ys is not me.side:
                    far_q(u).start()
            qx.free()

        def r_stage1(u):
            far_r(u).wait_recv()
            add_block(kept(u // 2, me.side), r_rows(u), wide, ALONG, shared.at[24 + u // 2, :, ALONG], r_rows(u))
            pl.when(edge)(lambda: r1.start(u, own_ref(u, r_rows(u), wide, ALONG)))

        def q_stage2(u):
            far_q(u).wait_recv()
            first = q_rows(u, xb)
            add_block(kept(u // 2, me.side), first, half, ACROSS, shared.at[24 + u // 2, :, ACROSS], first)
            pl.when(edge)(lambda: q1.start(u, own_ref(u, first, half, ACROSS)))

        def r_stage2(u):
            @pl.when(inner)
            def _():
                r1.wait(u)
                add_block(kept(u // 2, me.side), r_rows(u), wide, ALONG, r1.buf.at[u % DEPTH])
                r1.free()
                r2.start(u, own_ref(u, r_rows(u) + (1 - hb) * half, half, ALONG))

        def q_stage3(u):
            @pl.when(inner)
            def _():
                first = q_rows(u, xb)
                q1.wait(u)
                add_block(kept(u // 2, me.side), first, half, ACROSS, q1.buf.at[u % DEPTH])
                q1.free()
                q2.start(u, own_ref(u, first + (1 - hb) * small_half, small_half, ACROSS))

        def r_stage3(u):
            @pl.when(inner)
            def _():
                first = r_rows(u) + hb * half
                r2.wait(u)
                add_block(kept(u // 2, me.side), first, half, ALONG, r2.buf.at[u % DEPTH])
                r2.free()
                rx.start(u, own_ref(u, first + (1 - xb) * small_half, small_half, ALONG))

        def q_stage4(u):
            @pl.when(inner)
            def _():
                q2.wait(u)
                first = q_rows(u, xb) + hb * small_half
                add_block(kept(u // 2, me.side), first, small_half, ACROSS, q2.buf.at[u % DEPTH])
                q2.free()
                q_inner(u, hb).start()
                q_out(u).start()

        def r_stage4(u):
            @pl.when(inner)
            def _():
                rx.wait(u)
                first = r_rows(u) + hb * half + xb * small_half
                add_block(kept(u // 2, me.side), first, small_half, ALONG, rx.buf.at[u % DEPTH])
                rx.free()
                r_x(u, xb).start()
                r_out(u).start()

        def q_stage5(u):
            @pl.when(inner)
            def _():
                q_out(u).wait()
                q_inner(u, 1 - hb).wait_recv()
                q_edge(u).start()
                q_x(u, xb).start()

        def r_stage5(u):
            @pl.when(inner)
            def _():
                r_out(u).wait()
                r_x(u, 1 - xb).wait_recv()
                r_inner(u, hb).start()

        def q_stage6(u):
            @pl.when(edge)
            def _():
                q_edge(u).wait_recv()
                q_x(u, xb).start()

        def r_stage6(u):
            @pl.when(inner)
            def _():
                r_inner(u, 1 - hb).wait_recv()
                r_edge(u).start()

        def q_stage7(u):
            q_x(u, 1 - xb).wait_recv()

        def r_stage7(u):
            pl.when(edge)(lambda: r_edge(u).wait_recv())

        def drain_ways(u, carry):
            far_q(u).wait_send()
            far_r(u).wait_send()
            q_x(u, xb).wait_send()

            @pl.when(inner)
            def _():
                q_inner(u, hb).wait_send()
                q_edge(u).wait_send()
                r_x(u, xb).wait_send()
                r_inner(u, hb).wait_send()
                r_edge(u).wait_send()

            return carry

        def finish_lanes():
            qx.finish()

            @pl.when(edge)
            def _():
                q1.finish()
                r1.finish()

            @pl.when(inner)
            def _():
                q2.finish()
                r2.finish()
                rx.finish()

        line_stages = [
            [q_stage1, r_stage1], [q_stage2, r_stage2], [q_stage3, r_stage3], [q_stage4, r_stage4],
            [q_stage5, r_stage5], [q_stage6, r_stage6], [q_stage7, r_stage7],
        ]

    def back_prev(i, rows):
        return remote(
            edge_out.at[0, pl.ds(0, rows)], edge_in.at[i % 2, 0, pl.ds(0, rows)],
            edge_send.at[0], edge_recv.at[i % 2, 0], prev_dev,
        )

    def back_next(i, rows):
        return remote(
            edge_out.at[1, pl.ds(EDGE - rows, rows)], edge_in.at[i % 2, 1, pl.ds(EDGE - rows, rows)],
            edge_send.at[1], edge_recv.at[i % 2, 1], next_dev,
        )

    def back_edge(i, f):
        by_edge(LAYERS - 1 - i, f)

    def apply_edges(i):
        def finish(rows):
            @pl.when(has_next)
            def _():
                back_next(i, rows).wait_send()
                back_prev(i, rows).wait_recv()

            @pl.when(has_prev)
            def _():
                back_prev(i, rows).wait_send()
                back_next(i, rows).wait_recv()

        back_edge(i, finish)
        tap0[pl.ds(BLOCK, EDGE), :] = edge_in[i % 2, 0].astype(F32)
        tap2[pl.ds(0, EDGE), :] = edge_in[i % 2, 1].astype(F32)
        for layer in range(LAYERS):
            d = 2**layer

            @pl.when(LAYERS - 1 - i == layer)
            def _():
                grad[...] += tap0[pl.ds(d, BLOCK), :] + tap2[pl.ds(EDGE - d, BLOCK), :]

    def backward_open(i):
        l = LAYERS - 1 - i
        pl.when(i > 0)(lambda: apply_edges(i - 1))
        now = grad[...].astype(BF16)
        low[:, :WIDTH] = now
        low_t[...] = now.T
        sums_out[pl.ds(72 + l, 1), :] = jnp.sum(now.astype(F32), axis=0, keepdims=True)
        tap0[pl.ds(0, BLOCK), :] = jnp.zeros((BLOCK, WIDTH), F32)
        tap2[pl.ds(EDGE, BLOCK), :] = jnp.zeros((BLOCK, WIDTH), F32)

        @pl.when(i >= 2)
        def _():
            ext_back(l).wait()
            acts_back(l).wait()

    def backward_shards(i, h):
        l = LAYERS - 1 - i
        p = l % 2

        def one(k, carry):
            j = 2 * h + k
            q = i * SHARDS + j
            b = q % 2
            s = shard_of(j)
            pl.when(q + 1 < LAYERS * SHARDS)(lambda: w_start(q + 1))

            @pl.when((j % 2 == 0) & (i >= 2))
            def _():
                to_core(i - 2, side_of(j)).wait_send()

            w_copy(q).wait()
            slot = jnp.where(j % 2 == 0, 2 * (i % 2) + side_of(j), kept(i, side_of(j)))
            gated = acts[p, s, 0]
            res = jnp.concatenate(
                [
                    wbuf[b, :, EXT : EXT + ROWS],
                    wbuf[b, :, EXT + ROWS :],
                    fold[s, l],
                    jnp.zeros((ROWS - 4 * CH, ROWS), BF16),
                ],
                axis=0,
            )
            back = dot(low[...], res)
            pg = jnp.concatenate(
                [(back * acts[p, s, 1].astype(F32)).astype(BF16), (back * acts[p, s, 2].astype(F32)).astype(BF16)],
                axis=1,
            )
            pg_t = pg.T
            tap0[pl.ds(0, BLOCK), :] += dot(pg, wbuf[b, :, :WIDTH])
            grad[...] += dot(pg, wbuf[b, :, WIDTH : 2 * WIDTH])
            last_tap = dot(pg, wbuf[b, :, 2 * WIDTH : EXT])
            tap2[pl.ds(EDGE, BLOCK), :] += last_tap[:, :WIDTH]
            mel_sum[...] += last_tap[:, WIDTH:]
            for cols in (slice(0, 6 * ROWS), slice(6 * ROWS, EXT)):
                shared[slot, :, cols] = dot(pg_t, ext[p, :, cols]).astype(BF16)
            side = dot(low_t[...], gated).astype(BF16)
            shared[slot, :, EXT : EXT + ROWS] = side[: 2 * ROWS]
            shared[slot, :, EXT + ROWS :] = side[2 * ROWS :]
            e = dot(og_rows[...], gated)
            sums_out[pl.ds(pl.multiple_of(l * CH, CH), CH), pl.ds(pl.multiple_of(s * ROWS, ROWS), ROWS)] = e[:CH] + e[CH:]

            @pl.when(j % 2 == 0)
            def _():
                pl.when(q == 0)(lambda: pl.semaphore_wait(phase.at[0], 1))
                pl.when(i >= 2)(lambda: pl.semaphore_wait(credit.at[side_of(j)], 1))
                to_core(i, side_of(j)).start()

            return carry

        lax.fori_loop(0, 2, one, 0)

    def backward_close(i):
        l = LAYERS - 1 - i

        @pl.when(l >= 2)
        def _():
            ext_back(l - 2).start()
            acts_back(l - 2).start()

        edge_out[0] = tap0[pl.ds(0, EDGE), :].astype(BF16)
        edge_out[1] = tap2[pl.ds(BLOCK, EDGE), :].astype(BF16)

        def start(rows):
            pl.when(has_next)(lambda: back_next(i, rows).start())
            pl.when(has_prev)(lambda: back_prev(i, rows).start())

        back_edge(i, start)

    sum_devs = [core_dev, far_dev] + [me.dp_device(bit) for bit, _, _ in levels]

    def sum_copy(k):
        return remote(sums_out, small_in.at[k], sum_send.at[k], sum_recv.at[k], sum_devs[k])

    def end_copy(k):
        return remote(end_out, end_in.at[k], end_send.at[k], end_recv.at[k], sum_devs[k])

    def frames_copy(k):
        ref = frames_out.at[:, mine]
        return remote(ref, ref, frames_send.at[k], frames_recv.at[k], chan_devs[k])

    mel_rows = BLOCK // HOP

    def mel_copy(k):
        ref = mel_out.at[pl.ds(pl.multiple_of(me.chan * mel_rows, mel_rows), mel_rows)]
        return remote(ref, ref, mel_send.at[k], mel_recv.at[k], chan_devs[k])

    def last(values, other, dims):
        return lax.dot_general(values, other, (dims, ((), ())), precision=HIGH, preferred_element_type=F32)

    def finish_frames():
        apply_edges(LAYERS - 1)
        hidden_grad = grad[...]
        sums_out[64:72, :] = last(keep[1], hidden_grad, ((1,), (0,)))
        mixed = keep[0]
        first_back = last(keep[2], hidden_grad, ((1,), (1,)))
        rows = lax.broadcasted_iota(jnp.int32, (CH, BLOCK), 0)
        mixed_grad = jnp.where(rows < HALF, mixed + first_back, keep[3])
        frames_out[CH : 2 * CH, mine] = last(inv_weight[...], mixed_grad, ((0,), (0,)))
        inv_part = last(mixed_grad, audio[...], ((1,), (1,)))
        sums_out[80:88, :] = jnp.concatenate([inv_part, end_sum, jnp.zeros((CH, WIDTH - CH - 1), F32)], axis=1)
        mel_out[pl.ds(pl.multiple_of(me.chan * mel_rows, mel_rows), mel_rows), :] = jnp.sum(
            mel_sum[...].reshape(mel_rows, HOP, ROWS), axis=1
        )
        for k in range(3):
            frames_copy(k).start()
            mel_copy(k).start()
        sum_copy(0).start()

    def sum_stage(k):
        sum_copy(k).wait_recv()
        sum_copy(k).wait_send()
        sums_out[...] = sums_out[...] + small_in[k]
        if k + 1 < len(sum_devs):
            sum_copy(k + 1).start()
            return
        e = sums_out[0:64, pl.ds(pl.multiple_of(me.chan * ROWS, ROWS), ROWS)]
        e_high, e_low = split(e)
        end = jnp.zeros((2 * CH, WIDTH), F32)
        for l in range(LAYERS):
            part = slice(l * CH, (l + 1) * CH)
            end = end + dot_nt(jnp.concatenate([e_high[part], e_low[part]], axis=0).astype(BF16), skip_weight[l])
        end_out[...] = end[:CH] + end[CH:]
        end_copy(0).start()

    def end_stage(k):
        end_copy(k).wait_recv()
        end_copy(k).wait_send()
        end_out[...] = end_out[...] + end_in[k]
        if k == 0:
            end_copy(1).start()

    small_stages = [finish_frames]
    small_stages += [functools.partial(sum_stage, k) for k in range(len(sum_devs))]
    small_stages += [functools.partial(end_stage, k) for k in range(2)]

    if line:
        stages = [[]] + line_stages
    else:
        stages = [[], [stage_far]]
        stages += [[functools.partial(stage_rs, k)] for k in range(len(levels))]
        stages += [[functools.partial(stage_ag, n)] for n in range(len(halving) - 1, -1, -1)]
    if line:
        steps = 2 * LAYERS + max(ACROSS_LAGS[-1] + 2, ALONG_LAGS[-1] + 1, len(small_stages))
    else:
        steps = 2 * LAYERS + max(2 * len(stages), len(small_stages))

    w_start(0)

    def step(v, carry):
        i, h = v // 2, v % 2

        @pl.when(v < 2 * LAYERS)
        def _():
            pl.when(h == 0)(lambda: backward_open(i))
            backward_shards(i, h)

            @pl.when(h == 1)
            def _():
                backward_close(i)

        core_from = v - 1
        pl.when((core_from >= 0) & (core_from < 2 * LAYERS) & (h == 1))(lambda: far_block(core_from // 2))
        pl.when((core_from >= 0) & (core_from < 2 * LAYERS) & (h == 0))(lambda: core_block(core_from // 2, me.side))

        if line:
            pl.when((v >= 1) & (v <= 2 * LAYERS))(lambda: far_r(v - 1).start())
            pl.when((v >= 2) & (v <= 2 * LAYERS + 1))(lambda: start_q(v - 2))
        def at_lag(at, count, stage, now=True):
            pl.when((at >= 0) & (at < count) & now)(lambda: stage(at))

        if line:
            for name in ORDER.split():
                k = int(name[1])
                if name[0] == "q":
                    at_lag(v - 2 - ACROSS_LAGS[k], 2 * LAYERS, stages[k][0])
                else:
                    at_lag(v - 1 - ALONG_LAGS[k], 2 * LAYERS, stages[k][1])
        else:
            for lag in range(len(stages) - 1, 0, -1):
                at_lag((v - 2) // 2 - lag + 1, LAYERS, stages[lag][0], (h == 0) & (v >= 2))

        for k, stage in enumerate(small_stages):
            pl.when(v == 2 * LAYERS + k)(stage)
        return carry

    lax.fori_loop(0, steps, step, 0)

    for i in (LAYERS - 2, LAYERS - 1):
        for ys in range(2):
            to_core(i, ys).wait_send()
            pl.semaphore_wait(credit.at[ys], 1)

    def drain(i, carry):
        to_far(i).wait_send()
        for k, (bit, rows, after) in enumerate(levels):
            if after < rows:
                rs(k, i).wait_send()
                ag(k, i, False).wait_send()
        return carry

    if line:
        lax.fori_loop(0, 2 * LAYERS, drain_ways, 0)
        finish_lanes()
    else:
        lax.fori_loop(0, LAYERS, drain, 0)
    for k, shard in enumerate([me.core_shard, me.far_shard, me.diag_shard]):
        frames_copy(k).wait_send()
        mel_copy(k).wait_send()
        frames_copy(k).wait_recv()
        mel_copy(k).wait_recv()
    own_lanes = pl.ds(pl.multiple_of(me.chan * ROWS, ROWS), ROWS)
    mine_out[...] = sums_out[:, own_lanes]
    end_own_out[...] = end_out[:, own_lanes]


def run_flow(dp_size, *args):
    levels = levels_of(dp_size)
    vmem = pl.BlockSpec(memory_space=pltpu.VMEM)
    hbm = pl.BlockSpec(memory_space=pl.ANY)
    dma = pltpu.SemaphoreType.DMA
    regular = pltpu.SemaphoreType.REGULAR
    block = (2 * ROWS, PACK)
    n = len(levels)
    return pl.pallas_call(
        functools.partial(flow_kernel, levels),
        out_shape=(
            jax.ShapeDtypeStruct((LAYERS,) + block, BF16),
            jax.ShapeDtypeStruct((LAYERS, SHARDS) + block, BF16),
            jax.ShapeDtypeStruct((LAYERS, BLOCK, EXT), BF16),
            jax.ShapeDtypeStruct((LAYERS, SHARDS, 3, BLOCK, ROWS), BF16),
            jax.ShapeDtypeStruct((3 * CH, FRAMES), F32),
            jax.ShapeDtypeStruct((FRAMES // HOP, ROWS), F32),
            jax.ShapeDtypeStruct((88, WIDTH), F32),
            jax.ShapeDtypeStruct((CH, 2 * CH), F32),
            jax.ShapeDtypeStruct((CH, ROWS), F32),
            jax.ShapeDtypeStruct((SHARDS, 24, ROWS), F32),
            jax.ShapeDtypeStruct((CH, WIDTH), F32),
            jax.ShapeDtypeStruct((88, ROWS), F32),
            jax.ShapeDtypeStruct((CH, ROWS), F32),
        ),
        in_specs=[hbm] * 3 + [vmem] * 6,
        out_specs=tuple([hbm] * 4 + [vmem] * 9),
        scratch_shapes=[
            pltpu.VMEM((LAYERS * SHARDS,) + block, BF16),
            pltpu.VMEM((PAD + BLOCK + PAD, WIDTH), F32),
            pltpu.VMEM((2, BLOCK, EXT), BF16),
            pltpu.VMEM((2, SHARDS, 3, BLOCK, ROWS), BF16),
            pltpu.VMEM((2, EDGE, WIDTH), BF16),
            pltpu.VMEM((2, EDGE, WIDTH), BF16),
            pltpu.VMEM((2,) + block, BF16),
            pltpu.VMEM((BLOCK, WIDTH + ROWS), BF16),
            pltpu.VMEM((WIDTH, BLOCK), BF16),
            pltpu.VMEM((BLOCK + EDGE, WIDTH), F32),
            pltpu.VMEM((EDGE + BLOCK, WIDTH), F32),
            pltpu.VMEM((BLOCK, WIDTH), F32),
            pltpu.VMEM((BLOCK, ROWS), F32),
            pltpu.VMEM((2, EDGE, WIDTH), BF16),
            pltpu.VMEM((2, 2, EDGE, WIDTH), BF16),
            pltpu.VMEM((SHARDS, LAYERS, 4 * CH, ROWS), BF16),
            pltpu.VMEM((4, CH, BLOCK), F32),
            pltpu.VMEM((2 * CH, BLOCK), BF16),
            pltpu.VMEM((2 * CH, BLOCK), F32),
            pltpu.VMEM((n + 2, 88, WIDTH), F32),
            pltpu.VMEM((2, CH, WIDTH), F32),
        ]
        + (
            [pltpu.VMEM((DEPTH,) + shape, BF16) for shape in line_shapes()]
            if mesh_line(levels)
            else [pltpu.VMEM((LAYERS, after, PACK), BF16) for _, _, after in levels]
        )
        + [
            dma((4, LAYERS)), dma((7, LAYERS)), dma((7, LAYERS)), dma((LAYERS,)), dma((2,)), dma((2,)),
            dma((2,)), dma((2,)), dma((2,)), dma((2,)),
            dma((3,)), dma((3,)), dma((3,)), dma((3,)),
            regular((2,)), dma((2,)), dma((2, 2)), dma((2, 2)), regular((2,)), dma((LAYERS,)), dma((LAYERS,)),
            dma((n, LAYERS)), dma((n, LAYERS)), dma((n, LAYERS)), dma((n, LAYERS)), dma((2, 2 * LAYERS)),
            dma((2,)), dma((2, 2)),
            dma((n + 2,)), dma((n + 2,)), dma((2,)), dma((2,)), dma((3,)), dma((3,)), dma((3,)), dma((3,)),
            dma((6, DEPTH)), dma((6, DEPTH)), regular((6,)), dma((8, 2 * LAYERS)), dma((8, 2 * LAYERS)),
        ],
        compiler_params=pltpu.CompilerParams(
            collective_id=0, has_side_effects=True, vmem_limit_bytes=VMEM_LIMIT
        ),
    )(*args)


def prepare_kernel(
    offset, clip, mel_frames, cond_weight, in_bias, start_weight, start_bias, res_bias, skip_bias, final, end_bias,
    audio, mel, cond_ext, local_small, end_column,
):
    chan = lax.axis_index("chan")
    first = offset[0] * HOP + chan * BLOCK
    length = clip.shape[2]
    audio[...] = pltpu.roll(clip[0], lax.rem(length - first, length), 1)[:, :BLOCK]
    mel_rows = BLOCK // HOP
    clip_rows = mel_frames.shape[1]
    frames = jnp.concatenate([mel_frames[0].astype(F32), jnp.ones((clip_rows, ROWS - MEL), F32)], axis=1)
    frames = pltpu.roll(frames, lax.rem(clip_rows - offset[0] - chan * mel_rows, clip_rows), 0)[:mel_rows]
    lane = lax.broadcasted_iota(jnp.int32, (mel_rows, ROWS), 1)
    mel[...] = jnp.where(lane < MEL + 2, frames, 0.0)
    for l in range(LAYERS):
        high, rest = split(in_bias[l])
        for g in range(2):
            part = jnp.concatenate(
                [
                    cond_weight[l, g].astype(F32),
                    high[g : g + 1],
                    rest[g : g + 1],
                    jnp.zeros((ROWS - MEL - 2, ROWS), F32),
                ],
                axis=0,
            )
            cond_ext[l, g * ROWS : (g + 1) * ROWS, :] = part.T.astype(BF16)
    local_small[...] = jnp.concatenate(
        [
            start_weight[...],
            start_bias[...],
            res_bias[...],
            jnp.zeros((1, ROWS), F32),
            skip_bias[...],
            jnp.zeros((2, ROWS), F32),
            final[...],
        ],
        axis=0,
    )
    row = jnp.concatenate([end_bias[...], jnp.zeros((1, ROWS - CH), F32)], axis=1)
    end_column[...] = jnp.broadcast_to(row, (ROWS, ROWS)).T[:CH, :1]


def run_prepare(*args):
    vmem = pl.BlockSpec(memory_space=pltpu.VMEM)
    return pl.pallas_call(
        prepare_kernel,
        out_shape=(
            jax.ShapeDtypeStruct((CH, BLOCK), F32),
            jax.ShapeDtypeStruct((BLOCK // HOP, ROWS), F32),
            jax.ShapeDtypeStruct((LAYERS, 2 * ROWS, ROWS), BF16),
            jax.ShapeDtypeStruct((24, ROWS), F32),
            jax.ShapeDtypeStruct((CH, 1), F32),
        ),
        in_specs=[pl.BlockSpec(memory_space=pltpu.SMEM)] + [vmem] * 10,
        out_specs=tuple([vmem] * 5),
    )(*args)


def finish_kernel(
    crops, total, sums, mine, small, frames, mel_in, inverse, log_abs, end_in, final_own, skip_bias,
    latent, log_det, loss, audio_grad, mel_grad, inv_grad, start_grad, start_bias_grad, cond_grad, in_grad,
    bias_grad, res_grad, res_bias_grad, skip_grad, skip_bias_grad, end_grad, end_bias_grad,
):
    l = pl.program_id(0)
    for g in range(2):
        rows = slice(g * ROWS, (g + 1) * ROWS)
        in_grad[0, g] = total[0, rows, :CONV].astype(F32)
        cond = total[0, rows, CONV:EXT].astype(F32)
        cond = cond.T
        cond_grad[0, g] = cond[:MEL]
        bias_grad[0, g : g + 1, :] = cond[MEL : MEL + 1]

    @pl.when(l < LAYERS - 1)
    def _():
        res_grad[0, : 2 * ROWS] = total[0, :, EXT : EXT + ROWS].astype(F32)
        res_grad[0, 2 * ROWS :] = total[0, :, EXT + ROWS :].astype(F32)

    final_high, final_low = split(jnp.concatenate([small[s, 16:24, :] for s in range(SHARDS)], axis=1))
    e_high, e_low = split(mine[pl.ds(pl.multiple_of(l * CH, CH), CH), :])
    skip_grad[0] = dot_tn(
        jnp.concatenate([final_high, final_high, final_low, jnp.zeros_like(final_low)], axis=0).astype(BF16),
        jnp.concatenate([e_high, e_low, e_high, jnp.zeros_like(e_low)], axis=0).astype(BF16),
    )

    @pl.when(l == 0)
    def _():
        z = frames[:CH]
        latent[0] = z
        audio_grad[0] = frames[CH : 2 * CH]
        mel_grad[0] = mel_in[:, :MEL]
        log_scale = frames[2 * CH : 2 * CH + HALF]
        det = jnp.sum(jnp.sum(log_scale, axis=1, keepdims=True), axis=0, keepdims=True) + FRAMES * log_abs[:1, :1]
        squares = jnp.sum(jnp.sum(z * z, axis=1, keepdims=True), axis=0, keepdims=True)
        log_det[...] = det
        loss[...] = (0.5 * squares - det) / (CH * FRAMES)
        tiny = sums[80:88, :ROWS]
        inv_grad[...] = tiny[:, :CH] - crops * FRAMES * inverse[:, CH:].T
        end_column = tiny[:, CH : CH + 1]
        end_bias_grad[...] = jnp.broadcast_to(end_column, (CH, ROWS)).T[:1, :]
        start_grad[...] = mine[64:68, :]
        start_bias_grad[...] = mine[68:69, :]
        res_bias_grad[...] = mine[72:79, :]
        skip_bias_grad[...] = jnp.sum(end_column * final_own[...], axis=0, keepdims=True)
        end_grad[...] = end_in[...] + end_column * skip_bias[...]


def run_finish(crops, total, *args):
    def whole(shape):
        return pl.BlockSpec(shape, lambda l: (0,) * len(shape))

    outs = [
        ((1, CH, FRAMES), None),
        ((1, 1), None),
        ((1, 1), None),
        ((1, CH, FRAMES), None),
        ((1, FRAMES // HOP, MEL), None),
        ((CH, CH), None),
        ((HALF, ROWS), None),
        ((1, ROWS), None),
        ((LAYERS, 2, MEL, ROWS), pl.BlockSpec((1, 2, MEL, ROWS), lambda l: (l, 0, 0, 0))),
        ((LAYERS, 2, ROWS, CONV), pl.BlockSpec((1, 2, ROWS, CONV), lambda l: (l, 0, 0, 0))),
        ((LAYERS, 2, ROWS), pl.BlockSpec((1, 2, ROWS), lambda l: (l, 0, 0))),
        (
            (LAYERS - 1, WIDTH, ROWS),
            pl.BlockSpec((1, WIDTH, ROWS), lambda l: (jnp.minimum(l, LAYERS - 2), 0, 0)),
        ),
        ((LAYERS - 1, ROWS), None),
        ((LAYERS, WIDTH, ROWS), pl.BlockSpec((1, WIDTH, ROWS), lambda l: (l, 0, 0))),
        ((1, ROWS), None),
        ((CH, ROWS), None),
        ((1, CH), None),
    ]
    return pl.pallas_call(
        functools.partial(finish_kernel, crops),
        grid=(LAYERS,),
        out_shape=tuple(jax.ShapeDtypeStruct(shape, F32) for shape, _ in outs),
        in_specs=[pl.BlockSpec((1, 2 * ROWS, PACK), lambda l: (l, 0, 0))] + [whole(a.shape) for a in args],
        out_specs=tuple(spec or whole(shape) for shape, spec in outs),
    )(total, *args)


def local(
    audio_clips,
    mel_frames,
    crop_offsets,
    inv_weight,
    initial_projection_weight,
    start_bias,
    cond_weight,
    in_weight,
    in_bias,
    res_weight,
    res_bias,
    skip_projection_weight,
    skip_output_bias,
    final_projection_weight,
    end_bias,
):
    skip_bias = skip_output_bias[None]
    audio, mel, cond_ext, local_small, end_column = run_prepare(
        crop_offsets,
        audio_clips,
        jnp.swapaxes(mel_frames, 1, 2),
        jnp.swapaxes(cond_weight, 2, 3),
        in_bias,
        initial_projection_weight.T,
        start_bias[None],
        res_bias,
        skip_bias,
        final_projection_weight,
        end_bias[None],
    )
    total, _, _, _, frames, mel_grad, sums, inverse, log_abs, small, _, mine, end_own = run_flow(
        lax.axis_size("dp"),
        in_weight.reshape(LAYERS, 2 * ROWS, CONV),
        cond_ext,
        res_weight,
        skip_projection_weight,
        audio,
        mel,
        inv_weight,
        local_small,
        end_column,
    )
    crops = lax.axis_size("dp") * audio_clips.shape[0]
    outs = list(
        run_finish(
            crops, total, sums, mine, small, frames, mel_grad, inverse, log_abs, end_own,
            final_projection_weight, skip_bias,
        )
    )
    for k, shape in ((1, (1,)), (2, (1,)), (7, (ROWS,)), (14, (ROWS,)), (16, (CH,))):
        outs[k] = outs[k].reshape(shape)
    outs[4] = jnp.swapaxes(outs[4], 1, 2)
    outs[6] = outs[6].T
    outs[8] = jnp.swapaxes(outs[8], 2, 3)
    return tuple(outs)


def solution(mesh):
    in_specs = (
        P("dp", None, None),
        P("dp", None, None),
        P("dp"),
        P(),
        P("chan", None),
        P("chan"),
        P(None, None, "chan", None),
        P(None, None, "chan", None),
        P(None, None, "chan"),
        P(None, None, "chan"),
        P(None, "chan"),
        P(None, None, "chan"),
        P("chan"),
        P(None, "chan"),
        P(),
    )
    out_specs = (
        P("dp", None, None),
        P("dp"),
        P("dp"),
        P("dp", None, None),
        P("dp", None, None),
        P(),
        P("chan", None),
        P("chan"),
        P(None, None, "chan", None),
        P(None, None, "chan", None),
        P(None, None, "chan"),
        P(None, None, "chan"),
        P(None, "chan"),
        P(None, None, "chan"),
        P("chan"),
        P(None, "chan"),
        P(),
    )
    return jax.shard_map(local, mesh=mesh, in_specs=in_specs, out_specs=out_specs, check_vma=False)
```

```python
import functools

import jax
import jax.numpy as jnp
from jax import lax
from jax.experimental import pallas as pl
from jax.experimental.pallas import tpu as pltpu
from jax.sharding import PartitionSpec as P

CH = 8
HALF = 4
MEL = 80
LAYERS = 8
HOP = 32
FRAMES = 2048
WIDTH = 512
CONV = 1536
EXT = 1664
PACK = 1920
SHARDS = 4
ROWS = 128
BLOCK = FRAMES // SHARDS
PAD = 16
EDGE = 128

HIGH = lax.Precision.HIGHEST
F32 = jnp.float32
BF16 = jnp.bfloat16
MESH = pl.DeviceIdType.MESH
VMEM_LIMIT = 62 << 20


def dot(a, b):
    return jnp.dot(a, b, preferred_element_type=F32)


def dot_nt(a, b):
    return lax.dot_general(a, b, (((1,), (1,)), ((), ())), preferred_element_type=F32)


def dot_tn(a, b):
    return lax.dot_general(a, b, (((0,), (0,)), ((), ())), preferred_element_type=F32)


def when(cond):
    if cond is True:
        return lambda f: f()
    return pl.when(cond)


class Place:
    def __init__(self):
        self.dp = lax.axis_index("dp")
        self.chan = lax.axis_index("chan")
        self.core = self.chan % 2
        self.side = self.chan // 2
        self.bit = self.dp % 2

    def chan_device(self, chan):
        return (self.dp, chan)

    @property
    def core_shard(self):
        return self.side * 2 + 1 - self.core

    @property
    def far_shard(self):
        return (1 - self.side) * 2 + self.core

    @property
    def diag_shard(self):
        return (1 - self.side) * 2 + 1 - self.core

    def dp_bit(self, k):
        return (self.dp // 2**k) % 2

    def dp_device(self, k):
        return (self.dp + 2**k * (1 - 2 * self.dp_bit(k)), self.chan)


def greet(devices):
    barrier = pltpu.get_barrier_semaphore()
    for device in devices:
        pl.semaphore_signal(barrier, inc=1, device_id=device, device_id_type=MESH)
    pl.semaphore_wait(barrier, len(devices))


def remote(src, dst, send, recv, device):
    return pltpu.make_async_remote_copy(
        src_ref=src, dst_ref=dst, send_sem=send, recv_sem=recv, device_id=device, device_id_type=MESH
    )


def levels_of(dp_size):
    levels, rows, bit = [], 2 * ROWS, 0
    while 2**bit < dp_size:
        after = rows // 2 if rows > PAD else rows
        levels.append((bit, rows, after))
        rows, bit = after, bit + 1
    return levels


ACROSS = pl.ds(0, 6 * ROWS)
ALONG = pl.ds(6 * ROWS, PACK - 6 * ROWS)
DEPTH = 8
ACROSS_LAGS = (0, 1, 2, 3, 4, 5, 6, 20)
ALONG_LAGS = (0, 1, 2, 3, 4, 5, 6, 21)
ORDER = 'q5 r6 q4 r5 q2 q1 r1 r4 r7 q7 q6 r3 q3 r2'


def mesh_line(levels):
    return len(levels) == 3


def line_shapes():
    a, b = ACROSS.size, ALONG.size
    return [(2, ROWS // 2, a), (ROWS // 2, a), (ROWS // 4, a), (ROWS, b), (ROWS // 2, b), (ROWS // 4, b)]


class Lane:
    def __init__(self, buf, send, recv, credit, device):
        self.buf, self.send, self.recv, self.credit, self.device = buf, send, recv, credit, device

    def copy(self, i, src):
        d = i % DEPTH
        return remote(src, self.buf.at[d], self.send.at[d], self.recv.at[d], self.device)

    def start(self, i, src):
        @pl.when(i >= DEPTH)
        def _():
            self.copy(i, src).wait_send()
            pl.semaphore_wait(self.credit, 1)

        self.copy(i, src).start()

    def wait(self, i):
        d = i % DEPTH
        remote(self.buf.at[d], self.buf.at[d], self.send.at[d], self.recv.at[d], self.device).wait_recv()

    def free(self):
        pl.semaphore_signal(self.credit, inc=1, device_id=self.device, device_id_type=MESH)

    def finish(self):
        for d in range(DEPTH):
            ref = self.buf.at[d]
            remote(ref, ref, self.send.at[d], self.recv.at[d], self.device).wait_send()
            pl.semaphore_wait(self.credit, 1)


def split(values):
    high = values.astype(BF16).astype(F32)
    return high, values - high


def flow_kernel(
    levels,
    in_weight, cond_weight, res_weight, skip_weight, audio, mel, inv_weight, local_small, end_bias,
    total, weights_out, ext_out, acts_out, frames_out, mel_out, sums_out, inverse_out, log_out, small, end_out,
    mine_out, end_own_out,
    shared, hid, ext, acts, top, bottom, wbuf, low, low_t, tap0, tap2, grad, mel_sum, edge_out, edge_in,
    fold, keep, og_rows, out, small_in, end_in, *rest,
):
    line = mesh_line(levels)
    n_bufs = len(line_shapes()) if line else len(levels)
    level_bufs = rest[:n_bufs]
    (
        own_sem, send, recv, keep_sem, ext_sem, acts_sem,
        top_send, top_recv, bottom_send, bottom_recv,
        small_send, small_recv, fold_send, fold_recv,
        phase, w_sem, core_send, core_recv, credit, far_send, far_recv,
        rs_send, rs_recv, ag_send, ag_recv, out_sem, edge_send, edge_recv,
        sum_send, sum_recv, end_send, end_recv, frames_send, frames_recv, mel_send, mel_recv,
        lane_send, lane_recv, lane_credit, way_send, way_recv,
    ) = rest[n_bufs:]
    me = Place()
    core_dev = me.chan_device(me.core_shard)
    far_dev = me.chan_device(me.far_shard)
    diag_dev = me.chan_device(me.diag_shard)
    chan_devs = [core_dev, far_dev, diag_dev]
    has_prev = me.chan > 0
    has_next = me.chan < SHARDS - 1
    prev_dev = me.chan_device(jnp.maximum(me.chan - 1, 0))
    next_dev = me.chan_device(jnp.minimum(me.chan + 1, SHARDS - 1))

    quarter = ROWS // 2
    xb, zb = me.dp_bit(0), me.dp_bit(1)

    def quarter_at(x, z, first=0, rows=quarter):
        return pl.ds(pl.multiple_of((x * 2 + z) * quarter + first, 32), rows)

    half_quarter = quarter // 2

    def own_copies(l):
        dst = shared.at[l * SHARDS + me.chan]
        return [
            pltpu.make_async_copy(in_weight.at[l], dst.at[:, pl.ds(0, CONV)], own_sem.at[0, l]),
            pltpu.make_async_copy(cond_weight.at[l], dst.at[:, pl.ds(CONV, ROWS)], own_sem.at[1, l]),
        ]

    def res_copies(l):
        dst = shared.at[l * SHARDS + me.chan]
        return [
            pltpu.make_async_copy(
                res_weight.at[l, pl.ds(h * 2 * ROWS, 2 * ROWS)],
                dst.at[:, pl.ds(EXT + h * ROWS, ROWS)],
                own_sem.at[2 + h, l],
            )
            for h in range(2)
        ]

    def link(kind, l, shard, at, device):
        ref = shared.at[l * SHARDS + shard, at] if at is not None else shared.at[l * SHARDS + shard]
        return remote(ref, ref, send.at[kind, l], recv.at[kind, l], device)

    x_dev, z_dev = me.dp_device(0), me.dp_device(1)

    def far_a(l, shard):
        return link(0, l, shard, quarter_at(xb, zb), far_dev)

    def far_b(l, shard):
        return link(1, l, shard, quarter_at(1 - xb, 1 - zb, 0, half_quarter), far_dev)

    def x_a(l, x):
        return link(2, l, me.far_shard, quarter_at(x, zb), x_dev)

    def z_a(l, z):
        return link(3, l, me.far_shard, quarter_at(xb, z), z_dev)

    def x_b(l, x):
        return link(4, l, me.far_shard, quarter_at(x, 1 - zb, half_quarter, half_quarter), x_dev)

    def core_a(l, shard):
        return link(5, l, shard, None, core_dev)

    def core_b(l, shard):
        return link(6, l, shard, None, core_dev)

    def issue(l):
        for copy in own_copies(l):
            copy.wait()

        @pl.when(l < LAYERS - 1)
        def _():
            for copy in res_copies(l):
                copy.wait()

        far_a(l, me.chan).start()
        far_b(l, me.chan).start()
        core_a(l, me.chan).start()

    def relay_a(l):
        far_a(l, me.far_shard).wait_recv()
        x_a(l, xb).start()
        z_a(l, zb).start()

    def relay_b(l):
        z_a(l, 1 - zb).wait_recv()
        x_b(l, xb).start()

    def relay_c(l):
        far_b(l, me.far_shard).wait_recv()
        x_a(l, 1 - xb).wait_recv()
        x_b(l, 1 - xb).wait_recv()
        core_b(l, me.far_shard).start()

    def arrive(l):
        core_a(l, me.core_shard).wait_recv()
        core_b(l, me.diag_shard).wait_recv()

    shared[(LAYERS - 1) * SHARDS + me.chan, :, EXT:] = jnp.zeros((2 * ROWS, 2 * ROWS), BF16)

    def first_copies(l, carry):
        for copy in own_copies(l):
            copy.start()

        @pl.when(l < LAYERS - 1)
        def _():
            for copy in res_copies(l):
                copy.start()

        return carry

    lax.fori_loop(0, LAYERS, first_copies, 0)

    @pl.when(jnp.logical_not(has_prev))
    def _():
        top[...] = jnp.zeros_like(top)

    @pl.when(jnp.logical_not(has_next))
    def _():
        bottom[...] = jnp.zeros_like(bottom)

    edge_in[...] = jnp.zeros_like(edge_in)
    opp_dev = (6 + 2 * xb - me.dp, me.chan) if line else None
    greet(chan_devs + [me.dp_device(bit) for bit, _, _ in levels] + ([opp_dev] if line else []))

    def small_copy(k):
        return remote(local_small, small.at[me.chan], small_send.at[k], small_recv.at[k], chan_devs[k])

    def fold_copy(k):
        return remote(fold.at[me.chan], fold.at[me.chan], fold_send.at[k], fold_recv.at[k], chan_devs[k])

    issue(0)
    for k in range(3):
        small_copy(k).start()
    small[me.chan] = local_small[...]

    rows8 = lax.broadcasted_iota(jnp.int32, (CH, BLOCK), 0)
    mixed = jnp.zeros((CH, BLOCK), F32)
    for j in range(CH):
        mixed = mixed + inv_weight[:, j : j + 1] * audio[j : j + 1, :]
    first_ext = jnp.where(rows8 < HALF, mixed, jnp.where(rows8 == HALF, 1.0, 0.0))
    keep[0] = mixed
    keep[1] = first_ext
    for r in range(BLOCK // HOP):
        row = jnp.broadcast_to(mel[r : r + 1, :], (HOP, ROWS)).astype(BF16)
        for slot in range(2):
            ext[slot, pl.ds(r * HOP, HOP), CONV:] = row
    out[...] = jnp.zeros_like(out)
    for k in range(3):
        small_copy(k).wait_recv()

    def small_row(lo, hi):
        return jnp.concatenate([small[s, lo:hi, :] for s in range(SHARDS)], axis=1)

    start_ext = jnp.where(rows8 <= HALF, small_row(0, 8), 0.0)
    keep[2] = start_ext
    hid[pl.ds(PAD, BLOCK), :] = lax.dot_general(
        first_ext, start_ext, (((0,), (0,)), ((), ())), precision=HIGH, preferred_element_type=F32
    )
    relay_a(0)
    issue(1)
    final = small_row(16, 24)
    final_high, final_low = split(final)
    final_rows = jnp.concatenate([final_high, final_low], axis=0).astype(BF16)
    for l in range(LAYERS):
        both = dot(final_rows, skip_weight[l])
        high, rest_of = split(both[:CH] + both[CH:])
        fold[me.chan, l] = jnp.concatenate([high, rest_of, high, jnp.zeros_like(high)], axis=0).astype(BF16)
    for k in range(3):
        fold_copy(k).start()
    skip_bias = small_row(13, 14)
    const = jnp.sum(final * skip_bias, axis=1, keepdims=True) + end_bias[...]

    relay_b(0)
    aug = jnp.concatenate(
        [
            inv_weight[...],
            jnp.where(
                lax.broadcasted_iota(jnp.int32, (CH, CH), 0) == lax.broadcasted_iota(jnp.int32, (CH, CH), 1), 1.0, 0.0
            ),
        ],
        axis=1,
    )
    aug_rows = lax.broadcasted_iota(jnp.int32, (CH, 2 * CH), 0)
    log_total = jnp.zeros((1, 1), F32)
    for c in range(CH):
        pivot = aug[c : c + 1, c : c + 1]
        log_total = log_total + jnp.log(pivot)
        pivot_row = aug[c : c + 1, :] / pivot
        aug = jnp.where(aug_rows == c, pivot_row, aug - aug[:, c : c + 1] * pivot_row)
    inverse_out[...] = aug
    log_out[...] = jnp.broadcast_to(log_total, log_out.shape)
    relay_a(1)
    issue(2)
    relay_c(0)
    relay_b(1)

    def ext_copy(l):
        return pltpu.make_async_copy(ext.at[l % 2], ext_out.at[l], ext_sem.at[l % 2])

    def acts_copy(l):
        return pltpu.make_async_copy(acts.at[l % 2], acts_out.at[l], acts_sem.at[l % 2])

    def keep_copy(l):
        return pltpu.make_async_copy(
            shared.at[pl.ds(l * SHARDS, SHARDS)], weights_out.at[l], keep_sem.at[l]
        )

    def to_next(l, rows):
        p = l % 2
        return remote(
            ext.at[p, pl.ds(BLOCK - rows, rows), pl.ds(WIDTH, WIDTH)],
            top.at[p, pl.ds(EDGE - rows, rows)],
            top_send.at[p], top_recv.at[p], next_dev,
        )

    def to_prev(l, rows):
        p = l % 2
        return remote(
            ext.at[p, pl.ds(0, rows), pl.ds(WIDTH, WIDTH)],
            bottom.at[p, pl.ds(0, rows)],
            bottom_send.at[p], bottom_recv.at[p], prev_dev,
        )

    def by_edge(l, f):
        pl.when(l <= 4)(lambda: f(PAD))
        pl.when(l > 4)(lambda: f(EDGE))

    def forward(l, carry):
        p = l % 2
        pl.when(l + 2 < LAYERS)(lambda: relay_a(l + 2))
        arrive(l)
        pl.when(l < LAYERS - 1)(lambda: keep_copy(l).start())

        @pl.when(l >= 2)
        def _():
            ext_copy(l - 2).wait()
            acts_copy(l - 2).wait()

        spilled = l < LAYERS - 2
        ext[p, :, WIDTH : 2 * WIDTH] = hid[pl.ds(PAD, BLOCK), :].astype(BF16)

        def start(rows):
            pl.when(has_next)(lambda: to_next(l, rows).start())
            pl.when(has_prev)(lambda: to_prev(l, rows).start())

        def finish(rows):
            @pl.when(has_next)
            def _():
                to_next(l, rows).wait_send()
                to_prev(l, rows).wait_recv()

            @pl.when(has_prev)
            def _():
                to_prev(l, rows).wait_send()
                to_next(l, rows).wait_recv()

        by_edge(l, start)
        pl.when(l + 3 < LAYERS)(lambda: issue(l + 3))
        by_edge(l, finish)
        hid[pl.ds(0, PAD), :] = top[p, pl.ds(EDGE - PAD, PAD), :].astype(F32)
        hid[pl.ds(PAD + BLOCK, PAD), :] = bottom[p, pl.ds(0, PAD), :].astype(F32)
        for layer in range(LAYERS):
            d = 2**layer

            @pl.when(l == layer)
            def _():
                if d < PAD:
                    ext[p, :, :WIDTH] = hid[pl.ds(PAD - d, BLOCK), :].astype(BF16)
                    ext[p, :, 2 * WIDTH : CONV] = hid[pl.ds(PAD + d, BLOCK), :].astype(BF16)
                else:
                    ext[p, :d, :WIDTH] = top[p, EDGE - d :, :]
                    ext[p, d:, :WIDTH] = ext[p, : BLOCK - d, WIDTH : 2 * WIDTH]
                    ext[p, BLOCK - d :, 2 * WIDTH : CONV] = bottom[p, :d, :]
                    ext[p, : BLOCK - d, 2 * WIDTH : CONV] = ext[p, d:, WIDTH : 2 * WIDTH]

        pl.when(spilled)(lambda: ext_copy(l).start())

        def one(s, carry):
            pre = dot_nt(ext[p], shared[l * SHARDS + s, :, :EXT])
            t = jnp.tanh(pre[:, :ROWS])
            g = 0.5 * jnp.tanh(0.5 * pre[:, ROWS:]) + 0.5
            tg = t * g
            acts[p, s, 0] = tg.astype(BF16)
            acts[p, s, 1] = (g - t * tg).astype(BF16)
            acts[p, s, 2] = (tg * (1.0 - g)).astype(BF16)
            return carry

        lax.fori_loop(0, SHARDS, one, 0)
        pl.when(spilled)(lambda: acts_copy(l).start())

        @pl.when(l == 0)
        def _():
            for k in range(3):
                fold_copy(k).wait_recv()

        gated = jnp.concatenate([acts[p, s, 0] for s in range(SHARDS)], axis=1)
        out[...] += dot_nt(jnp.concatenate([fold[s, l, : 2 * CH, :] for s in range(SHARDS)], axis=1), gated)

        @pl.when(l < LAYERS - 1)
        def _():
            for h in range(2):
                res = jnp.concatenate(
                    [shared[l * SHARDS + s, :, EXT + h * ROWS : EXT + (h + 1) * ROWS] for s in range(SHARDS)], axis=1
                )
                bias = jnp.concatenate([small[s, pl.ds(5 + l, 1), :] for s in (2 * h, 2 * h + 1)], axis=1)
                cols = slice(h * 2 * ROWS, (h + 1) * 2 * ROWS)
                hid[pl.ds(PAD, BLOCK), cols] += dot_nt(gated, res) + bias

        pl.when(l + 1 < LAYERS)(lambda: relay_c(l + 1))
        pl.when(l + 2 < LAYERS)(lambda: relay_b(l + 2))
        return carry

    lax.fori_loop(0, LAYERS, forward, 0)

    both = out[...]
    output = both[:CH] + both[CH:] + const
    log_scale, shift = output[:HALF], output[HALF:]
    scale = jnp.exp(log_scale)
    mixed = keep[0]
    second = mixed[HALF:]
    second_out = scale * second + shift
    mine = pl.ds(pl.multiple_of(me.chan * BLOCK, BLOCK), BLOCK)
    frames_out[0:CH, mine] = jnp.concatenate([mixed[:HALF], second_out], axis=0)
    frames_out[2 * CH : 3 * CH, mine] = jnp.concatenate([log_scale, jnp.zeros_like(log_scale)], axis=0)
    out_grad = jnp.concatenate([second_out * scale * second - 1.0, second_out], axis=0)
    keep[3] = jnp.concatenate([jnp.zeros_like(scale), second_out * scale], axis=0)
    og_high, og_low = split(out_grad)
    og_rows[...] = jnp.concatenate([og_high, og_low], axis=0).astype(BF16)
    og_stack = jnp.concatenate([og_high, og_high, og_low, jnp.zeros((ROWS - 3 * CH, BLOCK), F32)], axis=0)
    low[:, WIDTH:] = og_stack.T.astype(BF16)
    end_sum = jnp.sum(out_grad, axis=1, keepdims=True)
    grad[...] = jnp.zeros_like(grad)
    mel_sum[...] = jnp.zeros_like(mel_sum)

    def drain_forward(l, carry):
        far_a(l, me.chan).wait_send()
        far_b(l, me.chan).wait_send()
        x_a(l, xb).wait_send()
        z_a(l, zb).wait_send()
        x_b(l, xb).wait_send()
        core_a(l, me.chan).wait_send()
        core_b(l, me.far_shard).wait_send()
        pl.when(l < LAYERS - 1)(lambda: keep_copy(l).wait())
        return carry

    lax.fori_loop(0, LAYERS, drain_forward, 0)
    for k in range(3):
        small_copy(k).wait_send()
        fold_copy(k).wait_send()
    pl.semaphore_signal(phase.at[0], inc=1, device_id=core_dev, device_id_type=MESH)
    pl.semaphore_signal(phase.at[1], inc=1, device_id=far_dev, device_id_type=MESH)

    def side_of(j):
        return jnp.where(j < 2, 1 - me.side, me.side)

    def shard_of(j):
        return side_of(j) * 2 + jnp.where(j % 2 == 0, 1 - me.core, me.core)

    def w_copy(q):
        l, s = LAYERS - 1 - q // SHARDS, shard_of(q % SHARDS)
        return pltpu.make_async_copy(weights_out.at[l, s], wbuf.at[q % 2], w_sem.at[q % 2])

    def w_start(q):
        s = shard_of(q % SHARDS)
        here = pltpu.make_async_copy(shared.at[(LAYERS - 1) * SHARDS + s], wbuf.at[q % 2], w_sem.at[q % 2])
        pl.when(q < SHARDS)(lambda: here.start())
        pl.when(q >= SHARDS)(lambda: w_copy(q).start())

    def ext_back(l):
        return pltpu.make_async_copy(ext_out.at[l], ext.at[l % 2], ext_sem.at[l % 2])

    def acts_back(l):
        return pltpu.make_async_copy(acts_out.at[l], acts.at[l % 2], acts_sem.at[l % 2])

    def kept(i, ys):
        return 4 + 2 * i + ys

    def got_core(i, ys):
        return 20 + 2 * (i % 2) + ys

    def to_core(i, ys):
        p = i % 2
        return remote(
            shared.at[2 * p + ys], shared.at[got_core(i, ys)], core_send.at[p, ys], core_recv.at[p, ys], core_dev
        )

    def to_far(i):
        return remote(shared.at[kept(i, 1 - me.side)], shared.at[24 + i], far_send.at[i], far_recv.at[i], far_dev)

    def add_rows(block, base, rows, src, src_at):
        chunk = min(rows, 32)

        def body(k, carry):
            at = pl.ds(pl.multiple_of(base + k * chunk, PAD), chunk)
            shared[block, at, :] = shared[block, at, :] + src[src_at, pl.ds(pl.multiple_of(k * chunk, PAD), chunk), :]
            return carry

        lax.fori_loop(0, rows // chunk, body, 0)

    base_at = [0]
    for bit, rows, after in levels:
        base_at.append(base_at[-1] + (me.dp_bit(bit) * after if after < rows else 0))

    def rs(k, i):
        bit, rows, after = levels[k]
        first = base_at[k] + ((1 - me.dp_bit(bit)) * after if after < rows else 0)
        at = pl.ds(pl.multiple_of(first, PAD), after)
        return remote(
            shared.at[kept(i, me.side), at], level_bufs[k].at[i], rs_send.at[k, i], rs_recv.at[k, i], me.dp_device(bit)
        )

    def ag(k, i, arriving):
        bit, rows, after = levels[k]
        first = base_at[k] + (1 - me.dp_bit(bit)) * after if arriving else base_at[k + 1]
        ref = total.at[LAYERS - 1 - i, pl.ds(pl.multiple_of(first, PAD), after)]
        return remote(ref, ref, ag_send.at[k, i], ag_recv.at[k, i], me.dp_device(bit))

    halving = [k for k, (bit, rows, after) in enumerate(levels) if after < rows]

    def out_copy(i):
        at = pl.ds(pl.multiple_of(base_at[-1], PAD), levels[-1][2])
        return pltpu.make_async_copy(shared.at[kept(i, me.side), at], total.at[LAYERS - 1 - i, at], out_sem.at[0, i])

    def core_block(i, ys):
        to_core(i, ys).wait_recv()
        add_rows(kept(i, ys), 0, 2 * ROWS, shared, got_core(i, ys))
        pl.semaphore_signal(credit.at[ys], inc=1, device_id=core_dev, device_id_type=MESH)

    def far_block(i):
        core_block(i, 1 - me.side)
        pl.when(i == 0)(lambda: pl.semaphore_wait(phase.at[1], 1))
        if not line:
            to_far(i).start()

    def stage_far(i):
        to_far(i).wait_recv()
        add_rows(kept(i, me.side), 0, 2 * ROWS, shared, 24 + i)
        rs(0, i).start()

    def stage_rs(k, i):
        bit, rows, after = levels[k]
        rs(k, i).wait_recv()
        if after == rows:
            rs(k, i).wait_send()
        add_rows(kept(i, me.side), base_at[k + 1], after, level_bufs[k], i)
        if k + 1 < len(levels):
            rs(k + 1, i).start()
        else:
            out_copy(i).start()
            out_copy(i).wait()
            ag(halving[-1], i, False).start()

    def stage_ag(n, i):
        ag(halving[n], i, True).wait_recv()
        if n > 0:
            ag(halving[n - 1], i, False).start()

    def add_block(block, base, rows, cols, src, src_base=0):
        chunk = min(rows, 64)

        def body(k, carry):
            at = pl.ds(pl.multiple_of(base + k * chunk, 32), chunk)
            got = src[pl.ds(pl.multiple_of(src_base + k * chunk, 32), chunk), :]
            shared[block, at, cols] = shared[block, at, cols] + got
            return carry

        lax.fori_loop(0, rows // chunk, body, 0)

    def rows_at(first, rows):
        return pl.ds(pl.multiple_of(first, 32), rows)

    if line:
        zc = me.dp // 2
        inner = (zc == 1) | (zc == 2)
        edge = jnp.logical_not(inner)
        hb = jnp.where(zc == 2, 1, 0)
        lane_devs = [x_dev, z_dev, opp_dev, z_dev, opp_dev, x_dev]
        lanes = [
            Lane(level_bufs[k], lane_send.at[k], lane_recv.at[k], lane_credit.at[k], lane_devs[k]) for k in range(6)
        ]
        qx, q1, q2, r1, r2, rx = lanes
        wide, half, small_half = ROWS, ROWS // 2, ROWS // 4

        def q_rows(u, x):
            return x * wide + u % 2 * half

        def r_rows(u):
            return u % 2 * wide

        def far_way(k, u, rows, cols):
            i = u // 2
            return remote(
                shared.at[kept(i, 1 - me.side), rows, cols], shared.at[24 + i, rows, cols],
                way_send.at[k, u], way_recv.at[k, u], far_dev,
            )

        def far_q(u):
            return far_way(0, u, rows_at(q_rows(u, xb), half), ACROSS)

        def far_r(u):
            return far_way(1, u, rows_at(r_rows(u), wide), ALONG)

        def own_ref(u, first, rows, cols):
            return shared.at[kept(u // 2, me.side), rows_at(first, rows), cols]

        def total_ref(u, first, rows, cols):
            return total.at[LAYERS - 1 - u // 2, rows_at(first, rows), cols]

        def way(k, u, src, dst, device):
            return remote(src, dst, way_send.at[k, u], way_recv.at[k, u], device)

        def q_inner(u, b):
            at = (u, q_rows(u, xb) + b * small_half, small_half, ACROSS)
            return way(2, u, own_ref(*at), total_ref(*at), opp_dev)

        def q_edge(u):
            ref = total_ref(u, q_rows(u, xb), half, ACROSS)
            return way(3, u, ref, ref, z_dev)

        def q_x(u, x):
            ref = total_ref(u, q_rows(u, x), half, ACROSS)
            return way(4, u, ref, ref, x_dev)

        def r_x(u, x):
            at = (u, r_rows(u) + hb * half + x * small_half, small_half, ALONG)
            return way(5, u, own_ref(*at), total_ref(*at), x_dev)

        def r_inner(u, b):
            ref = total_ref(u, r_rows(u) + b * half, half, ALONG)
            return way(6, u, ref, ref, opp_dev)

        def r_edge(u):
            ref = total_ref(u, r_rows(u), wide, ALONG)
            return way(7, u, ref, ref, z_dev)

        def q_out(u):
            at = (u, q_rows(u, xb) + hb * small_half, small_half, ACROSS)
            return pltpu.make_async_copy(own_ref(*at), total_ref(*at), out_sem.at[0, u])

        def r_out(u):
            at = (u, r_rows(u) + hb * half + xb * small_half, small_half, ALONG)
            return pltpu.make_async_copy(own_ref(*at), total_ref(*at), out_sem.at[1, u])

        def start_q(u):
            qx.start(u, shared.at[pl.ds(kept(u // 2, 0), 2), rows_at(q_rows(u, 1 - xb), half), ACROSS])

        def q_stage1(u):
            qx.wait(u)
            for ys in (1 - me.side, me.side):
                add_block(kept(u // 2, ys), q_rows(u, xb), half, ACROSS, qx.buf.at[u % DEPTH, ys])
                if ys is not me.side:
                    far_q(u).start()
            qx.free()

        def r_stage1(u):
            far_r(u).wait_recv()
            add_block(kept(u // 2, me.side), r_rows(u), wide, ALONG, shared.at[24 + u // 2, :, ALONG], r_rows(u))
            pl.when(edge)(lambda: r1.start(u, own_ref(u, r_rows(u), wide, ALONG)))

        def q_stage2(u):
            far_q(u).wait_recv()
            first = q_rows(u, xb)
            add_block(kept(u // 2, me.side), first, half, ACROSS, shared.at[24 + u // 2, :, ACROSS], first)
            pl.when(edge)(lambda: q1.start(u, own_ref(u, first, half, ACROSS)))

        def r_stage2(u):
            @pl.when(inner)
            def _():
                r1.wait(u)
                add_block(kept(u // 2, me.side), r_rows(u), wide, ALONG, r1.buf.at[u % DEPTH])
                r1.free()
                r2.start(u, own_ref(u, r_rows(u) + (1 - hb) * half, half, ALONG))

        def q_stage3(u):
            @pl.when(inner)
            def _():
                first = q_rows(u, xb)
                q1.wait(u)
                add_block(kept(u // 2, me.side), first, half, ACROSS, q1.buf.at[u % DEPTH])
                q1.free()
                q2.start(u, own_ref(u, first + (1 - hb) * small_half, small_half, ACROSS))

        def r_stage3(u):
            @pl.when(inner)
            def _():
                first = r_rows(u) + hb * half
                r2.wait(u)
                add_block(kept(u // 2, me.side), first, half, ALONG, r2.buf.at[u % DEPTH])
                r2.free()
                rx.start(u, own_ref(u, first + (1 - xb) * small_half, small_half, ALONG))

        def q_stage4(u):
            @pl.when(inner)
            def _():
                q2.wait(u)
                first = q_rows(u, xb) + hb * small_half
                add_block(kept(u // 2, me.side), first, small_half, ACROSS, q2.buf.at[u % DEPTH])
                q2.free()
                q_inner(u, hb).start()
                q_out(u).start()

        def r_stage4(u):
            @pl.when(inner)
            def _():
                rx.wait(u)
                first = r_rows(u) + hb * half + xb * small_half
                add_block(kept(u // 2, me.side), first, small_half, ALONG, rx.buf.at[u % DEPTH])
                rx.free()
                r_x(u, xb).start()
                r_out(u).start()

        def q_stage5(u):
            @pl.when(inner)
            def _():
                q_out(u).wait()
                q_inner(u, 1 - hb).wait_recv()
                q_edge(u).start()
                q_x(u, xb).start()

        def r_stage5(u):
            @pl.when(inner)
            def _():
                r_out(u).wait()
                r_x(u, 1 - xb).wait_recv()
                r_inner(u, hb).start()

        def q_stage6(u):
            @pl.when(edge)
            def _():
                q_edge(u).wait_recv()
                q_x(u, xb).start()

        def r_stage6(u):
            @pl.when(inner)
            def _():
                r_inner(u, 1 - hb).wait_recv()
                r_edge(u).start()

        def q_stage7(u):
            q_x(u, 1 - xb).wait_recv()

        def r_stage7(u):
            pl.when(edge)(lambda: r_edge(u).wait_recv())

        def drain_ways(u, carry):
            far_q(u).wait_send()
            far_r(u).wait_send()
            q_x(u, xb).wait_send()

            @pl.when(inner)
            def _():
                q_inner(u, hb).wait_send()
                q_edge(u).wait_send()
                r_x(u, xb).wait_send()
                r_inner(u, hb).wait_send()
                r_edge(u).wait_send()

            return carry

        def finish_lanes():
            qx.finish()

            @pl.when(edge)
            def _():
                q1.finish()
                r1.finish()

            @pl.when(inner)
            def _():
                q2.finish()
                r2.finish()
                rx.finish()

        line_stages = [
            [q_stage1, r_stage1], [q_stage2, r_stage2], [q_stage3, r_stage3], [q_stage4, r_stage4],
            [q_stage5, r_stage5], [q_stage6, r_stage6], [q_stage7, r_stage7],
        ]

    def back_prev(i, rows):
        return remote(
            edge_out.at[0, pl.ds(0, rows)], edge_in.at[i % 2, 0, pl.ds(0, rows)],
            edge_send.at[0], edge_recv.at[i % 2, 0], prev_dev,
        )

    def back_next(i, rows):
        return remote(
            edge_out.at[1, pl.ds(EDGE - rows, rows)], edge_in.at[i % 2, 1, pl.ds(EDGE - rows, rows)],
            edge_send.at[1], edge_recv.at[i % 2, 1], next_dev,
        )

    def back_edge(i, f):
        by_edge(LAYERS - 1 - i, f)

    def apply_edges(i):
        def finish(rows):
            @pl.when(has_next)
            def _():
                back_next(i, rows).wait_send()
                back_prev(i, rows).wait_recv()

            @pl.when(has_prev)
            def _():
                back_prev(i, rows).wait_send()
                back_next(i, rows).wait_recv()

        back_edge(i, finish)
        tap0[pl.ds(BLOCK, EDGE), :] = edge_in[i % 2, 0].astype(F32)
        tap2[pl.ds(0, EDGE), :] = edge_in[i % 2, 1].astype(F32)
        for layer in range(LAYERS):
            d = 2**layer

            @pl.when(LAYERS - 1 - i == layer)
            def _():
                grad[...] += tap0[pl.ds(d, BLOCK), :] + tap2[pl.ds(EDGE - d, BLOCK), :]

    def backward_open(i):
        l = LAYERS - 1 - i
        pl.when(i > 0)(lambda: apply_edges(i - 1))
        now = grad[...].astype(BF16)
        low[:, :WIDTH] = now
        low_t[...] = now.T
        sums_out[pl.ds(72 + l, 1), :] = jnp.sum(now.astype(F32), axis=0, keepdims=True)
        tap0[pl.ds(0, BLOCK), :] = jnp.zeros((BLOCK, WIDTH), F32)
        tap2[pl.ds(EDGE, BLOCK), :] = jnp.zeros((BLOCK, WIDTH), F32)

        @pl.when(i >= 2)
        def _():
            ext_back(l).wait()
            acts_back(l).wait()

    def backward_shards(i, h):
        l = LAYERS - 1 - i
        p = l % 2

        def one(k, carry):
            j = 2 * h + k
            q = i * SHARDS + j
            b = q % 2
            s = shard_of(j)
            pl.when(q + 1 < LAYERS * SHARDS)(lambda: w_start(q + 1))

            @pl.when((j % 2 == 0) & (i >= 2))
            def _():
                to_core(i - 2, side_of(j)).wait_send()

            w_copy(q).wait()
            slot = jnp.where(j % 2 == 0, 2 * (i % 2) + side_of(j), kept(i, side_of(j)))
            gated = acts[p, s, 0]
            res = jnp.concatenate(
                [
                    wbuf[b, :, EXT : EXT + ROWS],
                    wbuf[b, :, EXT + ROWS :],
                    fold[s, l],
                    jnp.zeros((ROWS - 4 * CH, ROWS), BF16),
                ],
                axis=0,
            )
            back = dot(low[...], res)
            pg = jnp.concatenate(
                [(back * acts[p, s, 1].astype(F32)).astype(BF16), (back * acts[p, s, 2].astype(F32)).astype(BF16)],
                axis=1,
            )
            pg_t = pg.T
            tap0[pl.ds(0, BLOCK), :] += dot(pg, wbuf[b, :, :WIDTH])
            grad[...] += dot(pg, wbuf[b, :, WIDTH : 2 * WIDTH])
            last_tap = dot(pg, wbuf[b, :, 2 * WIDTH : EXT])
            tap2[pl.ds(EDGE, BLOCK), :] += last_tap[:, :WIDTH]
            mel_sum[...] += last_tap[:, WIDTH:]
            for cols in (slice(0, 6 * ROWS), slice(6 * ROWS, EXT)):
                shared[slot, :, cols] = dot(pg_t, ext[p, :, cols]).astype(BF16)
            side = dot(low_t[...], gated).astype(BF16)
            shared[slot, :, EXT : EXT + ROWS] = side[: 2 * ROWS]
            shared[slot, :, EXT + ROWS :] = side[2 * ROWS :]
            e = dot(og_rows[...], gated)
            sums_out[pl.ds(pl.multiple_of(l * CH, CH), CH), pl.ds(pl.multiple_of(s * ROWS, ROWS), ROWS)] = e[:CH] + e[CH:]

            @pl.when(j % 2 == 0)
            def _():
                pl.when(q == 0)(lambda: pl.semaphore_wait(phase.at[0], 1))
                pl.when(i >= 2)(lambda: pl.semaphore_wait(credit.at[side_of(j)], 1))
                to_core(i, side_of(j)).start()

            return carry

        lax.fori_loop(0, 2, one, 0)

    def backward_close(i):
        l = LAYERS - 1 - i

        @pl.when(l >= 2)
        def _():
            ext_back(l - 2).start()
            acts_back(l - 2).start()

        edge_out[0] = tap0[pl.ds(0, EDGE), :].astype(BF16)
        edge_out[1] = tap2[pl.ds(BLOCK, EDGE), :].astype(BF16)

        def start(rows):
            pl.when(has_next)(lambda: back_next(i, rows).start())
            pl.when(has_prev)(lambda: back_prev(i, rows).start())

        back_edge(i, start)

    sum_devs = [core_dev, far_dev] + [me.dp_device(bit) for bit, _, _ in levels]

    def sum_copy(k):
        return remote(sums_out, small_in.at[k], sum_send.at[k], sum_recv.at[k], sum_devs[k])

    def end_copy(k):
        return remote(end_out, end_in.at[k], end_send.at[k], end_recv.at[k], sum_devs[k])

    def frames_copy(k):
        ref = frames_out.at[:, mine]
        return remote(ref, ref, frames_send.at[k], frames_recv.at[k], chan_devs[k])

    mel_rows = BLOCK // HOP

    def mel_copy(k):
        ref = mel_out.at[pl.ds(pl.multiple_of(me.chan * mel_rows, mel_rows), mel_rows)]
        return remote(ref, ref, mel_send.at[k], mel_recv.at[k], chan_devs[k])

    def last(values, other, dims):
        return lax.dot_general(values, other, (dims, ((), ())), precision=HIGH, preferred_element_type=F32)

    def finish_frames():
        apply_edges(LAYERS - 1)
        hidden_grad = grad[...]
        sums_out[64:72, :] = last(keep[1], hidden_grad, ((1,), (0,)))
        mixed = keep[0]
        first_back = last(keep[2], hidden_grad, ((1,), (1,)))
        rows = lax.broadcasted_iota(jnp.int32, (CH, BLOCK), 0)
        mixed_grad = jnp.where(rows < HALF, mixed + first_back, keep[3])
        frames_out[CH : 2 * CH, mine] = last(inv_weight[...], mixed_grad, ((0,), (0,)))
        inv_part = last(mixed_grad, audio[...], ((1,), (1,)))
        sums_out[80:88, :] = jnp.concatenate([inv_part, end_sum, jnp.zeros((CH, WIDTH - CH - 1), F32)], axis=1)
        mel_out[pl.ds(pl.multiple_of(me.chan * mel_rows, mel_rows), mel_rows), :] = jnp.sum(
            mel_sum[...].reshape(mel_rows, HOP, ROWS), axis=1
        )
        for k in range(3):
            frames_copy(k).start()
            mel_copy(k).start()
        sum_copy(0).start()

    def sum_stage(k):
        sum_copy(k).wait_recv()
        sum_copy(k).wait_send()
        sums_out[...] = sums_out[...] + small_in[k]
        if k + 1 < len(sum_devs):
            sum_copy(k + 1).start()
            return
        e = sums_out[0:64, pl.ds(pl.multiple_of(me.chan * ROWS, ROWS), ROWS)]
        e_high, e_low = split(e)
        end = jnp.zeros((2 * CH, WIDTH), F32)
        for l in range(LAYERS):
            part = slice(l * CH, (l + 1) * CH)
            end = end + dot_nt(jnp.concatenate([e_high[part], e_low[part]], axis=0).astype(BF16), skip_weight[l])
        end_out[...] = end[:CH] + end[CH:]
        end_copy(0).start()

    def end_stage(k):
        end_copy(k).wait_recv()
        end_copy(k).wait_send()
        end_out[...] = end_out[...] + end_in[k]
        if k == 0:
            end_copy(1).start()

    small_stages = [finish_frames]
    small_stages += [functools.partial(sum_stage, k) for k in range(len(sum_devs))]
    small_stages += [functools.partial(end_stage, k) for k in range(2)]

    if line:
        stages = [[]] + line_stages
    else:
        stages = [[], [stage_far]]
        stages += [[functools.partial(stage_rs, k)] for k in range(len(levels))]
        stages += [[functools.partial(stage_ag, n)] for n in range(len(halving) - 1, -1, -1)]
    if line:
        steps = 2 * LAYERS + max(ACROSS_LAGS[-1] + 2, ALONG_LAGS[-1] + 1, len(small_stages))
    else:
        steps = 2 * LAYERS + max(2 * len(stages), len(small_stages))

    w_start(0)

    def step(v, carry):
        i, h = v // 2, v % 2

        @pl.when(v < 2 * LAYERS)
        def _():
            pl.when(h == 0)(lambda: backward_open(i))
            backward_shards(i, h)

            @pl.when(h == 1)
            def _():
                backward_close(i)

        core_from = v - 1
        pl.when((core_from >= 0) & (core_from < 2 * LAYERS) & (h == 1))(lambda: far_block(core_from // 2))
        pl.when((core_from >= 0) & (core_from < 2 * LAYERS) & (h == 0))(lambda: core_block(core_from // 2, me.side))

        if line:
            pl.when((v >= 1) & (v <= 2 * LAYERS))(lambda: far_r(v - 1).start())
            pl.when((v >= 2) & (v <= 2 * LAYERS + 1))(lambda: start_q(v - 2))
        def at_lag(at, count, stage, now=True):
            pl.when((at >= 0) & (at < count) & now)(lambda: stage(at))

        if line:
            for name in ORDER.split():
                k = int(name[1])
                if name[0] == "q":
                    at_lag(v - 2 - ACROSS_LAGS[k], 2 * LAYERS, stages[k][0])
                else:
                    at_lag(v - 1 - ALONG_LAGS[k], 2 * LAYERS, stages[k][1])
        else:
            for lag in range(len(stages) - 1, 0, -1):
                at_lag((v - 2) // 2 - lag + 1, LAYERS, stages[lag][0], (h == 0) & (v >= 2))

        for k, stage in enumerate(small_stages):
            pl.when(v == 2 * LAYERS + k)(stage)
        return carry

    lax.fori_loop(0, steps, step, 0)

    for i in (LAYERS - 2, LAYERS - 1):
        for ys in range(2):
            to_core(i, ys).wait_send()
            pl.semaphore_wait(credit.at[ys], 1)

    def drain(i, carry):
        to_far(i).wait_send()
        for k, (bit, rows, after) in enumerate(levels):
            if after < rows:
                rs(k, i).wait_send()
                ag(k, i, False).wait_send()
        return carry

    if line:
        lax.fori_loop(0, 2 * LAYERS, drain_ways, 0)
        finish_lanes()
    else:
        lax.fori_loop(0, LAYERS, drain, 0)
    for k, shard in enumerate([me.core_shard, me.far_shard, me.diag_shard]):
        frames_copy(k).wait_send()
        mel_copy(k).wait_send()
        frames_copy(k).wait_recv()
        mel_copy(k).wait_recv()
    own_lanes = pl.ds(pl.multiple_of(me.chan * ROWS, ROWS), ROWS)
    mine_out[...] = sums_out[:, own_lanes]
    end_own_out[...] = end_out[:, own_lanes]


def run_flow(dp_size, *args):
    levels = levels_of(dp_size)
    vmem = pl.BlockSpec(memory_space=pltpu.VMEM)
    hbm = pl.BlockSpec(memory_space=pl.ANY)
    dma = pltpu.SemaphoreType.DMA
    regular = pltpu.SemaphoreType.REGULAR
    block = (2 * ROWS, PACK)
    n = len(levels)
    return pl.pallas_call(
        functools.partial(flow_kernel, levels),
        out_shape=(
            jax.ShapeDtypeStruct((LAYERS,) + block, BF16),
            jax.ShapeDtypeStruct((LAYERS, SHARDS) + block, BF16),
            jax.ShapeDtypeStruct((LAYERS, BLOCK, EXT), BF16),
            jax.ShapeDtypeStruct((LAYERS, SHARDS, 3, BLOCK, ROWS), BF16),
            jax.ShapeDtypeStruct((3 * CH, FRAMES), F32),
            jax.ShapeDtypeStruct((FRAMES // HOP, ROWS), F32),
            jax.ShapeDtypeStruct((88, WIDTH), F32),
            jax.ShapeDtypeStruct((CH, 2 * CH), F32),
            jax.ShapeDtypeStruct((CH, ROWS), F32),
            jax.ShapeDtypeStruct((SHARDS, 24, ROWS), F32),
            jax.ShapeDtypeStruct((CH, WIDTH), F32),
            jax.ShapeDtypeStruct((88, ROWS), F32),
            jax.ShapeDtypeStruct((CH, ROWS), F32),
        ),
        in_specs=[hbm] * 3 + [vmem] * 6,
        out_specs=tuple([hbm] * 4 + [vmem] * 9),
        scratch_shapes=[
            pltpu.VMEM((LAYERS * SHARDS,) + block, BF16),
            pltpu.VMEM((PAD + BLOCK + PAD, WIDTH), F32),
            pltpu.VMEM((2, BLOCK, EXT), BF16),
            pltpu.VMEM((2, SHARDS, 3, BLOCK, ROWS), BF16),
            pltpu.VMEM((2, EDGE, WIDTH), BF16),
            pltpu.VMEM((2, EDGE, WIDTH), BF16),
            pltpu.VMEM((2,) + block, BF16),
            pltpu.VMEM((BLOCK, WIDTH + ROWS), BF16),
            pltpu.VMEM((WIDTH, BLOCK), BF16),
            pltpu.VMEM((BLOCK + EDGE, WIDTH), F32),
            pltpu.VMEM((EDGE + BLOCK, WIDTH), F32),
            pltpu.VMEM((BLOCK, WIDTH), F32),
            pltpu.VMEM((BLOCK, ROWS), F32),
            pltpu.VMEM((2, EDGE, WIDTH), BF16),
            pltpu.VMEM((2, 2, EDGE, WIDTH), BF16),
            pltpu.VMEM((SHARDS, LAYERS, 4 * CH, ROWS), BF16),
            pltpu.VMEM((4, CH, BLOCK), F32),
            pltpu.VMEM((2 * CH, BLOCK), BF16),
            pltpu.VMEM((2 * CH, BLOCK), F32),
            pltpu.VMEM((n + 2, 88, WIDTH), F32),
            pltpu.VMEM((2, CH, WIDTH), F32),
        ]
        + (
            [pltpu.VMEM((DEPTH,) + shape, BF16) for shape in line_shapes()]
            if mesh_line(levels)
            else [pltpu.VMEM((LAYERS, after, PACK), BF16) for _, _, after in levels]
        )
        + [
            dma((4, LAYERS)), dma((7, LAYERS)), dma((7, LAYERS)), dma((LAYERS,)), dma((2,)), dma((2,)),
            dma((2,)), dma((2,)), dma((2,)), dma((2,)),
            dma((3,)), dma((3,)), dma((3,)), dma((3,)),
            regular((2,)), dma((2,)), dma((2, 2)), dma((2, 2)), regular((2,)), dma((LAYERS,)), dma((LAYERS,)),
            dma((n, LAYERS)), dma((n, LAYERS)), dma((n, LAYERS)), dma((n, LAYERS)), dma((2, 2 * LAYERS)),
            dma((2,)), dma((2, 2)),
            dma((n + 2,)), dma((n + 2,)), dma((2,)), dma((2,)), dma((3,)), dma((3,)), dma((3,)), dma((3,)),
            dma((6, DEPTH)), dma((6, DEPTH)), regular((6,)), dma((8, 2 * LAYERS)), dma((8, 2 * LAYERS)),
        ],
        compiler_params=pltpu.CompilerParams(
            collective_id=0, has_side_effects=True, vmem_limit_bytes=VMEM_LIMIT
        ),
    )(*args)


def prepare_kernel(
    offset, clip, mel_frames, cond_weight, in_bias, start_weight, start_bias, res_bias, skip_bias, final, end_bias,
    audio, mel, cond_ext, local_small, end_column,
):
    chan = lax.axis_index("chan")
    first = offset[0] * HOP + chan * BLOCK
    length = clip.shape[2]
    audio[...] = pltpu.roll(clip[0], lax.rem(length - first, length), 1)[:, :BLOCK]
    mel_rows = BLOCK // HOP
    clip_rows = mel_frames.shape[1]
    frames = jnp.concatenate([mel_frames[0].astype(F32), jnp.ones((clip_rows, ROWS - MEL), F32)], axis=1)
    frames = pltpu.roll(frames, lax.rem(clip_rows - offset[0] - chan * mel_rows, clip_rows), 0)[:mel_rows]
    lane = lax.broadcasted_iota(jnp.int32, (mel_rows, ROWS), 1)
    mel[...] = jnp.where(lane < MEL + 2, frames, 0.0)
    for l in range(LAYERS):
        high, rest = split(in_bias[l])
        for g in range(2):
            part = jnp.concatenate(
                [
                    cond_weight[l, g].astype(F32),
                    high[g : g + 1],
                    rest[g : g + 1],
                    jnp.zeros((ROWS - MEL - 2, ROWS), F32),
                ],
                axis=0,
            )
            cond_ext[l, g * ROWS : (g + 1) * ROWS, :] = part.T.astype(BF16)
    local_small[...] = jnp.concatenate(
        [
            start_weight[...],
            start_bias[...],
            res_bias[...],
            jnp.zeros((1, ROWS), F32),
            skip_bias[...],
            jnp.zeros((2, ROWS), F32),
            final[...],
        ],
        axis=0,
    )
    row = jnp.concatenate([end_bias[...], jnp.zeros((1, ROWS - CH), F32)], axis=1)
    end_column[...] = jnp.broadcast_to(row, (ROWS, ROWS)).T[:CH, :1]


def run_prepare(*args):
    vmem = pl.BlockSpec(memory_space=pltpu.VMEM)
    return pl.pallas_call(
        prepare_kernel,
        out_shape=(
            jax.ShapeDtypeStruct((CH, BLOCK), F32),
            jax.ShapeDtypeStruct((BLOCK // HOP, ROWS), F32),
            jax.ShapeDtypeStruct((LAYERS, 2 * ROWS, ROWS), BF16),
            jax.ShapeDtypeStruct((24, ROWS), F32),
            jax.ShapeDtypeStruct((CH, 1), F32),
        ),
        in_specs=[pl.BlockSpec(memory_space=pltpu.SMEM)] + [vmem] * 10,
        out_specs=tuple([vmem] * 5),
    )(*args)


def finish_kernel(
    crops, total, sums, mine, small, frames, mel_in, inverse, log_abs, end_in, final_own, skip_bias,
    latent, log_det, loss, audio_grad, mel_grad, inv_grad, start_grad, start_bias_grad, cond_grad, in_grad,
    bias_grad, res_grad, res_bias_grad, skip_grad, skip_bias_grad, end_grad, end_bias_grad,
):
    l = pl.program_id(0)
    for g in range(2):
        rows = slice(g * ROWS, (g + 1) * ROWS)
        in_grad[0, g] = total[0, rows, :CONV].astype(F32)
        cond = total[0, rows, CONV:EXT].astype(F32)
        cond = cond.T
        cond_grad[0, g] = cond[:MEL]
        bias_grad[0, g : g + 1, :] = cond[MEL : MEL + 1]

    @pl.when(l < LAYERS - 1)
    def _():
        res_grad[0, : 2 * ROWS] = total[0, :, EXT : EXT + ROWS].astype(F32)
        res_grad[0, 2 * ROWS :] = total[0, :, EXT + ROWS :].astype(F32)

    final_high, final_low = split(jnp.concatenate([small[s, 16:24, :] for s in range(SHARDS)], axis=1))
    e_high, e_low = split(mine[pl.ds(pl.multiple_of(l * CH, CH), CH), :])
    skip_grad[0] = dot_tn(
        jnp.concatenate([final_high, final_high, final_low, jnp.zeros_like(final_low)], axis=0).astype(BF16),
        jnp.concatenate([e_high, e_low, e_high, jnp.zeros_like(e_low)], axis=0).astype(BF16),
    )

    @pl.when(l == 0)
    def _():
        z = frames[:CH]
        latent[0] = z
        audio_grad[0] = frames[CH : 2 * CH]
        mel_grad[0] = mel_in[:, :MEL]
        log_scale = frames[2 * CH : 2 * CH + HALF]
        det = jnp.sum(jnp.sum(log_scale, axis=1, keepdims=True), axis=0, keepdims=True) + FRAMES * log_abs[:1, :1]
        squares = jnp.sum(jnp.sum(z * z, axis=1, keepdims=True), axis=0, keepdims=True)
        log_det[...] = det
        loss[...] = (0.5 * squares - det) / (CH * FRAMES)
        tiny = sums[80:88, :ROWS]
        inv_grad[...] = tiny[:, :CH] - crops * FRAMES * inverse[:, CH:].T
        end_column = tiny[:, CH : CH + 1]
        end_bias_grad[...] = jnp.broadcast_to(end_column, (CH, ROWS)).T[:1, :]
        start_grad[...] = mine[64:68, :]
        start_bias_grad[...] = mine[68:69, :]
        res_bias_grad[...] = mine[72:79, :]
        skip_bias_grad[...] = jnp.sum(end_column * final_own[...], axis=0, keepdims=True)
        end_grad[...] = end_in[...] + end_column * skip_bias[...]


def run_finish(crops, total, *args):
    def whole(shape):
        return pl.BlockSpec(shape, lambda l: (0,) * len(shape))

    outs = [
        ((1, CH, FRAMES), None),
        ((1, 1), None),
        ((1, 1), None),
        ((1, CH, FRAMES), None),
        ((1, FRAMES // HOP, MEL), None),
        ((CH, CH), None),
        ((HALF, ROWS), None),
        ((1, ROWS), None),
        ((LAYERS, 2, MEL, ROWS), pl.BlockSpec((1, 2, MEL, ROWS), lambda l: (l, 0, 0, 0))),
        ((LAYERS, 2, ROWS, CONV), pl.BlockSpec((1, 2, ROWS, CONV), lambda l: (l, 0, 0, 0))),
        ((LAYERS, 2, ROWS), pl.BlockSpec((1, 2, ROWS), lambda l: (l, 0, 0))),
        (
            (LAYERS - 1, WIDTH, ROWS),
            pl.BlockSpec((1, WIDTH, ROWS), lambda l: (jnp.minimum(l, LAYERS - 2), 0, 0)),
        ),
        ((LAYERS - 1, ROWS), None),
        ((LAYERS, WIDTH, ROWS), pl.BlockSpec((1, WIDTH, ROWS), lambda l: (l, 0, 0))),
        ((1, ROWS), None),
        ((CH, ROWS), None),
        ((1, CH), None),
    ]
    return pl.pallas_call(
        functools.partial(finish_kernel, crops),
        grid=(LAYERS,),
        out_shape=tuple(jax.ShapeDtypeStruct(shape, F32) for shape, _ in outs),
        in_specs=[pl.BlockSpec((1, 2 * ROWS, PACK), lambda l: (l, 0, 0))] + [whole(a.shape) for a in args],
        out_specs=tuple(spec or whole(shape) for shape, spec in outs),
    )(total, *args)


def local(
    audio_clips,
    mel_frames,
    crop_offsets,
    inv_weight,
    initial_projection_weight,
    start_bias,
    cond_weight,
    in_weight,
    in_bias,
    res_weight,
    res_bias,
    skip_projection_weight,
    skip_output_bias,
    final_projection_weight,
    end_bias,
):
    skip_bias = skip_output_bias[None]
    audio, mel, cond_ext, local_small, end_column = run_prepare(
        crop_offsets,
        audio_clips,
        jnp.swapaxes(mel_frames, 1, 2),
        jnp.swapaxes(cond_weight, 2, 3),
        in_bias,
        initial_projection_weight.T,
        start_bias[None],
        res_bias,
        skip_bias,
        final_projection_weight,
        end_bias[None],
    )
    total, _, _, _, frames, mel_grad, sums, inverse, log_abs, small, _, mine, end_own = run_flow(
        lax.axis_size("dp"),
        in_weight.reshape(LAYERS, 2 * ROWS, CONV),
        cond_ext,
        res_weight,
        skip_projection_weight,
        audio,
        mel,
        inv_weight,
        local_small,
        end_column,
    )
    crops = lax.axis_size("dp") * audio_clips.shape[0]
    outs = list(
        run_finish(
            crops, total, sums, mine, small, frames, mel_grad, inverse, log_abs, end_own,
            final_projection_weight, skip_bias,
        )
    )
    for k, shape in ((1, (1,)), (2, (1,)), (7, (ROWS,)), (14, (ROWS,)), (16, (CH,))):
        outs[k] = outs[k].reshape(shape)
    outs[4] = jnp.swapaxes(outs[4], 1, 2)
    outs[6] = outs[6].T
    outs[8] = jnp.swapaxes(outs[8], 2, 3)
    return tuple(outs)


def solution(mesh):
    in_specs = (
        P("dp", None, None),
        P("dp", None, None),
        P("dp"),
        P(),
        P("chan", None),
        P("chan"),
        P(None, None, "chan", None),
        P(None, None, "chan", None),
        P(None, None, "chan"),
        P(None, None, "chan"),
        P(None, "chan"),
        P(None, None, "chan"),
        P("chan"),
        P(None, "chan"),
        P(),
    )
    out_specs = (
        P("dp", None, None),
        P("dp"),
        P("dp"),
        P("dp", None, None),
        P("dp", None, None),
        P(),
        P("chan", None),
        P("chan"),
        P(None, None, "chan", None),
        P(None, None, "chan", None),
        P(None, None, "chan"),
        P(None, None, "chan"),
        P(None, "chan"),
        P(None, None, "chan"),
        P("chan"),
        P(None, "chan"),
        P(),
    )
    return jax.shard_map(local, mesh=mesh, in_specs=in_specs, out_specs=out_specs, check_vma=False)
```
